256 devices in a mesh: blocks: 64 (over x, z, core), cat: 4 (over y).
Axes of the slice: x: 4, y: 4, z: 8, core: 2. Of those that a mesh axis runs over, the one named last changes fastest.
Arguments:
- velocity: float32 [2, 30, 30, 32768], P(None, None, None, ('blocks', 'cat')), may hold values from -6 to 6
- strength: float32 [30, 30, 32768], P(None, None, ('blocks', 'cat')), may hold values from 0.3 to 3
- mass: float32 [30, 30, 32768], P(None, None, ('blocks', 'cat')), may hold values from 0.5 to 2
- ice_cover: int32 [30, 30, 32768], P(None, None, ('blocks', 'cat')), may hold values 0 or 1
- neighbour: int32 [4, 32768], P(None, ('blocks', 'cat')), may hold values from 0 to 32767, as said below
- rotation: int32 [4, 32768], P(None, ('blocks', 'cat')), may hold values from 0 to 3
- concentration: float32 [4, 64, 256, 256], P('cat', 'blocks'), may hold values from 0.05 to 1
- air_wind: float32 [2, 64, 256, 256], P(None, 'blocks'), may hold values from -6 to 6
- ocean_current: float32 [2, 64, 256, 256], P(None, 'blocks'), may hold values from -5 to 5
- drag: float32 [2, 4], P(None, 'cat'), may hold values from 0.3 to 3
- slot_cell: int32 [64, 256, 256], P(None, ('blocks', 'cat')), may hold values from 0 to 115199
- slot_count: int32 [64, 256], P(None, ('blocks', 'cat')), may hold values from 0 to 256, as said below
Outputs:
- moving: float32 [2, 30, 30, 32768], P(None, None, None, ('blocks', 'cat'))
- stress: float32 [3, 30, 30, 32768], P(None, None, None, ('blocks', 'cat'))
The draws below stay inside these ranges and needn't reach their ends.
Inputs may be any that keep to these rules, and one draw needn't show every extreme that they name: Each block's neighbour across every side lies on its own device or on one of the two adjacent devices in blocks+cat index order, the first and last device counting as adjacent; device d holds blocks d * 128 onward. `slot_count`: some ice device receives 256 live slots from every owner.
All inputs are finite; a program needn't handle non-finite values. No bound on the sum of `ice_cover` on one device may be relied on, other than what follows from the above.
Results may differ from the reference program's by a relative error of at most 0.0003.
Values sent between devices are 32-bit elements; how exact they have to be, the bound alone decides.
No kernel may reach another device: no remote copies, remote signals or barrier semaphores. Data moves between devices by JAX's collectives and lax.ppermute only.
A program may use at most 192 MiB of HBM per device.

```python
import math
import jax
import jax.numpy as jnp

BS = 30
BLK_DEV = 128
CAP = 256
SUBCYCLES = 2
CATS = 4
GROUPS = 64
DEVS = 256
BLOCKS = 32768


def draw_neighbour(key, part):
    key = jax.random.fold_in(key, 11)
    first_key, second_key = jax.random.split(key)
    holders = jnp.arange(BLOCKS, dtype=jnp.int32) // BLK_DEV
    offsets = jax.random.randint(first_key, (4, BLOCKS), -1, 2)
    locals_drawn = jax.random.randint(second_key, (4, BLOCKS), 0, BLK_DEV)
    return (jnp.mod(holders[None, :] + offsets, DEVS) * BLK_DEV + locals_drawn).astype(jnp.int32)


def draw_slot_count(key, part):
    key = jax.random.fold_in(key, 23)
    level_key, base_key, full_key = jax.random.split(key, 3)
    levels = jax.random.randint(level_key, (1, DEVS), 1, 5)
    base_counts = jax.random.randint(base_key, (GROUPS, DEVS), CAP // 8, CAP // 2 + 1)
    counts = jnp.minimum(levels * base_counts, CAP)
    full_column = jax.random.randint(full_key, (), 0, DEVS)
    counts = jnp.where(jnp.arange(DEVS, dtype=jnp.int32)[None, :] == full_column, CAP, counts)
    return counts.astype(jnp.int32)


def plant(entries, stream_key, smallest, largest):
    longest = entries.shape.index(max(entries.shape))
    spots = []
    for shift in (0, 1):
        where = [jax.random.randint(jax.random.fold_in(stream_key, axis), (), 0, length) for axis, length in enumerate(entries.shape)]
        where[longest] = (where[longest] + shift) % entries.shape[longest]
        spots.append(tuple(where))
    return entries.at[spots[0]].set(smallest).at[spots[1]].set(largest)


def level_of(own_key, dims, pieces, low, high):
    level = 1.0
    for dim, shards_of in pieces:
        heights = jax.random.uniform(jax.random.fold_in(jax.random.fold_in(own_key, 6), dim), (shards_of,), jnp.float32, low / len(pieces), high / len(pieces))
        level = level * jnp.repeat(jnp.exp(heights), dims[dim] // shards_of).reshape((-1,) + (1,) * (len(dims) - 1 - dim))
    return level


def scatter_about(stream_key, extent, deviation, most, cuts=(), held_as=jnp.bfloat16):
    result = jax.random.normal(stream_key, extent, jnp.float32) * deviation
    if len(cuts) > 0:
        result = level_of(stream_key, extent, cuts, -0.22, 0.18) * result
    return jnp.clip(result, min=-most, max=most).astype(held_as)


def setup_inputs(seed: int = 0) -> dict:
    streams_of = jax.random.split(jax.random.key(seed), 13)
    return {
        "velocity": scatter_about(streams_of[0], (2, BS, BS, BLOCKS), 1.0, 6.0, ((3, 256),), jnp.float32),
        "strength": jnp.clip(jnp.exp(math.log(3.0) - 2.3025851 * jax.random.uniform(streams_of[1], (BS, BS, BLOCKS), jnp.float32) ** level_of(streams_of[1], (BS, BS, BLOCKS), ((2, 256),), -0.2, 0.2)), 0.3, 3.0),
        "mass": jnp.clip(jnp.exp(math.log(2.0) - 1.3862944 * jax.random.uniform(streams_of[2], (BS, BS, BLOCKS), jnp.float32) ** level_of(streams_of[2], (BS, BS, BLOCKS), ((2, 256),), -0.2, 0.2)), 0.5, 2.0),
        "ice_cover": plant((jax.random.randint(streams_of[3], (BS, BS, BLOCKS), 0, 5) < 4).astype(jnp.int32), jax.random.fold_in(streams_of[3], 1), 0, 1),
        "neighbour": draw_neighbour(jax.random.fold_in(streams_of[12], 71), 0),
        "rotation": plant(jax.random.randint(streams_of[5], (4, BLOCKS), 0, 4), jax.random.fold_in(streams_of[5], 1), 0, 3).astype(jnp.int32),
        "concentration": jnp.clip(0.05 + 0.95 * jax.random.uniform(streams_of[6], (CATS, GROUPS, DEVS, CAP), jnp.float32) ** level_of(streams_of[6], (CATS, GROUPS, DEVS, CAP), ((0, 4), (1, 64)), -0.2, 0.2), 0.05, 1.0),
        "air_wind": scatter_about(streams_of[7], (2, GROUPS, DEVS, CAP), 1.0, 6.0, ((1, 64),), jnp.float32),
        "ocean_current": scatter_about(streams_of[8], (2, GROUPS, DEVS, CAP), 0.7, 5.0, ((1, 64),), jnp.float32),
        "drag": jnp.clip(jnp.exp(math.log(3.0) - 2.3025851 * jax.random.uniform(streams_of[9], (2, CATS), jnp.float32) ** level_of(streams_of[9], (2, CATS), ((1, 4),), -0.2, 0.2)), 0.3, 3.0),
        "slot_cell": plant(jax.random.randint(streams_of[10], (GROUPS, DEVS, CAP), 0, BLK_DEV * BS * BS), jax.random.fold_in(streams_of[10], 1), 0, (BLK_DEV * BS * BS) - 1).astype(jnp.int32),
        "slot_count": draw_slot_count(jax.random.fold_in(streams_of[12], 71), 0),
    }


ELLIPSE_SQUARE = 4.0
DELTA_FLOOR = 0.5
RELAX_RATE = 0.5
INERTIA_WEIGHT = 4.0
CORIOLIS_RATE = 0.5
WATER_DRAG = 1.0

def edge_strips(quantity):
    return jnp.stack([quantity[:, 0], quantity[:, :, 0], quantity[:, -1], quantity[:, :, -1]], axis=0)

def turn_vector(picked, turns):
    cosine = (turns == 0).astype(jnp.float32) - (turns == 2).astype(jnp.float32)
    sine = (turns == 1).astype(jnp.float32) - (turns == 3).astype(jnp.float32)
    eastward = cosine * picked[0] - sine * picked[1]
    northward = sine * picked[0] + cosine * picked[1]
    return jnp.stack([eastward, northward])

def turn_tensor(picked, turns):
    parity = 1.0 - 2.0 * (turns % 2).astype(jnp.float32)
    return jnp.stack([picked[0], parity * picked[1], parity * picked[2]])

def rim_from(strips, position, turns, turner):
    rim_list = []
    for edge_side in range(4):
        source = (edge_side + 2 + turns[edge_side]) % 4
        picked = strips[source, :, :, position[edge_side]]
        rim_list.append(turner(jnp.transpose(picked, (1, 2, 0)), turns[edge_side]))
    return rim_list

def pad_block(quantity, rim_list):
    members = quantity.shape[0]
    blocks_here = quantity.shape[3]
    middle = jnp.concatenate([rim_list[0][:, None], quantity, rim_list[2][:, None]], axis=1)
    corner = jnp.zeros((members, 1, blocks_here), quantity.dtype)
    lower_row = jnp.concatenate([corner, rim_list[1], corner], axis=1)
    upper_row = jnp.concatenate([corner, rim_list[3], corner], axis=1)
    return jnp.concatenate([lower_row[:, :, None], middle, upper_row[:, :, None]], axis=2)

def along_east(padded):
    return 0.5 * (padded[:, 2:, 1:-1] - padded[:, :-2, 1:-1])

def along_north(padded):
    return 0.5 * (padded[:, 1:-1, 2:] - padded[:, 1:-1, :-2])

def stress_update(stress, moving_pad, strength):
    east_grad = along_east(moving_pad)
    north_grad = along_north(moving_pad)
    divergence = east_grad[0] + north_grad[1]
    tension = east_grad[0] - north_grad[1]
    shearing = north_grad[0] + east_grad[1]
    delta_rate = jnp.sqrt(divergence * divergence + (tension * tension + shearing * shearing) / ELLIPSE_SQUARE + DELTA_FLOOR * DELTA_FLOOR)
    first_target = strength * (divergence / delta_rate - 1.0)
    second_target = strength * tension / (ELLIPSE_SQUARE * delta_rate)
    shear_target = strength * shearing / (2.0 * ELLIPSE_SQUARE * delta_rate)
    targets = jnp.stack([first_target, second_target, shear_target])
    return stress + RELAX_RATE * (targets - stress)

def velocity_update(moving, stress_pad, mass, forcing, covered):
    normal_one = 0.5 * (stress_pad[0] + stress_pad[1])
    normal_two = 0.5 * (stress_pad[0] - stress_pad[1])
    shear_pad = stress_pad[2]
    force_east = along_east(normal_one[None])[0] + along_north(shear_pad[None])[0]
    force_north = along_east(shear_pad[None])[0] + along_north(normal_two[None])[0]
    inverse_mass = 1.0 / mass
    denominator = INERTIA_WEIGHT + inverse_mass * WATER_DRAG
    eastward = (INERTIA_WEIGHT * moving[0] + inverse_mass * (force_east + forcing[0]) + CORIOLIS_RATE * moving[1]) / denominator
    northward = (INERTIA_WEIGHT * moving[1] + inverse_mass * (force_north + forcing[1]) - CORIOLIS_RATE * moving[0]) / denominator
    return jnp.stack([eastward, northward]) * covered

def category_partial(fraction, air_drag, ocean_drag, air_wind, ocean_current):
    air_speed = jnp.sqrt(air_wind[0] * air_wind[0] + air_wind[1] * air_wind[1])
    ocean_speed = jnp.sqrt(ocean_current[0] * ocean_current[0] + ocean_current[1] * ocean_current[1])
    return fraction * (air_drag * air_wind * air_speed + ocean_drag * ocean_current * ocean_speed)

def reference(velocity, strength, mass, ice_cover, neighbour, rotation, concentration, air_wind, ocean_current, drag, slot_cell, slot_count):
    covered = ice_cover.astype(jnp.float32)
    summed = category_partial(concentration[0], drag[0, 0], drag[1, 0], air_wind, ocean_current)
    for category in range(1, CATS):
        summed = summed + category_partial(concentration[category], drag[0, category], drag[1, category], air_wind, ocean_current)
    live_slot = (jnp.arange(CAP, dtype=jnp.int32)[None, None, :] < slot_count[:, :, None]).astype(jnp.float32)
    summed = summed * live_slot
    owners = jnp.arange(DEVS, dtype=jnp.int32)[None, :, None]
    target = slot_cell // BLK_DEV * BLOCKS + owners * BLK_DEV + slot_cell % BLK_DEV
    forcing = jnp.zeros((2, BS * BS * BLOCKS), jnp.float32).at[:, target.reshape(-1)].add(summed.reshape(2, -1))
    forcing = forcing.reshape(2, BS, BS, BLOCKS)
    moving = velocity * covered
    stress = jnp.zeros((3, BS, BS, BLOCKS), jnp.float32)
    for subcycle in range(SUBCYCLES):
        rim_list = rim_from(edge_strips(moving), neighbour, rotation, turn_vector)
        stress = stress_update(stress, pad_block(moving, rim_list), strength)
        rim_list = rim_from(edge_strips(stress), neighbour, rotation, turn_tensor)
        moving = velocity_update(moving, pad_block(stress, rim_list), mass, forcing, covered)
    return (moving, stress)
```

```python
import functools

import jax
import jax.numpy as jnp
from jax import lax
from jax.experimental import pallas as pl
from jax.experimental.pallas import tpu as pltpu
from jax.sharding import PartitionSpec as P

F32 = jnp.float32
BF16 = jnp.bfloat16
I32 = jnp.int32

SIDE = 30
ROWS = 32
LANES = 128
OWNERS = 64
SLOTS = 256
EXTRA = 8
CHUNK = 8
BOTH = ("blocks", "cat")

PARAMS = pltpu.CompilerParams(vmem_limit_bytes=48 * 1024 * 1024)
VMEM = pl.BlockSpec(memory_space=pltpu.VMEM)
SMEM = pl.BlockSpec(memory_space=pltpu.SMEM)


def shape(*dims, dtype=F32):
    return jax.ShapeDtypeStruct(dims, dtype)


def partial_kernel(mine_ref, first_ref, second_ref, third_ref, air_ref, ocean_ref, out_ref):
    parts = (mine_ref, first_ref, second_ref, third_ref)
    air_weight = jnp.zeros((OWNERS, SLOTS), F32)
    ocean_weight = jnp.zeros((OWNERS, SLOTS), F32)
    for part in parts:
        fraction = part[0:OWNERS, :]
        air_weight += fraction * part[OWNERS : OWNERS + 1, :]
        ocean_weight += fraction * part[OWNERS + 1 : OWNERS + 2, :]
    air_east, air_north = air_ref[0], air_ref[1]
    ocean_east, ocean_north = ocean_ref[0], ocean_ref[1]
    air_weight *= jnp.sqrt(air_east * air_east + air_north * air_north)
    ocean_weight *= jnp.sqrt(ocean_east * ocean_east + ocean_north * ocean_north)
    out_ref[:, 0, :] = air_weight * air_east + ocean_weight * ocean_east
    out_ref[:, 1, :] = air_weight * air_north + ocean_weight * ocean_north


def split_lanes(lane_hits, value):
    high = value.astype(BF16).astype(F32)
    return (
        jnp.where(lane_hits, high, 0.0).astype(BF16),
        jnp.where(lane_hits, value - high, 0.0).astype(BF16),
    )


def spread_values(cell_ref, value_ref, count_ref, spread, index, group):
    block = lax.broadcasted_iota(I32, (LANES, SLOTS), 0)
    slot = lax.broadcasted_iota(I32, (1, SLOTS), 1)
    columns = pl.ds(index * SLOTS, SLOTS)
    lane_hits = block == lax.bitwise_and(cell_ref[group], LANES - 1)
    live = slot < count_ref[group]
    for member in range(2):
        value = jnp.where(live, value_ref[group, member : member + 1, :], 0.0)
        high, low = split_lanes(lane_hits, value)
        spread[pl.ds(member * 2 * LANES, LANES), columns] = high
        spread[pl.ds(member * 2 * LANES + LANES, LANES), columns] = low


def cell_place(cell):
    number = lax.shift_right_logical(cell, 7)
    east = lax.shift_right_logical(number * 2185, 16)
    return east, number - east * SIDE


def accumulate(total, hot, spread):
    total[...] += lax.dot_general(
        hot[...], spread[...], (((1,), (1,)), ((), ())), preferred_element_type=F32
    )


def row_kernel(first, last, cell_ref, value_ref, count_ref, out_ref, hot, spread, total):
    step = pl.program_id(0)

    @pl.when(step == 0)
    def _():
        total[...] = jnp.zeros_like(total)

    north_of = lax.broadcasted_iota(I32, (ROWS, SLOTS), 0)
    for index in range(CHUNK):
        east, north = cell_place(cell_ref[index])
        columns = pl.ds(index * SLOTS, SLOTS)
        north_hot = (north_of == north).astype(F32).astype(BF16)
        for i in range(first, last):
            hot[pl.ds((i - first) * ROWS, ROWS), columns] = jnp.where(
                east == i, north_hot, jnp.zeros_like(north_hot)
            )
        spread_values(cell_ref, value_ref, count_ref, spread, index, index)
    accumulate(total, hot, spread)

    @pl.when(step == pl.num_programs(0) - 1)
    def _():
        for member in range(2):
            at = member * 2 * LANES
            summed = total[:, at : at + LANES] + total[:, at + LANES : at + 2 * LANES]
            out_ref[member] = summed.reshape(last - first, ROWS, LANES)


def scatter_rows(cell, value, count, first, last):
    rows = (last - first) * ROWS
    width = CHUNK * SLOTS
    return pl.pallas_call(
        functools.partial(row_kernel, first, last),
        out_shape=shape(2, last - first, ROWS, LANES),
        grid=(OWNERS // CHUNK,),
        in_specs=[
            pl.BlockSpec((CHUNK, 1, SLOTS), lambda k: (k, 0, 0)),
            pl.BlockSpec((CHUNK, 2, SLOTS), lambda k: (k, 0, 0)),
            pl.BlockSpec((CHUNK, 1, 1), lambda k: (k, 0, 0)),
        ],
        out_specs=pl.BlockSpec((2, last - first, ROWS, LANES), lambda k: (0, 0, 0, 0)),
        scratch_shapes=[
            pltpu.VMEM((rows, width), BF16),
            pltpu.VMEM((4 * LANES, width), BF16),
            pltpu.VMEM((rows, 4 * LANES), F32),
        ],
        compiler_params=PARAMS,
        cost_estimate=pl.CostEstimate(
            flops=2 * rows * 4 * LANES * OWNERS * SLOTS, bytes_accessed=1 << 20, transcendentals=0
        ),
    )(cell, value, count)


def gather_rims(strips, place_ref, turn_ref, store):
    for side in range(4):
        place = place_ref[side : side + 1, :]
        turns = turn_ref[side : side + 1, :]
        source = lax.bitwise_and(turns + (side + 2), 3)
        holder = lax.shift_right_logical(place, 7)
        lane = jnp.broadcast_to(lax.bitwise_and(place, LANES - 1), (ROWS, LANES))
        rows = [jnp.zeros((ROWS, LANES), F32) for _ in range(2)]
        for where, ref in enumerate(strips):
            for edge in range(4):
                hits = jnp.broadcast_to((holder == where) & (source == edge), (ROWS, LANES))
                for member in range(2):
                    picked = jnp.take_along_axis(
                        ref[member, edge], lane, axis=1, mode="promise_in_bounds"
                    )
                    rows[member] = jnp.where(hits, picked, rows[member])
        store(side, turns, rows)


def turned_vector(turns, rows):
    cosine = (turns == 0).astype(F32) - (turns == 2).astype(F32)
    sine = (turns == 1).astype(F32) - (turns == 3).astype(F32)
    return cosine * rows[0] - sine * rows[1], sine * rows[0] + cosine * rows[1]


def turned_stress(turns, rows):
    parity = (1 - 2 * lax.bitwise_and(turns, 1)).astype(F32)
    return rows[0], parity * rows[1]


def store_rim(pad, member, side, rim):
    if side == 0 or side == 2:
        pad[member, 0 if side == 0 else SIDE + 1, 8 : 8 + SIDE, :] = rim[0:SIDE]
    else:
        column = 7 if side == 1 else 8 + SIDE
        for i in range(SIDE):
            pad[member, i + 1, column : column + 1, :] = rim[i : i + 1]


def store_strips(out_ref, member, cell_of):
    out_ref[member, :, SIDE:ROWS, :] = jnp.zeros((4, ROWS - SIDE, LANES), F32)
    out_ref[member, 0, 0:SIDE, :] = cell_of(0, slice(0, SIDE))
    out_ref[member, 2, 0:SIDE, :] = cell_of(SIDE - 1, slice(0, SIDE))
    for i in range(SIDE):
        out_ref[member, 1, i : i + 1, :] = cell_of(i, slice(0, 1))
        out_ref[member, 3, i : i + 1, :] = cell_of(i, slice(SIDE - 1, SIDE))


def first_strips_kernel(velocity_ref, cover_ref, out_ref):
    for member in range(2):
        store_strips(
            out_ref,
            member,
            lambda i, j: velocity_ref[member, i, j, :] * cover_ref[i, j, :].astype(F32),
        )


def derivatives(pad, member, i):
    middle = slice(8, 8 + SIDE)
    east = 0.5 * (pad[member, i + 2, middle, :] - pad[member, i, middle, :])
    north = 0.5 * (pad[member, i + 1, 9 : 9 + SIDE, :] - pad[member, i + 1, 7 : 7 + SIDE, :])
    return east, north


def stress_targets(pad, strength, i):
    east_e, east_n = derivatives(pad, 0, i)
    north_e, north_n = derivatives(pad, 1, i)
    divergence = east_e + north_n
    tension = east_e - north_n
    shearing = east_n + north_e
    inverse = lax.rsqrt(
        divergence * divergence + (tension * tension + shearing * shearing) * 0.25 + 0.25
    )
    scaled = strength * inverse
    return (
        divergence * scaled - strength,
        0.25 * (tension * scaled),
        0.125 * (shearing * scaled),
    )


def face_strips(stress_ref, out_ref):
    out_ref[:, :, SIDE:ROWS, :] = jnp.zeros((2, 4, ROWS - SIDE, LANES), F32)
    for side, i in ((0, 0), (2, SIDE - 1)):
        out_ref[0, side, 0:SIDE, :] = 0.5 * (stress_ref[0, i] + stress_ref[1, i])
        out_ref[1, side, 0:SIDE, :] = stress_ref[2, i]
    for side, j in ((1, 0), (3, SIDE - 1)):
        for i in range(SIDE):
            cell = pl.ds(j, 1)
            out_ref[0, side, i : i + 1, :] = 0.5 * (
                stress_ref[0, i, cell, :] - stress_ref[1, i, cell, :]
            )
            out_ref[1, side, i : i + 1, :] = stress_ref[2, i, cell, :]


def stress_kernel(
    first,
    before_ref,
    own_ref,
    after_ref,
    place_ref,
    turn_ref,
    velocity_ref,
    cover_ref,
    strength_ref,
    *rest,
):
    if first:
        stress_ref, out_strips_ref, pad = rest
    else:
        old_ref, stress_ref, out_strips_ref, pad = rest

    def fill(i, carry):
        covered = cover_ref[i].astype(F32) if first else 1.0
        for member in range(2):
            pad[member, i + 1, 8 : 8 + SIDE, :] = velocity_ref[member, i] * covered
        return carry

    lax.fori_loop(0, SIDE, fill, 0, unroll=True)

    def store(side, turns, rows):
        for member, rim in enumerate(turned_vector(turns, rows)):
            store_rim(pad, member, side, rim)

    gather_rims((before_ref, own_ref, after_ref), place_ref, turn_ref, store)
    for i in range(SIDE):
        targets = stress_targets(pad, strength_ref[i], i)
        for member in range(3):
            old = 0.0 if first else old_ref[member, i]
            stress_ref[member, i] = old + 0.5 * (targets[member] - old)
    face_strips(stress_ref, out_strips_ref)


def moving_kernel(
    first,
    before_ref,
    own_ref,
    after_ref,
    place_ref,
    turn_ref,
    velocity_ref,
    cover_ref,
    mass_ref,
    stress_ref,
    forcing_ref,
    *rest,
):
    if first:
        out_ref, out_strips_ref, pad = rest
    else:
        out_ref, pad = rest
    for i in range(SIDE):
        first_stress, second_stress = stress_ref[0, i], stress_ref[1, i]
        pad[0, i + 1, 8 : 8 + SIDE, :] = 0.5 * (first_stress + second_stress)
        pad[1, i + 1, 8 : 8 + SIDE, :] = stress_ref[2, i]
        pad[2, i + 1, 8 : 8 + SIDE, :] = 0.5 * (first_stress - second_stress)

    def store(side, turns, rows):
        normal, shear = turned_stress(turns, rows)
        store_rim(pad, 0 if side in (0, 2) else 2, side, normal)
        store_rim(pad, 1, side, shear)

    gather_rims((before_ref, own_ref, after_ref), place_ref, turn_ref, store)
    middle = slice(8, 8 + SIDE)
    upper, lower = slice(9, 9 + SIDE), slice(7, 7 + SIDE)
    for i in range(SIDE):
        shear_east, shear_north = derivatives(pad, 1, i)
        force_east = 0.5 * (pad[0, i + 2, middle, :] - pad[0, i, middle, :]) + shear_north
        force_north = shear_east + 0.5 * (pad[2, i + 1, upper, :] - pad[2, i + 1, lower, :])
        covered = cover_ref[i].astype(F32)
        eastward, northward = velocity_ref[0, i], velocity_ref[1, i]
        if first:
            eastward, northward = eastward * covered, northward * covered
        mass = mass_ref[i]
        weight = covered / (4.0 * mass + 1.0)
        out_ref[0, i] = weight * (
            mass * (4.0 * eastward + 0.5 * northward) + force_east + forcing_ref[0, i, 0:SIDE, :]
        )
        out_ref[1, i] = weight * (
            mass * (4.0 * northward - 0.5 * eastward) + force_north + forcing_ref[1, i, 0:SIDE, :]
        )
    if first:
        for member in range(2):
            store_strips(out_strips_ref, member, lambda i, j: out_ref[member, i, j, :])


def call(kernel, outs, *args, specs=None, scratch=(), work=1 << 22):
    return pl.pallas_call(
        kernel,
        out_shape=outs,
        in_specs=specs or [VMEM] * len(args),
        out_specs=jax.tree.map(lambda _: VMEM, outs),
        scratch_shapes=list(scratch),
        compiler_params=PARAMS,
        cost_estimate=pl.CostEstimate(flops=work, bytes_accessed=1 << 22, transcendentals=0),
    )(*args)


def shards(
    velocity,
    strength,
    mass,
    ice_cover,
    neighbour,
    rotation,
    concentration,
    air_wind,
    ocean_current,
    drag,
    slot_cell,
    slot_count,
):
    devices = lax.axis_size(BOTH)
    here = lax.axis_index(BOTH)
    cat = lax.axis_index("cat")
    ring = [(i, (i + 1) % devices) for i in range(devices)]
    back = [(j, i) for i, j in ring]

    def both_ways(strips):
        return lax.ppermute(strips, BOTH, ring), lax.ppermute(strips, BOTH, back)

    strip_shape = shape(2, 4, ROWS, LANES)
    block = (SIDE, SIDE, LANES)

    fractions = concentration.reshape(OWNERS, 4, SLOTS)
    coefficients = jnp.broadcast_to(jnp.tile(drag, (EXTRA // 2, 1)), (EXTRA, SLOTS))

    def share_of(receiver):
        return jnp.concatenate(
            [lax.dynamic_index_in_dim(fractions, receiver, 1, keepdims=False), coefficients]
        )

    parts = [share_of(cat)]
    for step in (1, 2, 3):
        parts.append(
            lax.ppermute(
                share_of(lax.rem(cat + step, 4)), "cat", [(i, (i + step) % 4) for i in range(4)]
            )
        )
    winds = [
        lax.dynamic_index_in_dim(q.reshape(2, OWNERS, 4, SLOTS), cat, 2, keepdims=False)
        for q in (air_wind, ocean_current)
    ]
    summed = call(partial_kernel, shape(OWNERS, 2, SLOTS), *parts, *winds)
    arrived = lax.all_to_all(summed, "blocks", split_axis=0, concat_axis=0, tiled=True)

    place = lax.bitwise_and(neighbour - (here - 1) * LANES, devices * LANES - 1)
    strips = call(first_strips_kernel, strip_shape, velocity, ice_cover)
    before, after = both_ways(strips)
    pad2 = [pltpu.VMEM((2, ROWS, 48, LANES), F32)]
    pad3 = [pltpu.VMEM((3, ROWS, 48, LANES), F32)]
    stress, faces = call(
        functools.partial(stress_kernel, True),
        (shape(3, *block), strip_shape),
        before, strips, after, place, rotation, velocity, ice_cover, strength,
        scratch=pad2,
    )
    before, after = both_ways(faces)

    forcing = scatter_rows(slot_cell, arrived, slot_count[:, :, None], 0, SIDE)

    moving, strips = call(
        functools.partial(moving_kernel, True),
        (shape(2, *block), strip_shape),
        before, faces, after, place, rotation, velocity, ice_cover, mass, stress, forcing,
        scratch=pad3,
    )
    before, after = both_ways(strips)
    stress, faces = call(
        functools.partial(stress_kernel, False),
        (shape(3, *block), strip_shape),
        before, strips, after, place, rotation, moving, ice_cover, strength, stress,
        scratch=pad2,
    )
    before, after = both_ways(faces)
    moving = call(
        functools.partial(moving_kernel, False),
        shape(2, *block),
        before, faces, after, place, rotation, moving, ice_cover, mass, stress, forcing,
        scratch=pad3,
    )
    return (moving, stress)


def solution(mesh):
    placed = (
        P(None, None, None, BOTH),
        P(None, None, BOTH),
        P(None, None, BOTH),
        P(None, None, BOTH),
        P(None, BOTH),
        P(None, BOTH),
        P("cat", "blocks", None, None),
        P(None, "blocks", None, None),
        P(None, "blocks", None, None),
        P(None, "cat"),
        P(None, BOTH, None),
        P(None, BOTH),
    )
    return jax.shard_map(
        shards,
        mesh=mesh,
        in_specs=placed,
        out_specs=(P(None, None, None, BOTH), P(None, None, None, BOTH)),
        check_vma=False,
    )
```

```python
import functools

import jax
import jax.numpy as jnp
from jax import lax
from jax.experimental import pallas as pl
from jax.experimental.pallas import tpu as pltpu
from jax.sharding import PartitionSpec as P

F32 = jnp.float32
BF16 = jnp.bfloat16
I32 = jnp.int32

SIDE = 30
ROWS = 32
LANES = 128
OWNERS = 64
SLOTS = 256
EXTRA = 8
CHUNK = 8
INSIDE = SIDE - 4
HALF = INSIDE // 2
HALF_ROWS = 352
BOTH = ("blocks", "cat")

PARAMS = pltpu.CompilerParams(vmem_limit_bytes=6 * 1024 * 1024)
SCATTER_PARAMS = pltpu.CompilerParams(vmem_limit_bytes=8 * 1024 * 1024)
ALONE_PARAMS = pltpu.CompilerParams(vmem_limit_bytes=60 * 1024 * 1024)
ANY = pl.BlockSpec(memory_space=pl.ANY)
VMEM = pl.BlockSpec(memory_space=pltpu.VMEM)
SMEM = pl.BlockSpec(memory_space=pltpu.SMEM)


def shape(*dims, dtype=F32):
    return jax.ShapeDtypeStruct(dims, dtype)


def fill_halves(halves, value_of):
    for half in range(2):
        halves[half] = value_of(slice(half * LANES, half * LANES + LANES))


def quarter(halves, half, receiver):
    return halves[half, pl.ds(receiver, OWNERS, stride=4), :]


def pack_kernel(conc_ref, drag_ref, *rest):
    outs, halves = rest[:4], rest[4]
    cat = lax.axis_index("cat")
    row = lax.broadcasted_iota(I32, (EXTRA, SLOTS), 0)
    coefficients = jnp.where(row == 0, drag_ref[0, 0], drag_ref[0, 1])
    fill_halves(halves, lambda lanes: conc_ref[0, 0, :, lanes])
    for step, out_ref in enumerate(outs):
        receiver = lax.bitwise_and(cat + step, 3)
        for half in range(2):
            lanes = slice(half * LANES, half * LANES + LANES)
            out_ref[0:OWNERS, lanes] = quarter(halves, half, receiver)
        out_ref[OWNERS : OWNERS + EXTRA, :] = coefficients


def partial_kernel(mine_ref, first_ref, second_ref, third_ref, air_ref, ocean_ref, after_ref, *rest):
    out_ref, wind = rest
    cat = lax.axis_index("cat")
    parts = (mine_ref, first_ref, second_ref, third_ref)
    for which, ref in enumerate((air_ref, ocean_ref)):
        for member in range(2):
            fill_halves(wind.at[which, member], lambda lanes: ref[member, 0, :, lanes])
    for half in range(2):
        lanes = slice(half * LANES, half * LANES + LANES)
        totals = [0.0, 0.0]
        for which in range(2):
            weight = jnp.zeros((OWNERS, LANES), F32)
            at = OWNERS + which
            for part in parts:
                weight += part[0:OWNERS, lanes] * part[at : at + 1, lanes]
            east = quarter(wind.at[which, 0], half, cat)
            north = quarter(wind.at[which, 1], half, cat)
            weight *= jnp.sqrt(east * east + north * north)
            totals[0] += weight * east
            totals[1] += weight * north
        out_ref[:, 0, lanes] = totals[0]
        out_ref[:, 1, lanes] = totals[1]


def split_lanes(lane_hits, value):
    high = value.astype(BF16).astype(F32)
    return (
        jnp.where(lane_hits, high, 0.0).astype(BF16),
        jnp.where(lane_hits, value - high, 0.0).astype(BF16),
    )


def spread_values(cell_ref, value_ref, count_ref, spread, index):
    block = lax.broadcasted_iota(I32, (LANES, SLOTS), 0)
    slot = lax.broadcasted_iota(I32, (1, SLOTS), 1)
    columns = pl.ds(index * SLOTS, SLOTS)
    lane_hits = block == lax.bitwise_and(cell_ref[index], LANES - 1)
    live = slot < count_ref[0, pl.program_id(0) * CHUNK + index]
    for member in range(2):
        value = jnp.where(live, value_ref[index, member : member + 1, :], 0.0)
        high, low = split_lanes(lane_hits, value)
        spread[pl.ds(member * 2 * LANES, LANES), columns] = high
        spread[pl.ds(member * 2 * LANES + LANES, LANES), columns] = low


def cell_number(cell):
    return lax.shift_right_logical(cell, 7)


def accumulate(total, hot, spread):
    total[...] += lax.dot_general(
        hot[...], spread[...], (((1,), (1,)), ((), ())), preferred_element_type=F32
    )


def summed_terms(total, member):
    at = member * 2 * LANES
    return total[:, at : at + LANES] + total[:, at + LANES : at + 2 * LANES]


def edge_kernel(cell_ref, value_ref, count_ref, after_ref, out_ref, hot, spread, total):
    step = pl.program_id(0)

    @pl.when(step == 0)
    def _():
        total[...] = jnp.zeros_like(total)

    along = lax.broadcasted_iota(I32, (ROWS, SLOTS), 0)
    for index in range(CHUNK):
        number = cell_number(cell_ref[index])
        east = lax.shift_right_logical(number * 2185, 16)
        north = number - east * SIDE
        columns = pl.ds(index * SLOTS, SLOTS)
        east_hot = (along == east).astype(F32).astype(BF16)
        north_hot = (along == north).astype(F32).astype(BF16)
        empty = jnp.zeros_like(east_hot)
        for layer in range(2):
            for side, here in enumerate(
                (east == layer, north == layer, east == SIDE - 1 - layer, north == SIDE - 1 - layer)
            ):
                hot[pl.ds((layer * 4 + side) * ROWS, ROWS), columns] = jnp.where(
                    here, east_hot if side % 2 else north_hot, empty
                )
        spread_values(cell_ref, value_ref, count_ref, spread, index)
    accumulate(total, hot, spread)

    @pl.when(step == pl.num_programs(0) - 1)
    def _():
        for member in range(2):
            out_ref[member] = summed_terms(total, member).reshape(8, ROWS, LANES)


def inside_kernel(first, cell_ref, value_ref, count_ref, out_ref, hot, spread, total):
    step = pl.program_id(0)

    @pl.when(step == 0)
    def _():
        total[...] = jnp.zeros_like(total)

    row = lax.broadcasted_iota(I32, (HALF_ROWS, SLOTS), 0)
    east = lax.shift_right_logical(row * 2521, 16)
    wanted = jnp.where(
        east < HALF, (east + first) * SIDE + 2 + (row - east * INSIDE), -1
    )
    for index in range(CHUNK):
        columns = pl.ds(index * SLOTS, SLOTS)
        hits = wanted == cell_number(cell_ref[index])
        hot[:, columns] = hits.astype(F32).astype(BF16)
        spread_values(cell_ref, value_ref, count_ref, spread, index)
    accumulate(total, hot, spread)

    @pl.when(step == pl.num_programs(0) - 1)
    def _():
        for member in range(2):
            out_ref[member] = summed_terms(total, member)


def scatter_call(kernel, rows, outs, cell, value, count, *more):
    width = CHUNK * SLOTS

    def whole(ref):
        return pl.BlockSpec(ref.shape, lambda k, rank=len(ref.shape): (0,) * rank)

    return pl.pallas_call(
        kernel,
        out_shape=outs,
        grid=(OWNERS // CHUNK,),
        in_specs=[
            pl.BlockSpec((CHUNK, 1, SLOTS), lambda k: (k, 0, 0)),
            pl.BlockSpec((CHUNK, 2, SLOTS), lambda k: (k, 0, 0)),
            SMEM,
        ]
        + [ANY] * len(more),
        out_specs=jax.tree.map(whole, outs),
        scratch_shapes=[
            pltpu.VMEM((rows, width), BF16),
            pltpu.VMEM((4 * LANES, width), BF16),
            pltpu.VMEM((rows, 4 * LANES), F32),
        ],
        compiler_params=SCATTER_PARAMS,
        cost_estimate=pl.CostEstimate(
            flops=2 * rows * 4 * LANES * OWNERS * SLOTS, bytes_accessed=1 << 20, transcendentals=0
        ),
    )(cell, value, count, *more)


def gather_rims(strips, neighbour_ref, turn_ref, store):
    devices = lax.axis_size(BOTH)
    start = (lax.axis_index(BOTH) - 1) * LANES
    for side in range(4):
        place = lax.rem(
            neighbour_ref[side : side + 1, :] - start + devices * LANES, devices * LANES
        )
        turns = turn_ref[side : side + 1, :]
        source = lax.bitwise_and(turns + (side + 2), 3)
        holder = lax.shift_right_logical(place, 7)
        lane = jnp.broadcast_to(lax.bitwise_and(place, LANES - 1), (ROWS, LANES))
        rows = [jnp.zeros((ROWS, LANES), F32) for _ in range(2)]
        for where, ref in enumerate(strips):
            for edge in range(4):
                hits = jnp.broadcast_to((holder == where) & (source == edge), (ROWS, LANES))
                for member in range(2):
                    picked = jnp.take_along_axis(
                        ref[member, edge], lane, axis=1, mode="promise_in_bounds"
                    )
                    rows[member] = jnp.where(hits, picked, rows[member])
        store(side, turns, rows)


def turned_vector(turns, rows):
    cosine = (turns == 0).astype(F32) - (turns == 2).astype(F32)
    sine = (turns == 1).astype(F32) - (turns == 3).astype(F32)
    return cosine * rows[0] - sine * rows[1], sine * rows[0] + cosine * rows[1]


def turned_stress(turns, rows):
    parity = (1 - 2 * lax.bitwise_and(turns, 1)).astype(F32)
    return rows[0], parity * rows[1]


def store_rim(pad, member, side, rim):
    if side == 0 or side == 2:
        pad[member, 0 if side == 0 else SIDE + 1, 8 : 8 + SIDE, :] = rim[0:SIDE]
    else:
        column = 7 if side == 1 else 8 + SIDE
        for i in range(SIDE):
            pad[member, i + 1, column : column + 1, :] = rim[i : i + 1]


def store_strips(out_ref, member, cell_of, layer=0):
    far = SIDE - 1 - layer
    out_ref[member, :, SIDE:ROWS, :] = jnp.zeros((4, ROWS - SIDE, LANES), F32)
    out_ref[member, 0, 0:SIDE, :] = cell_of(layer, slice(0, SIDE))
    out_ref[member, 2, 0:SIDE, :] = cell_of(far, slice(0, SIDE))
    for i in range(SIDE):
        out_ref[member, 1, i : i + 1, :] = cell_of(i, slice(layer, layer + 1))
        out_ref[member, 3, i : i + 1, :] = cell_of(i, slice(far, far + 1))


def cell_rows(i, member, cells=slice(0, SIDE)):
    start = 2 * (SIDE * i + cells.start) + member
    count = cells.stop - cells.start
    return slice(start, start + 1) if count == 1 else pl.ds(start, count, stride=2)


def run_copies(pairs, sems):
    copies = [
        pltpu.make_async_copy(source, target, sems.at[at])
        for at, (source, target) in enumerate(pairs)
    ]
    for copy in copies:
        copy.start()
    return copies


VELOCITY_CUTS = ((0, 448), (448, 448), (896, 448), (1344, 456))
COVER_CUTS = ((0, 10), (10, 10), (20, 10))


def outer_strips_kernel(velocity_hbm, cover_hbm, out_ref, velocity_ref, cover_ref, sems):
    pairs = [
        (velocity_hbm.at[pl.ds(start, size)], velocity_ref.at[pl.ds(start, size)])
        for start, size in VELOCITY_CUTS
    ] + [
        (cover_hbm.at[pl.ds(start, size)], cover_ref.at[pl.ds(start, size)])
        for start, size in COVER_CUTS
    ]
    for copy in run_copies(pairs, sems):
        copy.wait()
    for member in range(2):
        store_strips(
            out_ref,
            member,
            lambda i, j: velocity_ref[cell_rows(i, member, j), :] * cover_ref[i, j, :].astype(F32),
        )


def weight_of(cover, mass):
    return cover.astype(F32) / (4.0 * mass + 1.0)


def inner_strips_kernel(
    velocity_ref, cover_ref, strength_ref, mass_ref, inner_ref, strength_strips_ref, weight_strips_ref
):
    for member in range(2):
        store_strips(
            inner_ref,
            member,
            lambda i, j: velocity_ref[cell_rows(i, member, j), :] * cover_ref[i, j, :].astype(F32),
            1,
        )
    store_strips(strength_strips_ref, 0, lambda i, j: strength_ref[i, j, :])
    for layer in range(2):
        at = slice(4 * layer, 4 * layer + 4)
        store_strips(
            weight_strips_ref.at[:, at],
            0,
            lambda i, j: weight_of(cover_ref[i, j, :], mass_ref[i, j, :]),
            layer,
        )


def derivatives(pad, member, i):
    middle = slice(8, 8 + SIDE)
    east = 0.5 * (pad[member, i + 2, middle, :] - pad[member, i, middle, :])
    north = 0.5 * (pad[member, i + 1, 9 : 9 + SIDE, :] - pad[member, i + 1, 7 : 7 + SIDE, :])
    return east, north


def targets_of(east_e, east_n, north_e, north_n, strength):
    divergence = east_e + north_n
    tension = east_e - north_n
    shearing = east_n + north_e
    inverse = lax.rsqrt(
        divergence * divergence + (tension * tension + shearing * shearing) * 0.25 + 0.25
    )
    scaled = strength * inverse
    return (
        divergence * scaled - strength,
        0.25 * (tension * scaled),
        0.125 * (shearing * scaled),
    )


def stress_targets(pad, strength, i):
    return targets_of(*derivatives(pad, 0, i), *derivatives(pad, 1, i), strength)


def forces(pad, i):
    middle = slice(8, 8 + SIDE)
    upper, lower = slice(9, 9 + SIDE), slice(7, 7 + SIDE)
    shear_east, shear_north = derivatives(pad, 1, i)
    force_east = 0.5 * (pad[0, i + 2, middle, :] - pad[0, i, middle, :]) + shear_north
    force_north = shear_east + 0.5 * (pad[2, i + 1, upper, :] - pad[2, i + 1, lower, :])
    return force_east, force_north


def stress_rims_kernel(before_ref, own_ref, after_ref, neighbour_ref, turn_ref, out_ref):
    def store(side, turns, rows):
        for member, rim in enumerate(turned_stress(turns, rows)):
            out_ref[member, side] = rim

    gather_rims((before_ref, own_ref, after_ref), neighbour_ref, turn_ref, store)


def fill_stress(pad, stress_ref):
    for i in range(SIDE):
        first_stress, second_stress = stress_ref[0, i], stress_ref[1, i]
        pad[0, i + 1, 8 : 8 + SIDE, :] = 0.5 * (first_stress + second_stress)
        pad[1, i + 1, 8 : 8 + SIDE, :] = stress_ref[2, i]
        pad[2, i + 1, 8 : 8 + SIDE, :] = 0.5 * (first_stress - second_stress)


def store_stress_rim(pad, side, normal, shear):
    store_rim(pad, 0 if side in (0, 2) else 2, side, normal)
    store_rim(pad, 1, side, shear)


def base_kernel(
    stress_rims_ref,
    rims_ref,
    velocity_ref,
    cover_ref,
    mass_ref,
    strength_ref,
    forcing_ref,
    weight_ref,
    base_ref,
    stress_ref,
    outer_ref,
    inner_ref,
    line,
    pad,
):
    for i in range(SIDE):
        covered = cover_ref[i].astype(F32)
        for member in range(2):
            line[member, i + 1, 8 : 8 + SIDE, :] = velocity_ref[cell_rows(i, member), :] * covered
    for member in range(2):
        for side in range(4):
            store_rim(line, member, side, rims_ref[member, side])
    for i in range(SIDE):
        targets = stress_targets(line, strength_ref[i], i)
        for member in range(3):
            stress_ref[member, i] = 0.5 * targets[member]
    fill_stress(pad, stress_ref)
    for side in range(4):
        store_stress_rim(pad, side, stress_rims_ref[0, side], stress_rims_ref[1, side])
    for i in range(SIDE):
        force_east, force_north = forces(pad, i)
        eastward = line[0, i + 1, 8 : 8 + SIDE, :]
        northward = line[1, i + 1, 8 : 8 + SIDE, :]
        mass = mass_ref[i]
        weight = weight_of(cover_ref[i], mass)
        base_ref[0, i] = weight * (mass * (4.0 * eastward + 0.5 * northward) + force_east)
        base_ref[1, i] = weight * (mass * (4.0 * northward - 0.5 * eastward) + force_north)
    for layer, out_ref in enumerate((outer_ref, inner_ref)):
        at = slice(4 * layer, 4 * layer + 4)
        for member in range(2):
            store_strips(out_ref, member, lambda i, j: base_ref[member, i, j, :], layer)
            out_ref[member] += weight_ref[0, at] * forcing_ref[member, at]


def edge_stress_kernel(
    before_ref,
    outer_ref,
    after_ref,
    inner_ref,
    neighbour_ref,
    turn_ref,
    strength_ref,
    *rest,
    opening,
):
    faces_ref, rims_ref, line = rest[-3:]

    def store(side, turns, rows):
        for member, rim in enumerate(turned_vector(turns, rows)):
            rims_ref[member, side] = rim

    gather_rims((before_ref, outer_ref, after_ref), neighbour_ref, turn_ref, store)
    faces_ref[:, :, SIDE:ROWS, :] = jnp.zeros((2, 4, ROWS - SIDE, LANES), F32)
    for side in range(4):
        end = 0 if side < 2 else SIDE - 1
        across, beside = [], []
        for member in range(2):
            line[member, side, 8 : 8 + SIDE, :] = outer_ref[member, side, 0:SIDE, :]
            lower, upper = (1, 3) if side % 2 == 0 else (0, 2)
            line[member, side, 7:8, :] = rims_ref[member, lower, end : end + 1, :]
            line[member, side, 8 + SIDE : 9 + SIDE, :] = rims_ref[member, upper, end : end + 1, :]
            step = 0.5 * (inner_ref[member, side, 0:SIDE, :] - rims_ref[member, side, 0:SIDE, :])
            across.append(step if side < 2 else -step)
            beside.append(
                0.5 * (line[member, side, 9 : 9 + SIDE, :] - line[member, side, 7 : 7 + SIDE, :])
            )
        east, north = (across, beside) if side % 2 == 0 else (beside, across)
        first, second, shear = targets_of(
            east[0], north[0], east[1], north[1], strength_ref[0, side, 0:SIDE, :]
        )
        normal = 0.5 * (first + second) if side % 2 == 0 else 0.5 * (first - second)
        for member, target in enumerate((normal, shear)):
            old = 0.0 if opening else rest[0][member, side, 0:SIDE, :]
            faces_ref[member, side, 0:SIDE, :] = old + 0.5 * (target - old)


def second_stress_kernel(
    base_ref,
    cover_ref,
    mass_ref,
    low_ref,
    high_ref,
    outer_ref,
    inner_ref,
    rims_ref,
    strength_ref,
    old_ref,
    moving_ref,
    stress_ref,
    stress_hbm,
    pad,
    sems,
):
    for member in range(2):
        for side in range(4):
            store_rim(pad, member, side, rims_ref[member, side])
        for i, ref, side in (
            (0, outer_ref, 0),
            (1, inner_ref, 0),
            (SIDE - 2, inner_ref, 2),
            (SIDE - 1, outer_ref, 2),
        ):
            pad[member, i + 1, 8 : 8 + SIDE, :] = ref[member, side, 0:SIDE, :]
        for i in range(2, SIDE - 2):
            for j, ref, side in (
                (0, outer_ref, 1),
                (1, inner_ref, 1),
                (SIDE - 2, inner_ref, 3),
                (SIDE - 1, outer_ref, 3),
            ):
                pad[member, i + 1, 8 + j : 9 + j, :] = ref[member, side, i : i + 1, :]
    inside = slice(2, SIDE - 2)
    for i in range(2, SIDE - 2):
        weight = weight_of(cover_ref[i, inside, :], mass_ref[i, inside, :])
        ref, at = (low_ref, i - 2) if i < 2 + HALF else (high_ref, i - 2 - HALF)
        for member in range(2):
            pad[member, i + 1, 10 : 10 + INSIDE, :] = base_ref[member, i, inside, :] + weight * (
                ref[member, at * INSIDE : at * INSIDE + INSIDE, :]
            )
    copies = []
    for i in range(SIDE):
        targets = stress_targets(pad, strength_ref[i], i)
        for member in range(3):
            old = old_ref[member, i]
            stress_ref[member, i] = old + 0.5 * (targets[member] - old)
        for member in range(2):
            moving_ref[member, i] = pad[member, i + 1, 8 : 8 + SIDE, :]
        if i % 10 == 9:
            part = pl.ds(i - 9, 10)
            copies.append(
                pltpu.make_async_copy(
                    stress_ref.at[:, part], stress_hbm.at[:, part], sems.at[i // 10]
                )
            )
            copies[-1].start()
    for copy in copies:
        copy.wait()


def last_kernel(
    before_ref,
    own_ref,
    after_ref,
    neighbour_ref,
    turn_ref,
    moving_ref,
    base_ref,
    cover_ref,
    mass_ref,
    stress_ref,
    out_hbm,
    pad,
    out_ref,
    sems,
):
    copies = []
    fill_stress(pad, stress_ref)

    def store(side, turns, rows):
        store_stress_rim(pad, side, *turned_stress(turns, rows))

    gather_rims((before_ref, own_ref, after_ref), neighbour_ref, turn_ref, store)
    for i in range(SIDE):
        force_east, force_north = forces(pad, i)
        eastward, northward = moving_ref[0, i], moving_ref[1, i]
        mass = mass_ref[i]
        weight = weight_of(cover_ref[i], mass)
        out_ref[cell_rows(i, 0), :] = weight * (
            mass * (4.0 * eastward + 0.5 * northward) + force_east
        ) + (eastward - base_ref[0, i])
        out_ref[cell_rows(i, 1), :] = weight * (
            mass * (4.0 * northward - 0.5 * eastward) + force_north
        ) + (northward - base_ref[1, i])
        if i % 6 == 5:
            part = pl.ds(60 * (i - 5), 360)
            copies.append(
                pltpu.make_async_copy(out_ref.at[part], out_hbm.at[part], sems.at[i // 6])
            )
            copies[-1].start()
    for copy in copies:
        copy.wait()


def call(kernel, outs, *args, specs=None, out_specs=None, scratch=(), work=1 << 22, params=PARAMS):
    return pl.pallas_call(
        kernel,
        out_shape=outs,
        in_specs=specs or [VMEM] * len(args),
        out_specs=out_specs or jax.tree.map(lambda _: VMEM, outs),
        scratch_shapes=list(scratch),
        compiler_params=params,
        cost_estimate=pl.CostEstimate(flops=work, bytes_accessed=1 << 22, transcendentals=0),
    )(*args)


def shards(
    velocity,
    strength,
    mass,
    ice_cover,
    neighbour,
    rotation,
    concentration,
    air_wind,
    ocean_current,
    drag,
    slot_cell,
    slot_count,
):
    devices = lax.axis_size(BOTH)
    ring = [(i, (i + 1) % devices) for i in range(devices)]
    back = [(j, i) for i, j in ring]

    def both_ways(strips):
        return lax.ppermute(strips, BOTH, ring), lax.ppermute(strips, BOTH, back)

    strip_shape = shape(2, 4, ROWS, LANES)
    block = (SIDE, SIDE, LANES)
    pad2 = [pltpu.VMEM((2, ROWS, 48, LANES), F32)]
    pad3 = [pltpu.VMEM((3, ROWS, 48, LANES), F32)]
    count = slot_count.reshape(1, OWNERS)

    sems = pltpu.SemaphoreType.DMA
    velocity = jnp.transpose(velocity, (1, 2, 0, 3)).reshape(2 * SIDE * SIDE, LANES)
    outer = call(
        outer_strips_kernel,
        strip_shape,
        velocity,
        ice_cover,
        specs=[ANY, ANY],
        scratch=[pltpu.VMEM((2 * SIDE * SIDE, LANES), F32), pltpu.VMEM(block, I32), sems((7,))],
        params=ALONE_PARAMS,
    )
    before, after = both_ways(outer)
    inner, strength_strips, weight_strips = call(
        inner_strips_kernel,
        (strip_shape, shape(1, 4, ROWS, LANES), shape(1, 8, ROWS, LANES)),
        velocity, ice_cover, strength, mass,
    )

    packed = call(
        pack_kernel,
        [shape(OWNERS + EXTRA, SLOTS)] * 4,
        concentration,
        drag.reshape(1, 2),
        specs=[VMEM, SMEM],
        scratch=[pltpu.VMEM((2, 4 * OWNERS, LANES), F32)],
    )
    parts = [packed[0]] + [
        lax.ppermute(packed[step], "cat", [(i, (i + step) % 4) for i in range(4)])
        for step in (1, 2, 3)
    ]

    line = [pltpu.VMEM((2, 4, 48, LANES), F32)]
    faces, rims = call(
        functools.partial(edge_stress_kernel, opening=True),
        (strip_shape, strip_shape),
        before, outer, after, inner, neighbour, rotation, strength_strips, *parts[1:],
        specs=[VMEM] * 7 + [ANY] * 3,
        scratch=line,
    )
    before, after = both_ways(faces)

    summed = call(
        partial_kernel,
        shape(OWNERS, 2, SLOTS),
        *parts, air_wind, ocean_current, faces,
        specs=[VMEM] * 6 + [ANY],
        scratch=[pltpu.VMEM((2, 2, 2, 4 * OWNERS, LANES), F32)],
    )
    arrived = lax.all_to_all(summed, "blocks", split_axis=0, concat_axis=0, tiled=True)

    stress_rims = call(
        stress_rims_kernel, strip_shape, before, faces, after, neighbour, rotation, work=1 << 34
    )
    forcing = scatter_call(
        edge_kernel, 8 * ROWS, shape(2, 8, ROWS, LANES), slot_cell, arrived, count, stress_rims
    )
    base, stress, outer, inner = call(
        base_kernel,
        (shape(2, *block), shape(3, *block), strip_shape, strip_shape),
        stress_rims, rims, velocity, ice_cover, mass, strength, forcing, weight_strips,
        scratch=pad2 + pad3,
    )
    before, after = both_ways(outer)
    low = scatter_call(
        functools.partial(inside_kernel, 2), HALF_ROWS, shape(2, HALF_ROWS, LANES),
        slot_cell, arrived, count,
    )
    faces, rims = call(
        functools.partial(edge_stress_kernel, opening=False),
        (strip_shape, strip_shape),
        before, outer, after, inner, neighbour, rotation, strength_strips, faces,
        scratch=line,
    )
    before, after = both_ways(faces)
    high = scatter_call(
        functools.partial(inside_kernel, 2 + HALF), HALF_ROWS, shape(2, HALF_ROWS, LANES),
        slot_cell, arrived, count,
    )
    moving, kept, stress = call(
        second_stress_kernel,
        (shape(2, *block), shape(3, *block), shape(3, *block)),
        base, ice_cover, mass, low, high, outer, inner, rims, strength, stress,
        out_specs=(VMEM, VMEM, ANY),
        scratch=pad2 + [sems((3,))],
    )
    moving = call(
        last_kernel,
        shape(2 * SIDE * SIDE, LANES),
        before, faces, after, neighbour, rotation, moving, base, ice_cover, mass, kept,
        out_specs=ANY,
        scratch=pad3 + [pltpu.VMEM((2 * SIDE * SIDE, LANES), F32), sems((5,))],
    )
    moving = jnp.transpose(moving.reshape(SIDE, SIDE, 2, LANES), (2, 0, 1, 3))
    return (moving, stress)


def solution(mesh):
    placed = (
        P(None, None, None, BOTH),
        P(None, None, BOTH),
        P(None, None, BOTH),
        P(None, None, BOTH),
        P(None, BOTH),
        P(None, BOTH),
        P("cat", "blocks", None, None),
        P(None, "blocks", None, None),
        P(None, "blocks", None, None),
        P(None, "cat"),
        P(None, BOTH, None),
        P(None, BOTH),
    )
    return jax.shard_map(
        shards,
        mesh=mesh,
        in_specs=placed,
        out_specs=(P(None, None, None, BOTH), P(None, None, None, BOTH)),
        check_vma=False,
    )
```

```python
import functools

import jax
import jax.numpy as jnp
from jax import lax
from jax.experimental import pallas as pl
from jax.experimental.pallas import tpu as pltpu
from jax.sharding import PartitionSpec as P

F32 = jnp.float32
BF16 = jnp.bfloat16
I32 = jnp.int32

SIDE = 30
ROWS = 32
LANES = 128
OWNERS = 64
SLOTS = 256
EXTRA = 8
CHUNK = 16
INSIDE = SIDE - 4
HALF = INSIDE // 2
HALF_ROWS = 352
BOTH = ("blocks", "cat")

PARAMS = pltpu.CompilerParams(vmem_limit_bytes=6 * 1024 * 1024)
SCATTER_PARAMS = pltpu.CompilerParams(vmem_limit_bytes=12 * 1024 * 1024)
ALONE_PARAMS = pltpu.CompilerParams(vmem_limit_bytes=60 * 1024 * 1024)
ANY = pl.BlockSpec(memory_space=pl.ANY)
VMEM = pl.BlockSpec(memory_space=pltpu.VMEM)
SMEM = pl.BlockSpec(memory_space=pltpu.SMEM)


def shape(*dims, dtype=F32):
    return jax.ShapeDtypeStruct(dims, dtype)


def fill_halves(halves, value_of):
    for half in range(2):
        halves[half] = value_of(slice(half * LANES, half * LANES + LANES))


def quarter(halves, half, receiver):
    return halves[half, pl.ds(receiver, OWNERS, stride=4), :]


def pack_kernel(conc_ref, drag_ref, *rest):
    outs, halves = rest[:4], rest[4]
    cat = lax.axis_index("cat")
    row = lax.broadcasted_iota(I32, (EXTRA, SLOTS), 0)
    coefficients = jnp.where(row == 0, drag_ref[0, 0], drag_ref[0, 1])
    fill_halves(halves, lambda lanes: conc_ref[0, 0, :, lanes])
    for step, out_ref in enumerate(outs):
        receiver = lax.bitwise_and(cat + step, 3)
        for half in range(2):
            lanes = slice(half * LANES, half * LANES + LANES)
            out_ref[0:OWNERS, lanes] = quarter(halves, half, receiver)
        out_ref[OWNERS : OWNERS + EXTRA, :] = coefficients


def partial_kernel(mine_ref, first_ref, second_ref, third_ref, air_ref, ocean_ref, out_ref, wind):
    cat = lax.axis_index("cat")
    parts = (mine_ref, first_ref, second_ref, third_ref)
    for which, ref in enumerate((air_ref, ocean_ref)):
        for member in range(2):
            fill_halves(wind.at[which, member], lambda lanes: ref[member, 0, :, lanes])
    for half in range(2):
        lanes = slice(half * LANES, half * LANES + LANES)
        totals = [0.0, 0.0]
        for which in range(2):
            weight = jnp.zeros((OWNERS, LANES), F32)
            at = OWNERS + which
            for part in parts:
                weight += part[0:OWNERS, lanes] * part[at : at + 1, lanes]
            east = quarter(wind.at[which, 0], half, cat)
            north = quarter(wind.at[which, 1], half, cat)
            weight *= jnp.sqrt(east * east + north * north)
            totals[0] += weight * east
            totals[1] += weight * north
        out_ref[:, 0, lanes] = totals[0]
        out_ref[:, 1, lanes] = totals[1]


def split_lanes(lane_hits, value):
    high = value.astype(BF16).astype(F32)
    return (
        jnp.where(lane_hits, high, 0.0).astype(BF16),
        jnp.where(lane_hits, value - high, 0.0).astype(BF16),
    )


def spread_values(cell_ref, value_ref, count_ref, spread, index):
    block = lax.broadcasted_iota(I32, (LANES, SLOTS), 0)
    slot = lax.broadcasted_iota(I32, (1, SLOTS), 1)
    columns = pl.ds(index * SLOTS, SLOTS)
    lane_hits = block == lax.bitwise_and(cell_ref[index], LANES - 1)
    live = slot < count_ref[0, pl.program_id(0) * CHUNK + index]
    for member in range(2):
        value = jnp.where(live, value_ref[index, member : member + 1, :], 0.0)
        high, low = split_lanes(lane_hits, value)
        spread[pl.ds(member * 2 * LANES, LANES), columns] = high
        spread[pl.ds(member * 2 * LANES + LANES, LANES), columns] = low


def cell_number(cell):
    return lax.shift_right_logical(cell, 7)


def accumulate(total, hot, spread):
    total[...] += lax.dot_general(
        hot[...], spread[...], (((1,), (1,)), ((), ())), preferred_element_type=F32
    )


def summed_terms(total, member):
    at = member * 2 * LANES
    return total[:, at : at + LANES] + total[:, at + LANES : at + 2 * LANES]


def edge_kernel(cell_ref, value_ref, count_ref, after_ref, out_ref, hot, spread, total):
    step = pl.program_id(0)

    @pl.when(step == 0)
    def _():
        total[...] = jnp.zeros_like(total)

    along = lax.broadcasted_iota(I32, (ROWS, SLOTS), 0)
    for index in range(CHUNK):
        number = cell_number(cell_ref[index])
        east = lax.shift_right_logical(number * 2185, 16)
        north = number - east * SIDE
        columns = pl.ds(index * SLOTS, SLOTS)
        east_hot = (along == east).astype(F32).astype(BF16)
        north_hot = (along == north).astype(F32).astype(BF16)
        empty = jnp.zeros_like(east_hot)
        for layer in range(2):
            for side, here in enumerate(
                (east == layer, north == layer, east == SIDE - 1 - layer, north == SIDE - 1 - layer)
            ):
                hot[pl.ds((layer * 4 + side) * ROWS, ROWS), columns] = jnp.where(
                    here, east_hot if side % 2 else north_hot, empty
                )
        spread_values(cell_ref, value_ref, count_ref, spread, index)
    accumulate(total, hot, spread)

    @pl.when(step == pl.num_programs(0) - 1)
    def _():
        for member in range(2):
            out_ref[member] = summed_terms(total, member).reshape(8, ROWS, LANES)


def inside_kernel(first, cell_ref, value_ref, count_ref, out_ref, hot, spread, total):
    step = pl.program_id(0)

    @pl.when(step == 0)
    def _():
        total[...] = jnp.zeros_like(total)

    row = lax.broadcasted_iota(I32, (HALF_ROWS, SLOTS), 0)
    east = lax.shift_right_logical(row * 2521, 16)
    wanted = jnp.where(
        east < HALF, (east + first) * SIDE + 2 + (row - east * INSIDE), -1
    )
    for index in range(CHUNK):
        columns = pl.ds(index * SLOTS, SLOTS)
        hits = wanted == cell_number(cell_ref[index])
        hot[:, columns] = hits.astype(F32).astype(BF16)
        spread_values(cell_ref, value_ref, count_ref, spread, index)
    accumulate(total, hot, spread)

    @pl.when(step == pl.num_programs(0) - 1)
    def _():
        for member in range(2):
            out_ref[member] = summed_terms(total, member)


def scatter_call(kernel, rows, outs, cell, value, count, *more):
    width = CHUNK * SLOTS

    def whole(ref):
        return pl.BlockSpec(ref.shape, lambda k, rank=len(ref.shape): (0,) * rank)

    return pl.pallas_call(
        kernel,
        out_shape=outs,
        grid=(OWNERS // CHUNK,),
        in_specs=[
            pl.BlockSpec((CHUNK, 1, SLOTS), lambda k: (k, 0, 0)),
            pl.BlockSpec((CHUNK, 2, SLOTS), lambda k: (k, 0, 0)),
            SMEM,
        ]
        + [ANY] * len(more),
        out_specs=jax.tree.map(whole, outs),
        scratch_shapes=[
            pltpu.VMEM((rows, width), BF16),
            pltpu.VMEM((4 * LANES, width), BF16),
            pltpu.VMEM((rows, 4 * LANES), F32),
        ],
        compiler_params=SCATTER_PARAMS,
        cost_estimate=pl.CostEstimate(
            flops=2 * rows * 4 * LANES * OWNERS * SLOTS, bytes_accessed=1 << 20, transcendentals=0
        ),
    )(cell, value, count, *more)


def gather_rims(strips, neighbour_ref, turn_ref, store):
    devices = lax.axis_size(BOTH)
    start = (lax.axis_index(BOTH) - 1) * LANES
    for side in range(4):
        place = lax.rem(
            neighbour_ref[side : side + 1, :] - start + devices * LANES, devices * LANES
        )
        turns = turn_ref[side : side + 1, :]
        source = lax.bitwise_and(turns + (side + 2), 3)
        holder = lax.shift_right_logical(place, 7)
        lane = jnp.broadcast_to(lax.bitwise_and(place, LANES - 1), (ROWS, LANES))
        rows = [jnp.zeros((ROWS, LANES), F32) for _ in range(2)]
        for where, ref in enumerate(strips):
            for edge in range(4):
                hits = jnp.broadcast_to((holder == where) & (source == edge), (ROWS, LANES))
                for member in range(2):
                    picked = jnp.take_along_axis(
                        ref[member, edge], lane, axis=1, mode="promise_in_bounds"
                    )
                    rows[member] = jnp.where(hits, picked, rows[member])
        store(side, turns, rows)


def turned_vector(turns, rows):
    cosine = (turns == 0).astype(F32) - (turns == 2).astype(F32)
    sine = (turns == 1).astype(F32) - (turns == 3).astype(F32)
    return cosine * rows[0] - sine * rows[1], sine * rows[0] + cosine * rows[1]


def turned_stress(turns, rows):
    parity = (1 - 2 * lax.bitwise_and(turns, 1)).astype(F32)
    return rows[0], parity * rows[1]


def store_rim(pad, member, side, rim):
    if side == 0 or side == 2:
        pad[member, 0 if side == 0 else SIDE + 1, 8 : 8 + SIDE, :] = rim[0:SIDE]
    else:
        column = 7 if side == 1 else 8 + SIDE
        for i in range(SIDE):
            pad[member, i + 1, column : column + 1, :] = rim[i : i + 1]


def store_strips(out_ref, member, cell_of, layer=0):
    far = SIDE - 1 - layer
    out_ref[member, :, SIDE:ROWS, :] = jnp.zeros((4, ROWS - SIDE, LANES), F32)
    out_ref[member, 0, 0:SIDE, :] = cell_of(layer, slice(0, SIDE))
    out_ref[member, 2, 0:SIDE, :] = cell_of(far, slice(0, SIDE))
    for i in range(SIDE):
        out_ref[member, 1, i : i + 1, :] = cell_of(i, slice(layer, layer + 1))
        out_ref[member, 3, i : i + 1, :] = cell_of(i, slice(far, far + 1))


def cell_rows(i, member, cells=slice(0, SIDE)):
    start = 2 * (SIDE * i + cells.start) + member
    count = cells.stop - cells.start
    return slice(start, start + 1) if count == 1 else pl.ds(start, count, stride=2)


def run_copies(pairs, sems):
    copies = [
        pltpu.make_async_copy(source, target, sems.at[at])
        for at, (source, target) in enumerate(pairs)
    ]
    for copy in copies:
        copy.start()
    return copies


def outer_strips_kernel(velocity_hbm, cover_hbm, *rest):
    out_ref, lines, cover_rows, cover_low, cover_high, sems = rest
    last = SIDE - 1
    pairs = [
        (velocity_hbm.at[0], lines.at[0]),
        (velocity_hbm.at[:, 0], lines.at[1]),
        (velocity_hbm.at[last], lines.at[2]),
        (velocity_hbm.at[:, last], lines.at[3]),
        (cover_hbm.at[0], cover_rows.at[0]),
        (cover_hbm.at[last], cover_rows.at[1]),
        (cover_hbm.at[:, 0:8], cover_low),
        (cover_hbm.at[:, 24:SIDE], cover_high),
    ]
    for copy in run_copies(pairs, sems):
        copy.wait()
    out_ref[:, :, SIDE:ROWS, :] = jnp.zeros((2, 4, ROWS - SIDE, LANES), F32)
    for side in range(4):
        for t in range(SIDE):
            if side % 2 == 0:
                covered = cover_rows[side // 2, t : t + 1, :]
            else:
                covered = cover_low[t, 0:1, :] if side == 1 else cover_high[t, 5:6, :]
            covered = covered.astype(F32)
            for member in range(2):
                out_ref[member, side, t : t + 1, :] = (
                    lines[side, t, member : member + 1, :] * covered
                )


def weight_of(cover, mass):
    return cover.astype(F32) / (4.0 * mass + 1.0)


def inner_strips_kernel(
    velocity_ref, cover_ref, strength_ref, mass_ref, inner_ref, strength_strips_ref, weight_strips_ref
):
    for member in range(2):
        store_strips(
            inner_ref,
            member,
            lambda i, j: velocity_ref[cell_rows(i, member, j), :] * cover_ref[i, j, :].astype(F32),
            1,
        )
    store_strips(strength_strips_ref, 0, lambda i, j: strength_ref[i, j, :])
    for layer in range(2):
        at = slice(4 * layer, 4 * layer + 4)
        store_strips(
            weight_strips_ref.at[:, at],
            0,
            lambda i, j: weight_of(cover_ref[i, j, :], mass_ref[i, j, :]),
            layer,
        )


def derivatives(pad, member, i):
    middle = slice(8, 8 + SIDE)
    east = 0.5 * (pad[member, i + 2, middle, :] - pad[member, i, middle, :])
    north = 0.5 * (pad[member, i + 1, 9 : 9 + SIDE, :] - pad[member, i + 1, 7 : 7 + SIDE, :])
    return east, north


def targets_of(east_e, east_n, north_e, north_n, strength):
    divergence = east_e + north_n
    tension = east_e - north_n
    shearing = east_n + north_e
    inverse = lax.rsqrt(
        divergence * divergence + (tension * tension + shearing * shearing) * 0.25 + 0.25
    )
    scaled = strength * inverse
    return (
        divergence * scaled - strength,
        0.25 * (tension * scaled),
        0.125 * (shearing * scaled),
    )


def stress_targets(pad, strength, i):
    return targets_of(*derivatives(pad, 0, i), *derivatives(pad, 1, i), strength)


def forces(pad, i):
    middle = slice(8, 8 + SIDE)
    upper, lower = slice(9, 9 + SIDE), slice(7, 7 + SIDE)
    shear_east, shear_north = derivatives(pad, 1, i)
    force_east = 0.5 * (pad[0, i + 2, middle, :] - pad[0, i, middle, :]) + shear_north
    force_north = shear_east + 0.5 * (pad[2, i + 1, upper, :] - pad[2, i + 1, lower, :])
    return force_east, force_north


def stress_rims_kernel(
    before_ref, own_ref, after_ref, neighbour_ref, turn_ref, forcing_ref, out_ref
):
    def store(side, turns, rows):
        for member, rim in enumerate(turned_stress(turns, rows)):
            out_ref[member, side] = rim

    gather_rims((before_ref, own_ref, after_ref), neighbour_ref, turn_ref, store)


def fill_stress(pad, stress_ref):
    for i in range(SIDE):
        first_stress, second_stress = stress_ref[0, i], stress_ref[1, i]
        pad[0, i + 1, 8 : 8 + SIDE, :] = 0.5 * (first_stress + second_stress)
        pad[1, i + 1, 8 : 8 + SIDE, :] = stress_ref[2, i]
        pad[2, i + 1, 8 : 8 + SIDE, :] = 0.5 * (first_stress - second_stress)


def store_stress_rim(pad, side, normal, shear):
    store_rim(pad, 0 if side in (0, 2) else 2, side, normal)
    store_rim(pad, 1, side, shear)


def base_kernel(
    stress_rims_ref,
    rims_ref,
    velocity_ref,
    cover_ref,
    mass_ref,
    strength_ref,
    forcing_ref,
    weight_ref,
    base_ref,
    stress_ref,
    outer_ref,
    inner_ref,
    line,
    pad,
):
    for i in range(SIDE):
        covered = cover_ref[i].astype(F32)
        for member in range(2):
            line[member, i + 1, 8 : 8 + SIDE, :] = velocity_ref[cell_rows(i, member), :] * covered
    for member in range(2):
        for side in range(4):
            store_rim(line, member, side, rims_ref[member, side])
    for i in range(SIDE):
        targets = stress_targets(line, strength_ref[i], i)
        for member in range(3):
            stress_ref[member, i] = 0.5 * targets[member]
    fill_stress(pad, stress_ref)
    for side in range(4):
        store_stress_rim(pad, side, stress_rims_ref[0, side], stress_rims_ref[1, side])
    for i in range(SIDE):
        force_east, force_north = forces(pad, i)
        eastward = line[0, i + 1, 8 : 8 + SIDE, :]
        northward = line[1, i + 1, 8 : 8 + SIDE, :]
        mass = mass_ref[i]
        weight = weight_of(cover_ref[i], mass)
        base_ref[0, i] = weight * (mass * (4.0 * eastward + 0.5 * northward) + force_east)
        base_ref[1, i] = weight * (mass * (4.0 * northward - 0.5 * eastward) + force_north)
    for layer, out_ref in enumerate((outer_ref, inner_ref)):
        at = slice(4 * layer, 4 * layer + 4)
        for member in range(2):
            store_strips(out_ref, member, lambda i, j: base_ref[member, i, j, :], layer)
            out_ref[member] += weight_ref[0, at] * forcing_ref[member, at]


def edge_stress_kernel(
    before_ref,
    outer_ref,
    after_ref,
    inner_ref,
    neighbour_ref,
    turn_ref,
    strength_ref,
    *rest,
    opening,
):
    faces_ref, rims_ref, line = rest[-3:]

    def store(side, turns, rows):
        for member, rim in enumerate(turned_vector(turns, rows)):
            rims_ref[member, side] = rim

    gather_rims((before_ref, outer_ref, after_ref), neighbour_ref, turn_ref, store)
    faces_ref[:, :, SIDE:ROWS, :] = jnp.zeros((2, 4, ROWS - SIDE, LANES), F32)
    for side in range(4):
        end = 0 if side < 2 else SIDE - 1
        across, beside = [], []
        for member in range(2):
            line[member, side, 8 : 8 + SIDE, :] = outer_ref[member, side, 0:SIDE, :]
            lower, upper = (1, 3) if side % 2 == 0 else (0, 2)
            line[member, side, 7:8, :] = rims_ref[member, lower, end : end + 1, :]
            line[member, side, 8 + SIDE : 9 + SIDE, :] = rims_ref[member, upper, end : end + 1, :]
            step = 0.5 * (inner_ref[member, side, 0:SIDE, :] - rims_ref[member, side, 0:SIDE, :])
            across.append(step if side < 2 else -step)
            beside.append(
                0.5 * (line[member, side, 9 : 9 + SIDE, :] - line[member, side, 7 : 7 + SIDE, :])
            )
        east, north = (across, beside) if side % 2 == 0 else (beside, across)
        first, second, shear = targets_of(
            east[0], north[0], east[1], north[1], strength_ref[0, side, 0:SIDE, :]
        )
        normal = 0.5 * (first + second) if side % 2 == 0 else 0.5 * (first - second)
        for member, target in enumerate((normal, shear)):
            old = 0.0 if opening else rest[0][member, side, 0:SIDE, :]
            faces_ref[member, side, 0:SIDE, :] = old + 0.5 * (target - old)


def second_stress_kernel(
    base_ref,
    cover_ref,
    mass_ref,
    low_ref,
    high_ref,
    outer_ref,
    inner_ref,
    rims_ref,
    strength_ref,
    old_ref,
    moving_ref,
    stress_ref,
    stress_hbm,
    pad,
    sems,
):
    for member in range(2):
        for side in range(4):
            store_rim(pad, member, side, rims_ref[member, side])
        for i, ref, side in (
            (0, outer_ref, 0),
            (1, inner_ref, 0),
            (SIDE - 2, inner_ref, 2),
            (SIDE - 1, outer_ref, 2),
        ):
            pad[member, i + 1, 8 : 8 + SIDE, :] = ref[member, side, 0:SIDE, :]
        for i in range(2, SIDE - 2):
            for j, ref, side in (
                (0, outer_ref, 1),
                (1, inner_ref, 1),
                (SIDE - 2, inner_ref, 3),
                (SIDE - 1, outer_ref, 3),
            ):
                pad[member, i + 1, 8 + j : 9 + j, :] = ref[member, side, i : i + 1, :]
    inside = slice(2, SIDE - 2)
    for i in range(2, SIDE - 2):
        weight = weight_of(cover_ref[i, inside, :], mass_ref[i, inside, :])
        ref, at = (low_ref, i - 2) if i < 2 + HALF else (high_ref, i - 2 - HALF)
        for member in range(2):
            pad[member, i + 1, 10 : 10 + INSIDE, :] = base_ref[member, i, inside, :] + weight * (
                ref[member, at * INSIDE : at * INSIDE + INSIDE, :]
            )
    copies = []
    for i in range(SIDE):
        targets = stress_targets(pad, strength_ref[i], i)
        for member in range(3):
            old = old_ref[member, i]
            stress_ref[member, i] = old + 0.5 * (targets[member] - old)
        for member in range(2):
            moving_ref[member, i] = pad[member, i + 1, 8 : 8 + SIDE, :]
        if i % 10 == 9:
            part = pl.ds(i - 9, 10)
            copies.append(
                pltpu.make_async_copy(
                    stress_ref.at[:, part], stress_hbm.at[:, part], sems.at[i // 10]
                )
            )
            copies[-1].start()
    for copy in copies:
        copy.wait()


def last_kernel(
    before_ref,
    own_ref,
    after_ref,
    neighbour_ref,
    turn_ref,
    moving_ref,
    base_ref,
    cover_ref,
    mass_ref,
    stress_ref,
    out_hbm,
    pad,
    out_ref,
    sems,
):
    copies = []
    fill_stress(pad, stress_ref)

    def store(side, turns, rows):
        store_stress_rim(pad, side, *turned_stress(turns, rows))

    gather_rims((before_ref, own_ref, after_ref), neighbour_ref, turn_ref, store)
    for i in range(SIDE):
        force_east, force_north = forces(pad, i)
        eastward, northward = moving_ref[0, i], moving_ref[1, i]
        mass = mass_ref[i]
        weight = weight_of(cover_ref[i], mass)
        out_ref[cell_rows(i, 0), :] = weight * (
            mass * (4.0 * eastward + 0.5 * northward) + force_east
        ) + (eastward - base_ref[0, i])
        out_ref[cell_rows(i, 1), :] = weight * (
            mass * (4.0 * northward - 0.5 * eastward) + force_north
        ) + (northward - base_ref[1, i])
        if i % 6 == 5:
            part = pl.ds(60 * (i - 5), 360)
            copies.append(
                pltpu.make_async_copy(out_ref.at[part], out_hbm.at[part], sems.at[i // 6])
            )
            copies[-1].start()
    for copy in copies:
        copy.wait()


def call(kernel, outs, *args, specs=None, out_specs=None, scratch=(), work=1 << 22, params=PARAMS):
    return pl.pallas_call(
        kernel,
        out_shape=outs,
        in_specs=specs or [VMEM] * len(args),
        out_specs=out_specs or jax.tree.map(lambda _: VMEM, outs),
        scratch_shapes=list(scratch),
        compiler_params=params,
        cost_estimate=pl.CostEstimate(flops=work, bytes_accessed=1 << 22, transcendentals=0),
    )(*args)


def shards(
    velocity,
    strength,
    mass,
    ice_cover,
    neighbour,
    rotation,
    concentration,
    air_wind,
    ocean_current,
    drag,
    slot_cell,
    slot_count,
):
    devices = lax.axis_size(BOTH)
    ring = [(i, (i + 1) % devices) for i in range(devices)]
    back = [(j, i) for i, j in ring]

    def both_ways(strips):
        return lax.ppermute(strips, BOTH, ring), lax.ppermute(strips, BOTH, back)

    strip_shape = shape(2, 4, ROWS, LANES)
    block = (SIDE, SIDE, LANES)
    pad2 = [pltpu.VMEM((2, ROWS, 48, LANES), F32)]
    pad3 = [pltpu.VMEM((3, ROWS, 48, LANES), F32)]
    count = slot_count.reshape(1, OWNERS)

    sems = pltpu.SemaphoreType.DMA
    packed = call(
        pack_kernel,
        [shape(OWNERS + EXTRA, SLOTS)] * 4,
        concentration,
        drag.reshape(1, 2),
        specs=[VMEM, SMEM],
        scratch=[pltpu.VMEM((2, 4 * OWNERS, LANES), F32)],
    )
    parts = [packed[0]] + [
        lax.ppermute(packed[step], "cat", [(i, (i + step) % 4) for i in range(4)])
        for step in (1, 2, 3)
    ]

    by_cell = jnp.transpose(velocity, (1, 2, 0, 3))
    velocity = by_cell.reshape(2 * SIDE * SIDE, LANES)
    outer = call(
        outer_strips_kernel,
        strip_shape,
        by_cell,
        ice_cover,
        specs=[ANY] * 2,
        scratch=[
            pltpu.VMEM((4, SIDE, 2, LANES), F32),
            pltpu.VMEM((2, SIDE, LANES), I32),
            pltpu.VMEM((SIDE, 8, LANES), I32),
            pltpu.VMEM((SIDE, 6, LANES), I32),
            sems((8,)),
        ],
        params=ALONE_PARAMS,
    )
    before, after = both_ways(outer)
    inner, strength_strips, weight_strips = call(
        inner_strips_kernel,
        (strip_shape, shape(1, 4, ROWS, LANES), shape(1, 8, ROWS, LANES)),
        velocity, ice_cover, strength, mass,
    )

    line = [pltpu.VMEM((2, 4, 48, LANES), F32)]
    faces, rims = call(
        functools.partial(edge_stress_kernel, opening=True),
        (strip_shape, strip_shape),
        before, outer, after, inner, neighbour, rotation, strength_strips,
        scratch=line,
        work=1 << 34,
    )
    before, after = both_ways(faces)

    summed = call(
        partial_kernel,
        shape(OWNERS, 2, SLOTS),
        *parts, air_wind, ocean_current,
        scratch=[pltpu.VMEM((2, 2, 2, 4 * OWNERS, LANES), F32)],
        work=1 << 31,
    )
    arrived = lax.all_to_all(summed, "blocks", split_axis=0, concat_axis=0, tiled=True)

    forcing = scatter_call(
        edge_kernel, 8 * ROWS, shape(2, 8, ROWS, LANES), slot_cell, arrived, count, faces
    )
    stress_rims = call(
        stress_rims_kernel,
        strip_shape,
        before, faces, after, neighbour, rotation, forcing,
        specs=[VMEM] * 5 + [ANY],
    )
    base, stress, outer, inner = call(
        base_kernel,
        (shape(2, *block), shape(3, *block), strip_shape, strip_shape),
        stress_rims, rims, velocity, ice_cover, mass, strength, forcing, weight_strips,
        scratch=pad2 + pad3,
    )
    before, after = both_ways(outer)
    low = scatter_call(
        functools.partial(inside_kernel, 2), HALF_ROWS, shape(2, HALF_ROWS, LANES),
        slot_cell, arrived, count,
    )
    faces, rims = call(
        functools.partial(edge_stress_kernel, opening=False),
        (strip_shape, strip_shape),
        before, outer, after, inner, neighbour, rotation, strength_strips, faces,
        scratch=line,
    )
    before, after = both_ways(faces)
    high = scatter_call(
        functools.partial(inside_kernel, 2 + HALF), HALF_ROWS, shape(2, HALF_ROWS, LANES),
        slot_cell, arrived, count,
    )
    moving, kept, stress = call(
        second_stress_kernel,
        (shape(2, *block), shape(3, *block), shape(3, *block)),
        base, ice_cover, mass, low, high, outer, inner, rims, strength, stress,
        out_specs=(VMEM, VMEM, ANY),
        scratch=pad2 + [sems((3,))],
    )
    moving = call(
        last_kernel,
        shape(2 * SIDE * SIDE, LANES),
        before, faces, after, neighbour, rotation, moving, base, ice_cover, mass, kept,
        out_specs=ANY,
        scratch=pad3 + [pltpu.VMEM((2 * SIDE * SIDE, LANES), F32), sems((5,))],
    )
    moving = jnp.transpose(moving.reshape(SIDE, SIDE, 2, LANES), (2, 0, 1, 3))
    return (moving, stress)


def solution(mesh):
    placed = (
        P(None, None, None, BOTH),
        P(None, None, BOTH),
        P(None, None, BOTH),
        P(None, None, BOTH),
        P(None, BOTH),
        P(None, BOTH),
        P("cat", "blocks", None, None),
        P(None, "blocks", None, None),
        P(None, "blocks", None, None),
        P(None, "cat"),
        P(None, BOTH, None),
        P(None, BOTH),
    )
    return jax.shard_map(
        shards,
        mesh=mesh,
        in_specs=placed,
        out_specs=(P(None, None, None, BOTH), P(None, None, None, BOTH)),
        check_vma=False,
    )
```

```python
import functools

import jax
import jax.numpy as jnp
from jax import lax
from jax.experimental import pallas as pl
from jax.experimental.pallas import tpu as pltpu
from jax.sharding import PartitionSpec as P

F32 = jnp.float32
BF16 = jnp.bfloat16
I32 = jnp.int32

SIDE = 30
ROWS = 32
LANES = 128
OWNERS = 64
SLOTS = 256
EXTRA = 8
CHUNK = 16
INSIDE = SIDE - 4
HALF = INSIDE // 2
HALF_ROWS = 352
BOTH = ("blocks", "cat")

PARAMS = pltpu.CompilerParams(vmem_limit_bytes=6 * 1024 * 1024)
SCATTER_PARAMS = pltpu.CompilerParams(vmem_limit_bytes=12 * 1024 * 1024)
ALONE_PARAMS = pltpu.CompilerParams(vmem_limit_bytes=60 * 1024 * 1024)
ANY = pl.BlockSpec(memory_space=pl.ANY)
VMEM = pl.BlockSpec(memory_space=pltpu.VMEM)
SMEM = pl.BlockSpec(memory_space=pltpu.SMEM)


def shape(*dims, dtype=F32):
    return jax.ShapeDtypeStruct(dims, dtype)


def fill_halves(halves, value_of):
    for half in range(2):
        halves[half] = value_of(slice(half * LANES, half * LANES + LANES))


def quarter(halves, half, receiver):
    return halves[half, pl.ds(receiver, OWNERS, stride=4), :]


def partial_kernel(mine_ref, first_ref, second_ref, third_ref, air_ref, ocean_ref, out_ref, wind):
    cat = lax.axis_index("cat")
    parts = (mine_ref, first_ref, second_ref, third_ref)
    for which, ref in enumerate((air_ref, ocean_ref)):
        for member in range(2):
            fill_halves(wind.at[which, member], lambda lanes: ref[member, 0, :, lanes])
    for half in range(2):
        lanes = slice(half * LANES, half * LANES + LANES)
        totals = [0.0, 0.0]
        for which in range(2):
            weight = jnp.zeros((OWNERS, LANES), F32)
            at = OWNERS + which
            for part in parts:
                weight += part[0:OWNERS, lanes] * part[at : at + 1, lanes]
            east = quarter(wind.at[which, 0], half, cat)
            north = quarter(wind.at[which, 1], half, cat)
            weight *= jnp.sqrt(east * east + north * north)
            totals[0] += weight * east
            totals[1] += weight * north
        out_ref[:, 0, lanes] = totals[0]
        out_ref[:, 1, lanes] = totals[1]


def split_lanes(lane_hits, value):
    high = value.astype(BF16).astype(F32)
    return (
        jnp.where(lane_hits, high, 0.0).astype(BF16),
        jnp.where(lane_hits, value - high, 0.0).astype(BF16),
    )


def spread_values(cell_ref, value_ref, count_ref, spread, index):
    block = lax.broadcasted_iota(I32, (LANES, SLOTS), 0)
    slot = lax.broadcasted_iota(I32, (1, SLOTS), 1)
    columns = pl.ds(index * SLOTS, SLOTS)
    lane_hits = block == lax.bitwise_and(cell_ref[index], LANES - 1)
    live = slot < count_ref[0, pl.program_id(0) * CHUNK + index]
    for member in range(2):
        value = jnp.where(live, value_ref[index, member : member + 1, :], 0.0)
        high, low = split_lanes(lane_hits, value)
        spread[pl.ds(member * 2 * LANES, LANES), columns] = high
        spread[pl.ds(member * 2 * LANES + LANES, LANES), columns] = low


def cell_number(cell):
    return lax.shift_right_logical(cell, 7)


def accumulate(total, hot, spread):
    total[...] += lax.dot_general(
        hot[...], spread[...], (((1,), (1,)), ((), ())), preferred_element_type=F32
    )


def summed_terms(total, member):
    at = member * 2 * LANES
    return total[:, at : at + LANES] + total[:, at + LANES : at + 2 * LANES]


def edge_kernel(cell_ref, value_ref, count_ref, after_ref, out_ref, hot, spread, total):
    step = pl.program_id(0)

    @pl.when(step == 0)
    def _():
        total[...] = jnp.zeros_like(total)

    along = lax.broadcasted_iota(I32, (ROWS, SLOTS), 0)
    for index in range(CHUNK):
        number = cell_number(cell_ref[index])
        east = lax.shift_right_logical(number * 2185, 16)
        north = number - east * SIDE
        columns = pl.ds(index * SLOTS, SLOTS)
        east_hot = (along == east).astype(F32).astype(BF16)
        north_hot = (along == north).astype(F32).astype(BF16)
        empty = jnp.zeros_like(east_hot)
        for layer in range(2):
            for side, here in enumerate(
                (east == layer, north == layer, east == SIDE - 1 - layer, north == SIDE - 1 - layer)
            ):
                hot[pl.ds((layer * 4 + side) * ROWS, ROWS), columns] = jnp.where(
                    here, east_hot if side % 2 else north_hot, empty
                )
        spread_values(cell_ref, value_ref, count_ref, spread, index)
    accumulate(total, hot, spread)

    @pl.when(step == pl.num_programs(0) - 1)
    def _():
        for member in range(2):
            out_ref[member] = summed_terms(total, member).reshape(8, ROWS, LANES)


def inside_kernel(first, cell_ref, value_ref, count_ref, out_ref, hot, spread, total):
    step = pl.program_id(0)

    @pl.when(step == 0)
    def _():
        total[...] = jnp.zeros_like(total)

    row = lax.broadcasted_iota(I32, (HALF_ROWS, SLOTS), 0)
    east = lax.shift_right_logical(row * 2521, 16)
    wanted = jnp.where(
        east < HALF, (east + first) * SIDE + 2 + (row - east * INSIDE), -1
    )
    for index in range(CHUNK):
        columns = pl.ds(index * SLOTS, SLOTS)
        hits = wanted == cell_number(cell_ref[index])
        hot[:, columns] = hits.astype(F32).astype(BF16)
        spread_values(cell_ref, value_ref, count_ref, spread, index)
    accumulate(total, hot, spread)

    @pl.when(step == pl.num_programs(0) - 1)
    def _():
        for member in range(2):
            out_ref[member] = summed_terms(total, member)


def scatter_call(kernel, rows, outs, cell, value, count, *more):
    width = CHUNK * SLOTS

    def whole(ref):
        return pl.BlockSpec(ref.shape, lambda k, rank=len(ref.shape): (0,) * rank)

    return pl.pallas_call(
        kernel,
        out_shape=outs,
        grid=(OWNERS // CHUNK,),
        in_specs=[
            pl.BlockSpec((CHUNK, 1, SLOTS), lambda k: (k, 0, 0)),
            pl.BlockSpec((CHUNK, 2, SLOTS), lambda k: (k, 0, 0)),
            SMEM,
        ]
        + [ANY] * len(more),
        out_specs=jax.tree.map(whole, outs),
        scratch_shapes=[
            pltpu.VMEM((rows, width), BF16),
            pltpu.VMEM((4 * LANES, width), BF16),
            pltpu.VMEM((rows, 4 * LANES), F32),
        ],
        compiler_params=SCATTER_PARAMS,
        cost_estimate=pl.CostEstimate(
            flops=2 * rows * 4 * LANES * OWNERS * SLOTS, bytes_accessed=1 << 20, transcendentals=0
        ),
    )(cell, value, count, *more)


def gather_rims(strips, neighbour_ref, turn_ref, store):
    devices = lax.axis_size(BOTH)
    here = lax.axis_index(BOTH)
    start = (here - 1) * LANES
    odd = lax.bitwise_and(here, 1)
    holders = (2 * odd, 1, 2 - 2 * odd)
    for side in range(4):
        place = lax.rem(
            neighbour_ref[side : side + 1, :] - start + devices * LANES, devices * LANES
        )
        turns = turn_ref[side : side + 1, :]
        source = lax.bitwise_and(turns + (side + 2), 3)
        holder = lax.shift_right_logical(place, 7)
        lane = jnp.broadcast_to(lax.bitwise_and(place, LANES - 1), (ROWS, LANES))
        rows = [jnp.zeros((ROWS, LANES), F32) for _ in range(2)]
        for where, ref in zip(holders, strips):
            for edge in range(4):
                hits = jnp.broadcast_to((holder == where) & (source == edge), (ROWS, LANES))
                for member in range(2):
                    picked = jnp.take_along_axis(
                        ref[member, edge], lane, axis=1, mode="promise_in_bounds"
                    )
                    rows[member] = jnp.where(hits, picked, rows[member])
        store(side, turns, rows)


def turned_vector(turns, rows):
    cosine = (turns == 0).astype(F32) - (turns == 2).astype(F32)
    sine = (turns == 1).astype(F32) - (turns == 3).astype(F32)
    return cosine * rows[0] - sine * rows[1], sine * rows[0] + cosine * rows[1]


def turned_stress(turns, rows):
    parity = (1 - 2 * lax.bitwise_and(turns, 1)).astype(F32)
    return rows[0], parity * rows[1]


def store_rim(pad, member, side, rim):
    if side == 0 or side == 2:
        pad[member, 0 if side == 0 else SIDE + 1, 8 : 8 + SIDE, :] = rim[0:SIDE]
    else:
        column = 7 if side == 1 else 8 + SIDE
        for i in range(SIDE):
            pad[member, i + 1, column : column + 1, :] = rim[i : i + 1]


def store_strips(out_ref, member, cell_of, layer=0):
    far = SIDE - 1 - layer
    out_ref[member, :, SIDE:ROWS, :] = jnp.zeros((4, ROWS - SIDE, LANES), F32)
    out_ref[member, 0, 0:SIDE, :] = cell_of(layer, slice(0, SIDE))
    out_ref[member, 2, 0:SIDE, :] = cell_of(far, slice(0, SIDE))
    for i in range(SIDE):
        out_ref[member, 1, i : i + 1, :] = cell_of(i, slice(layer, layer + 1))
        out_ref[member, 3, i : i + 1, :] = cell_of(i, slice(far, far + 1))


def cell_rows(i, member, cells=slice(0, SIDE)):
    start = 2 * (SIDE * i + cells.start) + member
    count = cells.stop - cells.start
    return slice(start, start + 1) if count == 1 else pl.ds(start, count, stride=2)


def run_copies(pairs, sems):
    copies = [
        pltpu.make_async_copy(source, target, sems.at[at])
        for at, (source, target) in enumerate(pairs)
    ]
    for copy in copies:
        copy.start()
    return copies


def opening_kernel(conc_hbm, drag_ref, velocity_hbm, cover_hbm, *rest):
    outs, out_ref = rest[:4], rest[4]
    halves, lines, cover_rows, cover_low, cover_high, sems = rest[5:]
    last = SIDE - 1
    copies = run_copies(
        [
            (conc_hbm.at[0, 0, :, 0:LANES], halves.at[0]),
            (conc_hbm.at[0, 0, :, LANES : 2 * LANES], halves.at[1]),
            (velocity_hbm.at[0], lines.at[0]),
            (velocity_hbm.at[:, 0], lines.at[1]),
            (velocity_hbm.at[last], lines.at[2]),
            (velocity_hbm.at[:, last], lines.at[3]),
            (cover_hbm.at[0], cover_rows.at[0]),
            (cover_hbm.at[last], cover_rows.at[1]),
            (cover_hbm.at[:, 0:8], cover_low),
            (cover_hbm.at[:, 24:SIDE], cover_high),
        ],
        sems,
    )
    cat = lax.axis_index("cat")
    row = lax.broadcasted_iota(I32, (EXTRA, SLOTS), 0)
    coefficients = jnp.where(row == 0, drag_ref[0, 0], drag_ref[0, 1])
    for half in range(2):
        copies[half].wait()
    for step, packed_ref in enumerate(outs):
        receiver = lax.bitwise_xor(cat, step)
        for half in range(2):
            lanes = slice(half * LANES, half * LANES + LANES)
            packed_ref[0:OWNERS, lanes] = quarter(halves, half, receiver)
        packed_ref[OWNERS : OWNERS + EXTRA, :] = coefficients
    for copy in copies[2:]:
        copy.wait()
    out_ref[:, :, SIDE:ROWS, :] = jnp.zeros((2, 4, ROWS - SIDE, LANES), F32)
    for side in range(4):
        for t in range(SIDE):
            if side % 2 == 0:
                covered = cover_rows[side // 2, t : t + 1, :]
            else:
                covered = cover_low[t, 0:1, :] if side == 1 else cover_high[t, 5:6, :]
            covered = covered.astype(F32)
            for member in range(2):
                out_ref[member, side, t : t + 1, :] = (
                    lines[side, t, member : member + 1, :] * covered
                )


def weight_of(cover, mass):
    return cover.astype(F32) / (4.0 * mass + 1.0)


def inner_strips_kernel(
    velocity_ref,
    cover_ref,
    strength_ref,
    mass_ref,
    summed_ref,
    inner_ref,
    strength_strips_ref,
    weight_strips_ref,
):
    for member in range(2):
        store_strips(
            inner_ref,
            member,
            lambda i, j: velocity_ref[cell_rows(i, member, j), :] * cover_ref[i, j, :].astype(F32),
            1,
        )
    store_strips(strength_strips_ref, 0, lambda i, j: strength_ref[i, j, :])
    for layer in range(2):
        at = slice(4 * layer, 4 * layer + 4)
        store_strips(
            weight_strips_ref.at[:, at],
            0,
            lambda i, j: weight_of(cover_ref[i, j, :], mass_ref[i, j, :]),
            layer,
        )


def derivatives(pad, member, i):
    middle = slice(8, 8 + SIDE)
    east = 0.5 * (pad[member, i + 2, middle, :] - pad[member, i, middle, :])
    north = 0.5 * (pad[member, i + 1, 9 : 9 + SIDE, :] - pad[member, i + 1, 7 : 7 + SIDE, :])
    return east, north


def targets_of(east_e, east_n, north_e, north_n, strength):
    divergence = east_e + north_n
    tension = east_e - north_n
    shearing = east_n + north_e
    inverse = lax.rsqrt(
        divergence * divergence + (tension * tension + shearing * shearing) * 0.25 + 0.25
    )
    scaled = strength * inverse
    return (
        divergence * scaled - strength,
        0.25 * (tension * scaled),
        0.125 * (shearing * scaled),
    )


def stress_targets(pad, strength, i):
    return targets_of(*derivatives(pad, 0, i), *derivatives(pad, 1, i), strength)


def forces(pad, i):
    middle = slice(8, 8 + SIDE)
    upper, lower = slice(9, 9 + SIDE), slice(7, 7 + SIDE)
    shear_east, shear_north = derivatives(pad, 1, i)
    force_east = 0.5 * (pad[0, i + 2, middle, :] - pad[0, i, middle, :]) + shear_north
    force_north = shear_east + 0.5 * (pad[2, i + 1, upper, :] - pad[2, i + 1, lower, :])
    return force_east, force_north


def stress_rims_kernel(
    one_ref, own_ref, two_ref, neighbour_ref, turn_ref, forcing_ref, out_ref
):
    def store(side, turns, rows):
        for member, rim in enumerate(turned_stress(turns, rows)):
            out_ref[member, side] = rim

    gather_rims((one_ref, own_ref, two_ref), neighbour_ref, turn_ref, store)


def fill_stress(pad, stress_ref):
    for i in range(SIDE):
        first_stress, second_stress = stress_ref[0, i], stress_ref[1, i]
        pad[0, i + 1, 8 : 8 + SIDE, :] = 0.5 * (first_stress + second_stress)
        pad[1, i + 1, 8 : 8 + SIDE, :] = stress_ref[2, i]
        pad[2, i + 1, 8 : 8 + SIDE, :] = 0.5 * (first_stress - second_stress)


def store_stress_rim(pad, side, normal, shear):
    store_rim(pad, 0 if side in (0, 2) else 2, side, normal)
    store_rim(pad, 1, side, shear)


def base_kernel(
    stress_rims_ref,
    rims_ref,
    velocity_ref,
    cover_ref,
    mass_ref,
    strength_ref,
    forcing_ref,
    weight_ref,
    base_ref,
    stress_ref,
    outer_ref,
    inner_ref,
    line,
    pad,
):
    for i in range(SIDE):
        covered = cover_ref[i].astype(F32)
        for member in range(2):
            line[member, i + 1, 8 : 8 + SIDE, :] = velocity_ref[cell_rows(i, member), :] * covered
    for member in range(2):
        for side in range(4):
            store_rim(line, member, side, rims_ref[member, side])
    for i in range(SIDE):
        targets = stress_targets(line, strength_ref[i], i)
        for member in range(3):
            stress_ref[member, i] = 0.5 * targets[member]
    fill_stress(pad, stress_ref)
    for side in range(4):
        store_stress_rim(pad, side, stress_rims_ref[0, side], stress_rims_ref[1, side])
    for i in range(SIDE):
        force_east, force_north = forces(pad, i)
        eastward = line[0, i + 1, 8 : 8 + SIDE, :]
        northward = line[1, i + 1, 8 : 8 + SIDE, :]
        mass = mass_ref[i]
        weight = weight_of(cover_ref[i], mass)
        base_ref[0, i] = weight * (mass * (4.0 * eastward + 0.5 * northward) + force_east)
        base_ref[1, i] = weight * (mass * (4.0 * northward - 0.5 * eastward) + force_north)
    for layer, out_ref in enumerate((outer_ref, inner_ref)):
        at = slice(4 * layer, 4 * layer + 4)
        for member in range(2):
            store_strips(out_ref, member, lambda i, j: base_ref[member, i, j, :], layer)
            out_ref[member] += weight_ref[0, at] * forcing_ref[member, at]


def edge_stress_kernel(
    one_ref,
    outer_ref,
    two_ref,
    inner_ref,
    neighbour_ref,
    turn_ref,
    strength_ref,
    *rest,
    opening,
):
    faces_ref, rims_ref, line = rest[-3:]

    def store(side, turns, rows):
        for member, rim in enumerate(turned_vector(turns, rows)):
            rims_ref[member, side] = rim

    gather_rims((one_ref, outer_ref, two_ref), neighbour_ref, turn_ref, store)
    faces_ref[:, :, SIDE:ROWS, :] = jnp.zeros((2, 4, ROWS - SIDE, LANES), F32)
    for side in range(4):
        end = 0 if side < 2 else SIDE - 1
        across, beside = [], []
        for member in range(2):
            line[member, side, 8 : 8 + SIDE, :] = outer_ref[member, side, 0:SIDE, :]
            lower, upper = (1, 3) if side % 2 == 0 else (0, 2)
            line[member, side, 7:8, :] = rims_ref[member, lower, end : end + 1, :]
            line[member, side, 8 + SIDE : 9 + SIDE, :] = rims_ref[member, upper, end : end + 1, :]
            step = 0.5 * (inner_ref[member, side, 0:SIDE, :] - rims_ref[member, side, 0:SIDE, :])
            across.append(step if side < 2 else -step)
            beside.append(
                0.5 * (line[member, side, 9 : 9 + SIDE, :] - line[member, side, 7 : 7 + SIDE, :])
            )
        east, north = (across, beside) if side % 2 == 0 else (beside, across)
        first, second, shear = targets_of(
            east[0], north[0], east[1], north[1], strength_ref[0, side, 0:SIDE, :]
        )
        normal = 0.5 * (first + second) if side % 2 == 0 else 0.5 * (first - second)
        for member, target in enumerate((normal, shear)):
            old = 0.0 if opening else rest[0][member, side, 0:SIDE, :]
            faces_ref[member, side, 0:SIDE, :] = old + 0.5 * (target - old)


def second_stress_kernel(
    base_ref,
    cover_ref,
    mass_ref,
    low_ref,
    high_ref,
    outer_ref,
    inner_ref,
    rims_ref,
    strength_ref,
    old_ref,
    moving_ref,
    stress_ref,
    stress_hbm,
    pad,
    sems,
):
    for member in range(2):
        for side in range(4):
            store_rim(pad, member, side, rims_ref[member, side])
        for i, ref, side in (
            (0, outer_ref, 0),
            (1, inner_ref, 0),
            (SIDE - 2, inner_ref, 2),
            (SIDE - 1, outer_ref, 2),
        ):
            pad[member, i + 1, 8 : 8 + SIDE, :] = ref[member, side, 0:SIDE, :]
        for i in range(2, SIDE - 2):
            for j, ref, side in (
                (0, outer_ref, 1),
                (1, inner_ref, 1),
                (SIDE - 2, inner_ref, 3),
                (SIDE - 1, outer_ref, 3),
            ):
                pad[member, i + 1, 8 + j : 9 + j, :] = ref[member, side, i : i + 1, :]
    inside = slice(2, SIDE - 2)
    for i in range(2, SIDE - 2):
        weight = weight_of(cover_ref[i, inside, :], mass_ref[i, inside, :])
        ref, at = (low_ref, i - 2) if i < 2 + HALF else (high_ref, i - 2 - HALF)
        for member in range(2):
            pad[member, i + 1, 10 : 10 + INSIDE, :] = base_ref[member, i, inside, :] + weight * (
                ref[member, at * INSIDE : at * INSIDE + INSIDE, :]
            )
    copies = []
    for i in range(SIDE):
        targets = stress_targets(pad, strength_ref[i], i)
        for member in range(3):
            old = old_ref[member, i]
            stress_ref[member, i] = old + 0.5 * (targets[member] - old)
        for member in range(2):
            moving_ref[member, i] = pad[member, i + 1, 8 : 8 + SIDE, :]
        if i % 10 == 9:
            part = pl.ds(i - 9, 10)
            copies.append(
                pltpu.make_async_copy(
                    stress_ref.at[:, part], stress_hbm.at[:, part], sems.at[i // 10]
                )
            )
            copies[-1].start()
    for copy in copies:
        copy.wait()


def last_kernel(
    one_ref,
    own_ref,
    two_ref,
    neighbour_ref,
    turn_ref,
    moving_ref,
    base_ref,
    cover_ref,
    mass_ref,
    stress_ref,
    out_hbm,
    pad,
    out_ref,
    sems,
):
    copies = []
    fill_stress(pad, stress_ref)

    def store(side, turns, rows):
        store_stress_rim(pad, side, *turned_stress(turns, rows))

    gather_rims((one_ref, own_ref, two_ref), neighbour_ref, turn_ref, store)
    for i in range(SIDE):
        force_east, force_north = forces(pad, i)
        eastward, northward = moving_ref[0, i], moving_ref[1, i]
        mass = mass_ref[i]
        weight = weight_of(cover_ref[i], mass)
        out_ref[cell_rows(i, 0), :] = weight * (
            mass * (4.0 * eastward + 0.5 * northward) + force_east
        ) + (eastward - base_ref[0, i])
        out_ref[cell_rows(i, 1), :] = weight * (
            mass * (4.0 * northward - 0.5 * eastward) + force_north
        ) + (northward - base_ref[1, i])
        if i % 6 == 5:
            part = pl.ds(60 * (i - 5), 360)
            copies.append(
                pltpu.make_async_copy(out_ref.at[part], out_hbm.at[part], sems.at[i // 6])
            )
            copies[-1].start()
    for copy in copies:
        copy.wait()


def call(kernel, outs, *args, specs=None, out_specs=None, scratch=(), work=1 << 22, params=PARAMS):
    return pl.pallas_call(
        kernel,
        out_shape=outs,
        in_specs=specs or [VMEM] * len(args),
        out_specs=out_specs or jax.tree.map(lambda _: VMEM, outs),
        scratch_shapes=list(scratch),
        compiler_params=params,
        cost_estimate=pl.CostEstimate(flops=work, bytes_accessed=1 << 22, transcendentals=0),
    )(*args)


def shards(
    velocity,
    strength,
    mass,
    ice_cover,
    neighbour,
    rotation,
    concentration,
    air_wind,
    ocean_current,
    drag,
    slot_cell,
    slot_count,
):
    devices = lax.axis_size(BOTH)
    pairs = [[(i, i + 1) for i in range(start, devices, 2)] for start in (1, 0)]
    swaps = [[(i, j % devices) for i, j in p] + [(j % devices, i) for i, j in p] for p in pairs]

    def both_ways(strips):
        return [lax.ppermute(strips, BOTH, swap) for swap in swaps]

    strip_shape = shape(2, 4, ROWS, LANES)
    block = (SIDE, SIDE, LANES)
    pad2 = [pltpu.VMEM((2, ROWS, 48, LANES), F32)]
    pad3 = [pltpu.VMEM((3, ROWS, 48, LANES), F32)]
    count = slot_count.reshape(1, OWNERS)

    sems = pltpu.SemaphoreType.DMA
    by_cell = jnp.transpose(velocity, (1, 2, 0, 3))
    velocity = by_cell.reshape(2 * SIDE * SIDE, LANES)
    *packed, outer = call(
        opening_kernel,
        [shape(OWNERS + EXTRA, SLOTS)] * 4 + [strip_shape],
        concentration,
        drag.reshape(1, 2),
        by_cell,
        ice_cover,
        specs=[ANY, SMEM, ANY, ANY],
        scratch=[
            pltpu.VMEM((2, 4 * OWNERS, LANES), F32),
            pltpu.VMEM((4, SIDE, 2, LANES), F32),
            pltpu.VMEM((2, SIDE, LANES), I32),
            pltpu.VMEM((SIDE, 8, LANES), I32),
            pltpu.VMEM((SIDE, 6, LANES), I32),
            sems((10,)),
        ],
        params=ALONE_PARAMS,
    )
    parts = [packed[0]] + [
        lax.ppermute(packed[step], "cat", [(i, i ^ step) for i in range(4)])
        for step in (1, 2, 3)
    ]

    line = [pltpu.VMEM((2, 4, 48, LANES), F32)]
    summed = call(
        partial_kernel,
        shape(OWNERS, 2, SLOTS),
        *parts, air_wind, ocean_current,
        scratch=[pltpu.VMEM((2, 2, 2, 4 * OWNERS, LANES), F32)],
        work=1 << 31,
    )
    arrived = lax.all_to_all(summed, "blocks", split_axis=0, concat_axis=0, tiled=True)

    first, second = both_ways(outer)
    inner, strength_strips, weight_strips = call(
        inner_strips_kernel,
        (strip_shape, shape(1, 4, ROWS, LANES), shape(1, 8, ROWS, LANES)),
        velocity, ice_cover, strength, mass, summed,
        specs=[VMEM] * 4 + [ANY],
    )
    faces, rims = call(
        functools.partial(edge_stress_kernel, opening=True),
        (strip_shape, strip_shape),
        first, outer, second, inner, neighbour, rotation, strength_strips,
        scratch=line,
        work=1 << 34,
    )
    first, second = both_ways(faces)

    forcing = scatter_call(
        edge_kernel, 8 * ROWS, shape(2, 8, ROWS, LANES), slot_cell, arrived, count, faces
    )
    stress_rims = call(
        stress_rims_kernel,
        strip_shape,
        first, faces, second, neighbour, rotation, forcing,
        specs=[VMEM] * 5 + [ANY],
    )
    base, stress, outer, inner = call(
        base_kernel,
        (shape(2, *block), shape(3, *block), strip_shape, strip_shape),
        stress_rims, rims, velocity, ice_cover, mass, strength, forcing, weight_strips,
        scratch=pad2 + pad3,
    )
    first, second = both_ways(outer)
    low = scatter_call(
        functools.partial(inside_kernel, 2), HALF_ROWS, shape(2, HALF_ROWS, LANES),
        slot_cell, arrived, count,
    )
    faces, rims = call(
        functools.partial(edge_stress_kernel, opening=False),
        (strip_shape, strip_shape),
        first, outer, second, inner, neighbour, rotation, strength_strips, faces,
        scratch=line,
    )
    first, second = both_ways(faces)
    high = scatter_call(
        functools.partial(inside_kernel, 2 + HALF), HALF_ROWS, shape(2, HALF_ROWS, LANES),
        slot_cell, arrived, count,
    )
    moving, kept, stress = call(
        second_stress_kernel,
        (shape(2, *block), shape(3, *block), shape(3, *block)),
        base, ice_cover, mass, low, high, outer, inner, rims, strength, stress,
        out_specs=(VMEM, VMEM, ANY),
        scratch=pad2 + [sems((3,))],
    )
    moving = call(
        last_kernel,
        shape(2 * SIDE * SIDE, LANES),
        first, faces, second, neighbour, rotation, moving, base, ice_cover, mass, kept,
        out_specs=ANY,
        scratch=pad3 + [pltpu.VMEM((2 * SIDE * SIDE, LANES), F32), sems((5,))],
    )
    moving = jnp.transpose(moving.reshape(SIDE, SIDE, 2, LANES), (2, 0, 1, 3))
    return (moving, stress)


def solution(mesh):
    placed = (
        P(None, None, None, BOTH),
        P(None, None, BOTH),
        P(None, None, BOTH),
        P(None, None, BOTH),
        P(None, BOTH),
        P(None, BOTH),
        P("cat", "blocks", None, None),
        P(None, "blocks", None, None),
        P(None, "blocks", None, None),
        P(None, "cat"),
        P(None, BOTH, None),
        P(None, BOTH),
    )
    return jax.shard_map(
        shards,
        mesh=mesh,
        in_specs=placed,
        out_specs=(P(None, None, None, BOTH), P(None, None, None, BOTH)),
        check_vma=False,
    )
```

```python
import functools

import jax
import jax.numpy as jnp
from jax import lax
from jax.experimental import pallas as pl
from jax.experimental.pallas import tpu as pltpu
from jax.sharding import PartitionSpec as P

F32 = jnp.float32
BF16 = jnp.bfloat16
I32 = jnp.int32

SIDE = 30
ROWS = 32
LANES = 128
OWNERS = 64
SLOTS = 256
EXTRA = 8
CHUNK = 16
INSIDE = SIDE - 4
HALF = INSIDE // 2
HALF_ROWS = 352
BOTH = ("blocks", "cat")

PARAMS = pltpu.CompilerParams(vmem_limit_bytes=6 * 1024 * 1024)
SCATTER_PARAMS = pltpu.CompilerParams(vmem_limit_bytes=12 * 1024 * 1024)
ALONE_PARAMS = pltpu.CompilerParams(vmem_limit_bytes=60 * 1024 * 1024)
ANY = pl.BlockSpec(memory_space=pl.ANY)
VMEM = pl.BlockSpec(memory_space=pltpu.VMEM)
SMEM = pl.BlockSpec(memory_space=pltpu.SMEM)


def shape(*dims, dtype=F32):
    return jax.ShapeDtypeStruct(dims, dtype)


def fill_halves(halves, value_of):
    for half in range(2):
        halves[half] = value_of(slice(half * LANES, half * LANES + LANES))


def quarter(halves, half, receiver):
    return halves[half, pl.ds(receiver, OWNERS, stride=4), :]


def wind_kernel(air_ref, ocean_ref, out_ref, wind):
    cat = lax.axis_index("cat")
    for which, ref in enumerate((air_ref, ocean_ref)):
        for member in range(2):
            fill_halves(wind.at[which, member], lambda lanes: ref[member, 0, :, lanes])
    for half in range(2):
        lanes = slice(half * LANES, half * LANES + LANES)
        for which in range(2):
            east = quarter(wind.at[which, 0], half, cat)
            north = quarter(wind.at[which, 1], half, cat)
            speed = jnp.sqrt(east * east + north * north)
            out_ref[2 * which, :, lanes] = speed * east
            out_ref[2 * which + 1, :, lanes] = speed * north


def partial_kernel(mine_ref, first_ref, second_ref, third_ref, wind_ref, out_ref):
    parts = (mine_ref, first_ref, second_ref, third_ref)
    totals = [0.0, 0.0]
    for which in range(2):
        at = OWNERS + which
        weight = jnp.zeros((OWNERS, SLOTS), F32)
        for part in parts:
            weight += part[0:OWNERS, :] * part[at : at + 1, :]
        for member in range(2):
            totals[member] += weight * wind_ref[2 * which + member]
    for member in range(2):
        out_ref[:, member, :] = totals[member]


def split_lanes(lane_hits, value):
    high = value.astype(BF16).astype(F32)
    return (
        jnp.where(lane_hits, high, 0.0).astype(BF16),
        jnp.where(lane_hits, value - high, 0.0).astype(BF16),
    )


def spread_values(cell_ref, value_ref, count_ref, spread, index):
    block = lax.broadcasted_iota(I32, (LANES, SLOTS), 0)
    slot = lax.broadcasted_iota(I32, (1, SLOTS), 1)
    columns = pl.ds(index * SLOTS, SLOTS)
    lane_hits = block == lax.bitwise_and(cell_ref[index], LANES - 1)
    live = slot < count_ref[0, pl.program_id(0) * CHUNK + index]
    for member in range(2):
        value = jnp.where(live, value_ref[index, member : member + 1, :], 0.0)
        high, low = split_lanes(lane_hits, value)
        spread[pl.ds(member * 2 * LANES, LANES), columns] = high
        spread[pl.ds(member * 2 * LANES + LANES, LANES), columns] = low


def cell_number(cell):
    return lax.shift_right_logical(cell, 7)


def accumulate(total, hot, spread):
    total[...] += lax.dot_general(
        hot[...], spread[...], (((1,), (1,)), ((), ())), preferred_element_type=F32
    )


def summed_terms(total, member):
    at = member * 2 * LANES
    return total[:, at : at + LANES] + total[:, at + LANES : at + 2 * LANES]


def edge_kernel(cell_ref, value_ref, count_ref, after_ref, out_ref, hot, spread, total):
    step = pl.program_id(0)

    @pl.when(step == 0)
    def _():
        total[...] = jnp.zeros_like(total)

    along = lax.broadcasted_iota(I32, (ROWS, SLOTS), 0)
    for index in range(CHUNK):
        number = cell_number(cell_ref[index])
        east = lax.shift_right_logical(number * 2185, 16)
        north = number - east * SIDE
        columns = pl.ds(index * SLOTS, SLOTS)
        east_hot = (along == east).astype(F32).astype(BF16)
        north_hot = (along == north).astype(F32).astype(BF16)
        empty = jnp.zeros_like(east_hot)
        for layer in range(2):
            for side, here in enumerate(
                (east == layer, north == layer, east == SIDE - 1 - layer, north == SIDE - 1 - layer)
            ):
                hot[pl.ds((layer * 4 + side) * ROWS, ROWS), columns] = jnp.where(
                    here, east_hot if side % 2 else north_hot, empty
                )
        spread_values(cell_ref, value_ref, count_ref, spread, index)
    accumulate(total, hot, spread)

    @pl.when(step == pl.num_programs(0) - 1)
    def _():
        for member in range(2):
            out_ref[member] = summed_terms(total, member).reshape(8, ROWS, LANES)


def inside_kernel(first, cell_ref, value_ref, count_ref, out_ref, hot, spread, total):
    step = pl.program_id(0)

    @pl.when(step == 0)
    def _():
        total[...] = jnp.zeros_like(total)

    row = lax.broadcasted_iota(I32, (HALF_ROWS, SLOTS), 0)
    east = lax.shift_right_logical(row * 2521, 16)
    wanted = jnp.where(
        east < HALF, (east + first) * SIDE + 2 + (row - east * INSIDE), -1
    )
    for index in range(CHUNK):
        columns = pl.ds(index * SLOTS, SLOTS)
        hits = wanted == cell_number(cell_ref[index])
        hot[:, columns] = hits.astype(F32).astype(BF16)
        spread_values(cell_ref, value_ref, count_ref, spread, index)
    accumulate(total, hot, spread)

    @pl.when(step == pl.num_programs(0) - 1)
    def _():
        for member in range(2):
            out_ref[member] = summed_terms(total, member)


def scatter_call(kernel, rows, outs, cell, value, count, *more):
    width = CHUNK * SLOTS

    def whole(ref):
        return pl.BlockSpec(ref.shape, lambda k, rank=len(ref.shape): (0,) * rank)

    return pl.pallas_call(
        kernel,
        out_shape=outs,
        grid=(OWNERS // CHUNK,),
        in_specs=[
            pl.BlockSpec((CHUNK, 1, SLOTS), lambda k: (k, 0, 0)),
            pl.BlockSpec((CHUNK, 2, SLOTS), lambda k: (k, 0, 0)),
            SMEM,
        ]
        + [ANY] * len(more),
        out_specs=jax.tree.map(whole, outs),
        scratch_shapes=[
            pltpu.VMEM((rows, width), BF16),
            pltpu.VMEM((4 * LANES, width), BF16),
            pltpu.VMEM((rows, 4 * LANES), F32),
        ],
        compiler_params=SCATTER_PARAMS,
        cost_estimate=pl.CostEstimate(
            flops=2 * rows * 4 * LANES * OWNERS * SLOTS, bytes_accessed=1 << 20, transcendentals=0
        ),
    )(cell, value, count, *more)


def gather_rims(strips, neighbour_ref, turn_ref, store):
    devices = lax.axis_size(BOTH)
    here = lax.axis_index(BOTH)
    start = (here - 1) * LANES
    odd = lax.bitwise_and(here, 1)
    holders = (2 * odd, 1, 2 - 2 * odd)
    for side in range(4):
        place = lax.rem(
            neighbour_ref[side : side + 1, :] - start + devices * LANES, devices * LANES
        )
        turns = turn_ref[side : side + 1, :]
        source = lax.bitwise_and(turns + (side + 2), 3)
        holder = lax.shift_right_logical(place, 7)
        lane = jnp.broadcast_to(lax.bitwise_and(place, LANES - 1), (ROWS, LANES))
        rows = [jnp.zeros((ROWS, LANES), F32) for _ in range(2)]
        for where, ref in zip(holders, strips):
            for edge in range(4):
                hits = jnp.broadcast_to((holder == where) & (source == edge), (ROWS, LANES))
                for member in range(2):
                    picked = jnp.take_along_axis(
                        ref[member, edge], lane, axis=1, mode="promise_in_bounds"
                    )
                    rows[member] = jnp.where(hits, picked, rows[member])
        store(side, turns, rows)


def turned_vector(turns, rows):
    cosine = (turns == 0).astype(F32) - (turns == 2).astype(F32)
    sine = (turns == 1).astype(F32) - (turns == 3).astype(F32)
    return cosine * rows[0] - sine * rows[1], sine * rows[0] + cosine * rows[1]


def turned_stress(turns, rows):
    parity = (1 - 2 * lax.bitwise_and(turns, 1)).astype(F32)
    return rows[0], parity * rows[1]


def store_rim(pad, member, side, rim):
    if side == 0 or side == 2:
        pad[member, 0 if side == 0 else SIDE + 1, 8 : 8 + SIDE, :] = rim[0:SIDE]
    else:
        column = 7 if side == 1 else 8 + SIDE
        for i in range(SIDE):
            pad[member, i + 1, column : column + 1, :] = rim[i : i + 1]


def store_strips(out_ref, member, cell_of, layer=0):
    far = SIDE - 1 - layer
    out_ref[member, :, SIDE:ROWS, :] = jnp.zeros((4, ROWS - SIDE, LANES), F32)
    out_ref[member, 0, 0:SIDE, :] = cell_of(layer, slice(0, SIDE))
    out_ref[member, 2, 0:SIDE, :] = cell_of(far, slice(0, SIDE))
    for i in range(SIDE):
        out_ref[member, 1, i : i + 1, :] = cell_of(i, slice(layer, layer + 1))
        out_ref[member, 3, i : i + 1, :] = cell_of(i, slice(far, far + 1))


def cell_rows(i, member, cells=slice(0, SIDE)):
    start = 2 * (SIDE * i + cells.start) + member
    count = cells.stop - cells.start
    return slice(start, start + 1) if count == 1 else pl.ds(start, count, stride=2)


def run_copies(pairs, sems):
    copies = [
        pltpu.make_async_copy(source, target, sems.at[at])
        for at, (source, target) in enumerate(pairs)
    ]
    for copy in copies:
        copy.start()
    return copies


def pack_kernel(conc_hbm, drag_ref, *rest):
    outs, halves, sems = rest[:4], rest[4], rest[5]
    cuts = [(half, start) for half in range(2) for start in (0, 2 * OWNERS)]
    copies = run_copies(
        [
            (
                conc_hbm.at[0, 0, pl.ds(start, 2 * OWNERS), half * LANES : half * LANES + LANES],
                halves.at[half, pl.ds(start, 2 * OWNERS)],
            )
            for half, start in cuts
        ],
        sems,
    )
    cat = lax.axis_index("cat")
    row = lax.broadcasted_iota(I32, (EXTRA, SLOTS), 0)
    coefficients = jnp.where(row == 0, drag_ref[0, 0], drag_ref[0, 1])
    for packed_ref in outs:
        packed_ref[OWNERS : OWNERS + EXTRA, :] = coefficients
    for copy in copies:
        copy.wait()
    for step, packed_ref in enumerate(outs):
        receiver = lax.bitwise_xor(cat, step)
        for half in range(2):
            lanes = slice(half * LANES, half * LANES + LANES)
            packed_ref[0:OWNERS, lanes] = quarter(halves, half, receiver)


def outer_strips_kernel(
    velocity_hbm, cover_hbm, out_ref, lines, cover_rows, cover_low, cover_high, sems
):
    last = SIDE - 1
    copies = run_copies(
        [
            (velocity_hbm.at[0], lines.at[0]),
            (velocity_hbm.at[:, 0], lines.at[1]),
            (velocity_hbm.at[last], lines.at[2]),
            (velocity_hbm.at[:, last], lines.at[3]),
            (cover_hbm.at[0], cover_rows.at[0]),
            (cover_hbm.at[last], cover_rows.at[1]),
            (cover_hbm.at[:, 0:8], cover_low),
            (cover_hbm.at[:, 24:SIDE], cover_high),
        ],
        sems,
    )
    for copy in copies:
        copy.wait()
    out_ref[:, :, SIDE:ROWS, :] = jnp.zeros((2, 4, ROWS - SIDE, LANES), F32)
    for side in range(4):
        for t in range(SIDE):
            if side % 2 == 0:
                covered = cover_rows[side // 2, t : t + 1, :]
            else:
                covered = cover_low[t, 0:1, :] if side == 1 else cover_high[t, 5:6, :]
            covered = covered.astype(F32)
            for member in range(2):
                out_ref[member, side, t : t + 1, :] = (
                    lines[side, t, member : member + 1, :] * covered
                )


def weight_of(cover, mass):
    return cover.astype(F32) / (4.0 * mass + 1.0)


def inner_strips_kernel(
    velocity_ref,
    cover_ref,
    strength_ref,
    mass_ref,
    summed_ref,
    inner_ref,
    strength_strips_ref,
    weight_strips_ref,
):
    for member in range(2):
        store_strips(
            inner_ref,
            member,
            lambda i, j: velocity_ref[cell_rows(i, member, j), :] * cover_ref[i, j, :].astype(F32),
            1,
        )
    store_strips(strength_strips_ref, 0, lambda i, j: strength_ref[i, j, :])
    for layer in range(2):
        at = slice(4 * layer, 4 * layer + 4)
        store_strips(
            weight_strips_ref.at[:, at],
            0,
            lambda i, j: weight_of(cover_ref[i, j, :], mass_ref[i, j, :]),
            layer,
        )


def derivatives(pad, member, i):
    middle = slice(8, 8 + SIDE)
    east = 0.5 * (pad[member, i + 2, middle, :] - pad[member, i, middle, :])
    north = 0.5 * (pad[member, i + 1, 9 : 9 + SIDE, :] - pad[member, i + 1, 7 : 7 + SIDE, :])
    return east, north


def targets_of(east_e, east_n, north_e, north_n, strength):
    divergence = east_e + north_n
    tension = east_e - north_n
    shearing = east_n + north_e
    inverse = lax.rsqrt(
        divergence * divergence + (tension * tension + shearing * shearing) * 0.25 + 0.25
    )
    scaled = strength * inverse
    return (
        divergence * scaled - strength,
        0.25 * (tension * scaled),
        0.125 * (shearing * scaled),
    )


def stress_targets(pad, strength, i):
    return targets_of(*derivatives(pad, 0, i), *derivatives(pad, 1, i), strength)


def forces(pad, i):
    middle = slice(8, 8 + SIDE)
    upper, lower = slice(9, 9 + SIDE), slice(7, 7 + SIDE)
    shear_east, shear_north = derivatives(pad, 1, i)
    force_east = 0.5 * (pad[0, i + 2, middle, :] - pad[0, i, middle, :]) + shear_north
    force_north = shear_east + 0.5 * (pad[2, i + 1, upper, :] - pad[2, i + 1, lower, :])
    return force_east, force_north


def stress_rims_kernel(
    one_ref, own_ref, two_ref, neighbour_ref, turn_ref, forcing_ref, out_ref
):
    def store(side, turns, rows):
        for member, rim in enumerate(turned_stress(turns, rows)):
            out_ref[member, side] = rim

    gather_rims((one_ref, own_ref, two_ref), neighbour_ref, turn_ref, store)


def fill_stress(pad, stress_ref):
    for i in range(SIDE):
        first_stress, second_stress = stress_ref[0, i], stress_ref[1, i]
        pad[0, i + 1, 8 : 8 + SIDE, :] = 0.5 * (first_stress + second_stress)
        pad[1, i + 1, 8 : 8 + SIDE, :] = stress_ref[2, i]
        pad[2, i + 1, 8 : 8 + SIDE, :] = 0.5 * (first_stress - second_stress)


def store_stress_rim(pad, side, normal, shear):
    store_rim(pad, 0 if side in (0, 2) else 2, side, normal)
    store_rim(pad, 1, side, shear)


def base_kernel(
    stress_rims_ref,
    rims_ref,
    velocity_ref,
    cover_ref,
    mass_ref,
    strength_ref,
    forcing_ref,
    weight_ref,
    base_ref,
    stress_ref,
    outer_ref,
    inner_ref,
    line,
    pad,
):
    for i in range(SIDE):
        covered = cover_ref[i].astype(F32)
        for member in range(2):
            line[member, i + 1, 8 : 8 + SIDE, :] = velocity_ref[cell_rows(i, member), :] * covered
    for member in range(2):
        for side in range(4):
            store_rim(line, member, side, rims_ref[member, side])
    for i in range(SIDE):
        targets = stress_targets(line, strength_ref[i], i)
        for member in range(3):
            stress_ref[member, i] = 0.5 * targets[member]
    fill_stress(pad, stress_ref)
    for side in range(4):
        store_stress_rim(pad, side, stress_rims_ref[0, side], stress_rims_ref[1, side])
    for i in range(SIDE):
        force_east, force_north = forces(pad, i)
        eastward = line[0, i + 1, 8 : 8 + SIDE, :]
        northward = line[1, i + 1, 8 : 8 + SIDE, :]
        mass = mass_ref[i]
        weight = weight_of(cover_ref[i], mass)
        base_ref[0, i] = weight * (mass * (4.0 * eastward + 0.5 * northward) + force_east)
        base_ref[1, i] = weight * (mass * (4.0 * northward - 0.5 * eastward) + force_north)
    for layer, out_ref in enumerate((outer_ref, inner_ref)):
        at = slice(4 * layer, 4 * layer + 4)
        for member in range(2):
            store_strips(out_ref, member, lambda i, j: base_ref[member, i, j, :], layer)
            out_ref[member] += weight_ref[0, at] * forcing_ref[member, at]


def edge_stress_kernel(
    one_ref,
    outer_ref,
    two_ref,
    inner_ref,
    neighbour_ref,
    turn_ref,
    strength_ref,
    *rest,
    opening,
):
    faces_ref, rims_ref, line = rest[-3:]

    def store(side, turns, rows):
        for member, rim in enumerate(turned_vector(turns, rows)):
            rims_ref[member, side] = rim

    gather_rims((one_ref, outer_ref, two_ref), neighbour_ref, turn_ref, store)
    faces_ref[:, :, SIDE:ROWS, :] = jnp.zeros((2, 4, ROWS - SIDE, LANES), F32)
    for side in range(4):
        end = 0 if side < 2 else SIDE - 1
        across, beside = [], []
        for member in range(2):
            line[member, side, 8 : 8 + SIDE, :] = outer_ref[member, side, 0:SIDE, :]
            lower, upper = (1, 3) if side % 2 == 0 else (0, 2)
            line[member, side, 7:8, :] = rims_ref[member, lower, end : end + 1, :]
            line[member, side, 8 + SIDE : 9 + SIDE, :] = rims_ref[member, upper, end : end + 1, :]
            step = 0.5 * (inner_ref[member, side, 0:SIDE, :] - rims_ref[member, side, 0:SIDE, :])
            across.append(step if side < 2 else -step)
            beside.append(
                0.5 * (line[member, side, 9 : 9 + SIDE, :] - line[member, side, 7 : 7 + SIDE, :])
            )
        east, north = (across, beside) if side % 2 == 0 else (beside, across)
        first, second, shear = targets_of(
            east[0], north[0], east[1], north[1], strength_ref[0, side, 0:SIDE, :]
        )
        normal = 0.5 * (first + second) if side % 2 == 0 else 0.5 * (first - second)
        for member, target in enumerate((normal, shear)):
            old = 0.0 if opening else rest[0][member, side, 0:SIDE, :]
            faces_ref[member, side, 0:SIDE, :] = old + 0.5 * (target - old)


def second_stress_kernel(
    base_ref,
    cover_ref,
    mass_ref,
    low_ref,
    high_ref,
    outer_ref,
    inner_ref,
    rims_ref,
    strength_ref,
    old_ref,
    moving_ref,
    stress_ref,
    stress_hbm,
    pad,
    sems,
):
    for member in range(2):
        for side in range(4):
            store_rim(pad, member, side, rims_ref[member, side])
        for i, ref, side in (
            (0, outer_ref, 0),
            (1, inner_ref, 0),
            (SIDE - 2, inner_ref, 2),
            (SIDE - 1, outer_ref, 2),
        ):
            pad[member, i + 1, 8 : 8 + SIDE, :] = ref[member, side, 0:SIDE, :]
        for i in range(2, SIDE - 2):
            for j, ref, side in (
                (0, outer_ref, 1),
                (1, inner_ref, 1),
                (SIDE - 2, inner_ref, 3),
                (SIDE - 1, outer_ref, 3),
            ):
                pad[member, i + 1, 8 + j : 9 + j, :] = ref[member, side, i : i + 1, :]
    inside = slice(2, SIDE - 2)
    for i in range(2, SIDE - 2):
        weight = weight_of(cover_ref[i, inside, :], mass_ref[i, inside, :])
        ref, at = (low_ref, i - 2) if i < 2 + HALF else (high_ref, i - 2 - HALF)
        for member in range(2):
            pad[member, i + 1, 10 : 10 + INSIDE, :] = base_ref[member, i, inside, :] + weight * (
                ref[member, at * INSIDE : at * INSIDE + INSIDE, :]
            )
    copies = []
    for i in range(SIDE):
        targets = stress_targets(pad, strength_ref[i], i)
        for member in range(3):
            old = old_ref[member, i]
            stress_ref[member, i] = old + 0.5 * (targets[member] - old)
        for member in range(2):
            moving_ref[member, i] = pad[member, i + 1, 8 : 8 + SIDE, :]
        if i % 10 == 9:
            part = pl.ds(i - 9, 10)
            copies.append(
                pltpu.make_async_copy(
                    stress_ref.at[:, part], stress_hbm.at[:, part], sems.at[i // 10]
                )
            )
            copies[-1].start()
    for copy in copies:
        copy.wait()


def last_kernel(
    one_ref,
    own_ref,
    two_ref,
    neighbour_ref,
    turn_ref,
    moving_ref,
    base_ref,
    cover_ref,
    mass_ref,
    stress_ref,
    out_hbm,
    pad,
    out_ref,
    sems,
):
    copies = []
    fill_stress(pad, stress_ref)

    def store(side, turns, rows):
        store_stress_rim(pad, side, *turned_stress(turns, rows))

    gather_rims((one_ref, own_ref, two_ref), neighbour_ref, turn_ref, store)
    for i in range(SIDE):
        force_east, force_north = forces(pad, i)
        eastward, northward = moving_ref[0, i], moving_ref[1, i]
        mass = mass_ref[i]
        weight = weight_of(cover_ref[i], mass)
        out_ref[cell_rows(i, 0), :] = weight * (
            mass * (4.0 * eastward + 0.5 * northward) + force_east
        ) + (eastward - base_ref[0, i])
        out_ref[cell_rows(i, 1), :] = weight * (
            mass * (4.0 * northward - 0.5 * eastward) + force_north
        ) + (northward - base_ref[1, i])
        if i % 6 == 5:
            part = pl.ds(60 * (i - 5), 360)
            copies.append(
                pltpu.make_async_copy(out_ref.at[part], out_hbm.at[part], sems.at[i // 6])
            )
            copies[-1].start()
    for copy in copies:
        copy.wait()


def call(kernel, outs, *args, specs=None, out_specs=None, scratch=(), work=1 << 22, params=PARAMS):
    return pl.pallas_call(
        kernel,
        out_shape=outs,
        in_specs=specs or [VMEM] * len(args),
        out_specs=out_specs or jax.tree.map(lambda _: VMEM, outs),
        scratch_shapes=list(scratch),
        compiler_params=params,
        cost_estimate=pl.CostEstimate(flops=work, bytes_accessed=1 << 22, transcendentals=0),
    )(*args)


def shards(
    velocity,
    strength,
    mass,
    ice_cover,
    neighbour,
    rotation,
    concentration,
    air_wind,
    ocean_current,
    drag,
    slot_cell,
    slot_count,
):
    devices = lax.axis_size(BOTH)
    pairs = [[(i, i + 1) for i in range(start, devices, 2)] for start in (1, 0)]
    swaps = [[(i, j % devices) for i, j in p] + [(j % devices, i) for i, j in p] for p in pairs]

    def both_ways(strips):
        return [lax.ppermute(strips, BOTH, swap) for swap in swaps]

    strip_shape = shape(2, 4, ROWS, LANES)
    block = (SIDE, SIDE, LANES)
    pad2 = [pltpu.VMEM((2, ROWS, 48, LANES), F32)]
    pad3 = [pltpu.VMEM((3, ROWS, 48, LANES), F32)]
    count = slot_count.reshape(1, OWNERS)

    sems = pltpu.SemaphoreType.DMA
    by_cell = jnp.transpose(velocity, (1, 2, 0, 3))
    velocity = by_cell.reshape(2 * SIDE * SIDE, LANES)
    packed = call(
        pack_kernel,
        [shape(OWNERS + EXTRA, SLOTS)] * 4,
        concentration,
        drag.reshape(1, 2),
        specs=[ANY, SMEM],
        scratch=[pltpu.VMEM((2, 4 * OWNERS, LANES), F32), sems((4,))],
        params=ALONE_PARAMS,
    )
    parts = [packed[0]] + [
        lax.ppermute(packed[step], "cat", [(i, i ^ step) for i in range(4)])
        for step in (1, 2, 3)
    ]

    line = [pltpu.VMEM((2, 4, 48, LANES), F32)]
    winds = call(
        wind_kernel,
        shape(4, OWNERS, SLOTS),
        air_wind,
        ocean_current,
        scratch=[pltpu.VMEM((2, 2, 2, 4 * OWNERS, LANES), F32)],
    )
    summed = call(partial_kernel, shape(OWNERS, 2, SLOTS), *parts, winds, work=1 << 31)
    arrived = lax.all_to_all(summed, "blocks", split_axis=0, concat_axis=0, tiled=True)

    outer = call(
        outer_strips_kernel,
        strip_shape,
        by_cell,
        ice_cover,
        specs=[ANY] * 2,
        scratch=[
            pltpu.VMEM((4, SIDE, 2, LANES), F32),
            pltpu.VMEM((2, SIDE, LANES), I32),
            pltpu.VMEM((SIDE, 8, LANES), I32),
            pltpu.VMEM((SIDE, 6, LANES), I32),
            sems((8,)),
        ],
        params=ALONE_PARAMS,
    )
    first, second = both_ways(outer)
    inner, strength_strips, weight_strips = call(
        inner_strips_kernel,
        (strip_shape, shape(1, 4, ROWS, LANES), shape(1, 8, ROWS, LANES)),
        velocity, ice_cover, strength, mass, summed,
        specs=[VMEM] * 4 + [ANY],
    )
    faces, rims = call(
        functools.partial(edge_stress_kernel, opening=True),
        (strip_shape, strip_shape),
        first, outer, second, inner, neighbour, rotation, strength_strips,
        scratch=line,
        work=1 << 34,
    )
    first, second = both_ways(faces)

    forcing = scatter_call(
        edge_kernel, 8 * ROWS, shape(2, 8, ROWS, LANES), slot_cell, arrived, count, faces
    )
    stress_rims = call(
        stress_rims_kernel,
        strip_shape,
        first, faces, second, neighbour, rotation, forcing,
        specs=[VMEM] * 5 + [ANY],
    )
    base, stress, outer, inner = call(
        base_kernel,
        (shape(2, *block), shape(3, *block), strip_shape, strip_shape),
        stress_rims, rims, velocity, ice_cover, mass, strength, forcing, weight_strips,
        scratch=pad2 + pad3,
    )
    first, second = both_ways(outer)
    low = scatter_call(
        functools.partial(inside_kernel, 2), HALF_ROWS, shape(2, HALF_ROWS, LANES),
        slot_cell, arrived, count,
    )
    faces, rims = call(
        functools.partial(edge_stress_kernel, opening=False),
        (strip_shape, strip_shape),
        first, outer, second, inner, neighbour, rotation, strength_strips, faces,
        scratch=line,
    )
    first, second = both_ways(faces)
    high = scatter_call(
        functools.partial(inside_kernel, 2 + HALF), HALF_ROWS, shape(2, HALF_ROWS, LANES),
        slot_cell, arrived, count,
    )
    moving, kept, stress = call(
        second_stress_kernel,
        (shape(2, *block), shape(3, *block), shape(3, *block)),
        base, ice_cover, mass, low, high, outer, inner, rims, strength, stress,
        out_specs=(VMEM, VMEM, ANY),
        scratch=pad2 + [sems((3,))],
    )
    moving = call(
        last_kernel,
        shape(2 * SIDE * SIDE, LANES),
        first, faces, second, neighbour, rotation, moving, base, ice_cover, mass, kept,
        out_specs=ANY,
        scratch=pad3 + [pltpu.VMEM((2 * SIDE * SIDE, LANES), F32), sems((5,))],
    )
    moving = jnp.transpose(moving.reshape(SIDE, SIDE, 2, LANES), (2, 0, 1, 3))
    return (moving, stress)


def solution(mesh):
    placed = (
        P(None, None, None, BOTH),
        P(None, None, BOTH),
        P(None, None, BOTH),
        P(None, None, BOTH),
        P(None, BOTH),
        P(None, BOTH),
        P("cat", "blocks", None, None),
        P(None, "blocks", None, None),
        P(None, "blocks", None, None),
        P(None, "cat"),
        P(None, BOTH, None),
        P(None, BOTH),
    )
    return jax.shard_map(
        shards,
        mesh=mesh,
        in_specs=placed,
        out_specs=(P(None, None, None, BOTH), P(None, None, None, BOTH)),
        check_vma=False,
    )
```

```python
import functools

import jax
import jax.numpy as jnp
from jax import lax
from jax.experimental import pallas as pl
from jax.experimental.pallas import tpu as pltpu
from jax.sharding import PartitionSpec as P

F32 = jnp.float32
BF16 = jnp.bfloat16
I32 = jnp.int32

SIDE = 30
ROWS = 32
LANES = 128
OWNERS = 64
SLOTS = 256
EXTRA = 8
CHUNK = 16
INSIDE = SIDE - 4
HALF = INSIDE // 2
HALF_ROWS = 352
BOTH = ("blocks", "cat")

PARAMS = pltpu.CompilerParams(vmem_limit_bytes=6 * 1024 * 1024)
SCATTER_PARAMS = pltpu.CompilerParams(vmem_limit_bytes=12 * 1024 * 1024)
ALONE_PARAMS = pltpu.CompilerParams(vmem_limit_bytes=60 * 1024 * 1024)
WIND_PARAMS = pltpu.CompilerParams(vmem_limit_bytes=59600 * 1024)
ANY = pl.BlockSpec(memory_space=pl.ANY)
VMEM = pl.BlockSpec(memory_space=pltpu.VMEM)
SMEM = pl.BlockSpec(memory_space=pltpu.SMEM)


def shape(*dims, dtype=F32):
    return jax.ShapeDtypeStruct(dims, dtype)


def fill_halves(halves, value_of):
    for half in range(2):
        halves[half] = value_of(slice(half * LANES, half * LANES + LANES))


def quarter(halves, half, receiver):
    return halves[half, pl.ds(receiver, OWNERS, stride=4), :]


def wind_kernel(air_hbm, ocean_hbm, out_ref, wind, sems):
    cat = lax.axis_index("cat")
    copies = run_copies(
        [
            (
                hbm.at[member, 0, :, half * LANES : half * LANES + LANES],
                wind.at[which, member, half],
            )
            for which, hbm in enumerate((air_hbm, ocean_hbm))
            for member in range(2)
            for half in range(2)
        ],
        sems,
    )
    for copy in copies:
        copy.wait()
    for half in range(2):
        lanes = slice(half * LANES, half * LANES + LANES)
        for which in range(2):
            east = quarter(wind.at[which, 0], half, cat)
            north = quarter(wind.at[which, 1], half, cat)
            speed = jnp.sqrt(east * east + north * north)
            out_ref[2 * which, :, lanes] = speed * east
            out_ref[2 * which + 1, :, lanes] = speed * north


def partial_kernel(mine_ref, first_ref, second_ref, third_ref, wind_ref, out_ref):
    parts = (mine_ref, first_ref, second_ref, third_ref)
    totals = [0.0, 0.0]
    for which in range(2):
        at = OWNERS + which
        weight = jnp.zeros((OWNERS, SLOTS), F32)
        for part in parts:
            weight += part[0:OWNERS, :] * part[at : at + 1, :]
        for member in range(2):
            totals[member] += weight * wind_ref[2 * which + member]
    for member in range(2):
        out_ref[:, member, :] = totals[member]


def split_lanes(lane_hits, value):
    high = value.astype(BF16).astype(F32)
    return (
        jnp.where(lane_hits, high, 0.0).astype(BF16),
        jnp.where(lane_hits, value - high, 0.0).astype(BF16),
    )


def spread_values(cell_ref, value_ref, count_ref, spread, index):
    block = lax.broadcasted_iota(I32, (LANES, SLOTS), 0)
    slot = lax.broadcasted_iota(I32, (1, SLOTS), 1)
    columns = pl.ds(index * SLOTS, SLOTS)
    lane_hits = block == lax.bitwise_and(cell_ref[index], LANES - 1)
    live = slot < count_ref[0, pl.program_id(0) * CHUNK + index]
    for member in range(2):
        value = jnp.where(live, value_ref[index, member : member + 1, :], 0.0)
        high, low = split_lanes(lane_hits, value)
        spread[pl.ds(member * 2 * LANES, LANES), columns] = high
        spread[pl.ds(member * 2 * LANES + LANES, LANES), columns] = low


def cell_number(cell):
    return lax.shift_right_logical(cell, 7)


def accumulate(total, hot, spread):
    total[...] += lax.dot_general(
        hot[...], spread[...], (((1,), (1,)), ((), ())), preferred_element_type=F32
    )


def summed_terms(total, member):
    at = member * 2 * LANES
    return total[:, at : at + LANES] + total[:, at + LANES : at + 2 * LANES]


def edge_kernel(cell_ref, value_ref, count_ref, after_ref, out_ref, hot, spread, total):
    step = pl.program_id(0)

    @pl.when(step == 0)
    def _():
        total[...] = jnp.zeros_like(total)

    along = lax.broadcasted_iota(I32, (ROWS, SLOTS), 0)
    for index in range(CHUNK):
        number = cell_number(cell_ref[index])
        east = lax.shift_right_logical(number * 2185, 16)
        north = number - east * SIDE
        columns = pl.ds(index * SLOTS, SLOTS)
        east_hot = (along == east).astype(F32).astype(BF16)
        north_hot = (along == north).astype(F32).astype(BF16)
        empty = jnp.zeros_like(east_hot)
        for layer in range(2):
            for side, here in enumerate(
                (east == layer, north == layer, east == SIDE - 1 - layer, north == SIDE - 1 - layer)
            ):
                hot[pl.ds((layer * 4 + side) * ROWS, ROWS), columns] = jnp.where(
                    here, east_hot if side % 2 else north_hot, empty
                )
        spread_values(cell_ref, value_ref, count_ref, spread, index)
    accumulate(total, hot, spread)

    @pl.when(step == pl.num_programs(0) - 1)
    def _():
        for member in range(2):
            out_ref[member] = summed_terms(total, member).reshape(8, ROWS, LANES)


def inside_kernel(first, cell_ref, value_ref, count_ref, out_ref, hot, spread, total):
    step = pl.program_id(0)

    @pl.when(step == 0)
    def _():
        total[...] = jnp.zeros_like(total)

    row = lax.broadcasted_iota(I32, (HALF_ROWS, SLOTS), 0)
    east = lax.shift_right_logical(row * 2521, 16)
    wanted = jnp.where(
        east < HALF, (east + first) * SIDE + 2 + (row - east * INSIDE), -1
    )
    for index in range(CHUNK):
        columns = pl.ds(index * SLOTS, SLOTS)
        hits = wanted == cell_number(cell_ref[index])
        hot[:, columns] = hits.astype(F32).astype(BF16)
        spread_values(cell_ref, value_ref, count_ref, spread, index)
    accumulate(total, hot, spread)

    @pl.when(step == pl.num_programs(0) - 1)
    def _():
        for member in range(2):
            out_ref[member] = summed_terms(total, member)


def scatter_call(kernel, rows, outs, cell, value, count, *more):
    width = CHUNK * SLOTS

    def whole(ref):
        return pl.BlockSpec(ref.shape, lambda k, rank=len(ref.shape): (0,) * rank)

    return pl.pallas_call(
        kernel,
        out_shape=outs,
        grid=(OWNERS // CHUNK,),
        in_specs=[
            pl.BlockSpec((CHUNK, 1, SLOTS), lambda k: (k, 0, 0)),
            pl.BlockSpec((CHUNK, 2, SLOTS), lambda k: (k, 0, 0)),
            SMEM,
        ]
        + [ANY] * len(more),
        out_specs=jax.tree.map(whole, outs),
        scratch_shapes=[
            pltpu.VMEM((rows, width), BF16),
            pltpu.VMEM((4 * LANES, width), BF16),
            pltpu.VMEM((rows, 4 * LANES), F32),
        ],
        compiler_params=SCATTER_PARAMS,
        cost_estimate=pl.CostEstimate(
            flops=2 * rows * 4 * LANES * OWNERS * SLOTS, bytes_accessed=1 << 20, transcendentals=0
        ),
    )(cell, value, count, *more)


def gather_rims(strips, neighbour_ref, turn_ref, store):
    devices = lax.axis_size(BOTH)
    here = lax.axis_index(BOTH)
    start = (here - 1) * LANES
    odd = lax.bitwise_and(here, 1)
    holders = (2 - 2 * odd, 1, 2 * odd)
    for side in range(4):
        place = lax.rem(
            neighbour_ref[side : side + 1, :] - start + devices * LANES, devices * LANES
        )
        turns = turn_ref[side : side + 1, :]
        source = lax.bitwise_and(turns + (side + 2), 3)
        holder = lax.shift_right_logical(place, 7)
        lane = jnp.broadcast_to(lax.bitwise_and(place, LANES - 1), (ROWS, LANES))
        rows = [jnp.zeros((ROWS, LANES), F32) for _ in range(2)]
        for where, ref in zip(holders, strips):
            for edge in range(4):
                hits = jnp.broadcast_to((holder == where) & (source == edge), (ROWS, LANES))
                for member in range(2):
                    picked = jnp.take_along_axis(
                        ref[member, edge], lane, axis=1, mode="promise_in_bounds"
                    )
                    rows[member] = jnp.where(hits, picked, rows[member])
        store(side, turns, rows)


def turned_vector(turns, rows):
    cosine = (turns == 0).astype(F32) - (turns == 2).astype(F32)
    sine = (turns == 1).astype(F32) - (turns == 3).astype(F32)
    return cosine * rows[0] - sine * rows[1], sine * rows[0] + cosine * rows[1]


def turned_stress(turns, rows):
    parity = (1 - 2 * lax.bitwise_and(turns, 1)).astype(F32)
    return rows[0], parity * rows[1]


def store_rim(pad, member, side, rim):
    if side == 0 or side == 2:
        pad[member, 0 if side == 0 else SIDE + 1, 8 : 8 + SIDE, :] = rim[0:SIDE]
    else:
        column = 7 if side == 1 else 8 + SIDE
        for i in range(SIDE):
            pad[member, i + 1, column : column + 1, :] = rim[i : i + 1]


def store_strips(out_ref, member, cell_of, layer=0):
    far = SIDE - 1 - layer
    out_ref[member, :, SIDE:ROWS, :] = jnp.zeros((4, ROWS - SIDE, LANES), F32)
    out_ref[member, 0, 0:SIDE, :] = cell_of(layer, slice(0, SIDE))
    out_ref[member, 2, 0:SIDE, :] = cell_of(far, slice(0, SIDE))
    for i in range(SIDE):
        out_ref[member, 1, i : i + 1, :] = cell_of(i, slice(layer, layer + 1))
        out_ref[member, 3, i : i + 1, :] = cell_of(i, slice(far, far + 1))


def cell_rows(i, member, cells=slice(0, SIDE)):
    start = 2 * (SIDE * i + cells.start) + member
    count = cells.stop - cells.start
    return slice(start, start + 1) if count == 1 else pl.ds(start, count, stride=2)


def run_copies(pairs, sems):
    copies = [
        pltpu.make_async_copy(source, target, sems.at[at])
        for at, (source, target) in enumerate(pairs)
    ]
    for copy in copies:
        copy.start()
    return copies


def pack_kernel(conc_ref, drag_ref, *rest):
    outs, halves = rest[:4], rest[4]
    cat = lax.axis_index("cat")
    row = lax.broadcasted_iota(I32, (EXTRA, SLOTS), 0)
    coefficients = jnp.where(row == 0, drag_ref[0, 0], drag_ref[0, 1])
    fill_halves(halves, lambda lanes: conc_ref[0, 0, :, lanes])
    for step, packed_ref in enumerate(outs):
        receiver = lax.bitwise_xor(cat, step)
        for half in range(2):
            lanes = slice(half * LANES, half * LANES + LANES)
            packed_ref[0:OWNERS, lanes] = quarter(halves, half, receiver)
        packed_ref[OWNERS : OWNERS + EXTRA, :] = coefficients


def outer_strips_kernel(
    velocity_hbm, cover_hbm, out_ref, lines, cover_rows, cover_low, cover_high, sems
):
    last = SIDE - 1
    copies = run_copies(
        [
            (velocity_hbm.at[0], lines.at[0]),
            (velocity_hbm.at[:, 0], lines.at[1]),
            (velocity_hbm.at[last], lines.at[2]),
            (velocity_hbm.at[:, last], lines.at[3]),
            (cover_hbm.at[0], cover_rows.at[0]),
            (cover_hbm.at[last], cover_rows.at[1]),
            (cover_hbm.at[:, 0:8], cover_low),
            (cover_hbm.at[:, 24:SIDE], cover_high),
        ],
        sems,
    )
    for copy in copies:
        copy.wait()
    out_ref[:, :, SIDE:ROWS, :] = jnp.zeros((2, 4, ROWS - SIDE, LANES), F32)
    for side in range(4):
        for t in range(SIDE):
            if side % 2 == 0:
                covered = cover_rows[side // 2, t : t + 1, :]
            else:
                covered = cover_low[t, 0:1, :] if side == 1 else cover_high[t, 5:6, :]
            covered = covered.astype(F32)
            for member in range(2):
                out_ref[member, side, t : t + 1, :] = (
                    lines[side, t, member : member + 1, :] * covered
                )


def weight_of(cover, mass):
    return cover.astype(F32) / (4.0 * mass + 1.0)


def inner_strips_kernel(
    velocity_ref,
    cover_ref,
    strength_ref,
    mass_ref,
    summed_ref,
    inner_ref,
    strength_strips_ref,
    weight_strips_ref,
):
    for member in range(2):
        store_strips(
            inner_ref,
            member,
            lambda i, j: velocity_ref[cell_rows(i, member, j), :] * cover_ref[i, j, :].astype(F32),
            1,
        )
    store_strips(strength_strips_ref, 0, lambda i, j: strength_ref[i, j, :])
    for layer in range(2):
        at = slice(4 * layer, 4 * layer + 4)
        store_strips(
            weight_strips_ref.at[:, at],
            0,
            lambda i, j: weight_of(cover_ref[i, j, :], mass_ref[i, j, :]),
            layer,
        )


def derivatives(pad, member, i):
    middle = slice(8, 8 + SIDE)
    east = 0.5 * (pad[member, i + 2, middle, :] - pad[member, i, middle, :])
    north = 0.5 * (pad[member, i + 1, 9 : 9 + SIDE, :] - pad[member, i + 1, 7 : 7 + SIDE, :])
    return east, north


def targets_of(east_e, east_n, north_e, north_n, strength):
    divergence = east_e + north_n
    tension = east_e - north_n
    shearing = east_n + north_e
    inverse = lax.rsqrt(
        divergence * divergence + (tension * tension + shearing * shearing) * 0.25 + 0.25
    )
    scaled = strength * inverse
    return (
        divergence * scaled - strength,
        0.25 * (tension * scaled),
        0.125 * (shearing * scaled),
    )


def stress_targets(pad, strength, i):
    return targets_of(*derivatives(pad, 0, i), *derivatives(pad, 1, i), strength)


def forces(pad, i):
    middle = slice(8, 8 + SIDE)
    upper, lower = slice(9, 9 + SIDE), slice(7, 7 + SIDE)
    shear_east, shear_north = derivatives(pad, 1, i)
    force_east = 0.5 * (pad[0, i + 2, middle, :] - pad[0, i, middle, :]) + shear_north
    force_north = shear_east + 0.5 * (pad[2, i + 1, upper, :] - pad[2, i + 1, lower, :])
    return force_east, force_north


def stress_rims_kernel(
    one_ref, own_ref, two_ref, neighbour_ref, turn_ref, forcing_ref, out_ref
):
    def store(side, turns, rows):
        for member, rim in enumerate(turned_stress(turns, rows)):
            out_ref[member, side] = rim

    gather_rims((one_ref, own_ref, two_ref), neighbour_ref, turn_ref, store)


def fill_stress(pad, stress_ref):
    for i in range(SIDE):
        first_stress, second_stress = stress_ref[0, i], stress_ref[1, i]
        pad[0, i + 1, 8 : 8 + SIDE, :] = 0.5 * (first_stress + second_stress)
        pad[1, i + 1, 8 : 8 + SIDE, :] = stress_ref[2, i]
        pad[2, i + 1, 8 : 8 + SIDE, :] = 0.5 * (first_stress - second_stress)


def store_stress_rim(pad, side, normal, shear):
    store_rim(pad, 0 if side in (0, 2) else 2, side, normal)
    store_rim(pad, 1, side, shear)


def base_kernel(
    stress_rims_ref,
    rims_ref,
    velocity_ref,
    cover_ref,
    mass_ref,
    strength_ref,
    forcing_ref,
    weight_ref,
    base_ref,
    stress_ref,
    outer_ref,
    inner_ref,
    line,
    pad,
):
    for i in range(SIDE):
        covered = cover_ref[i].astype(F32)
        for member in range(2):
            line[member, i + 1, 8 : 8 + SIDE, :] = velocity_ref[cell_rows(i, member), :] * covered
    for member in range(2):
        for side in range(4):
            store_rim(line, member, side, rims_ref[member, side])
    for i in range(SIDE):
        targets = stress_targets(line, strength_ref[i], i)
        for member in range(3):
            stress_ref[member, i] = 0.5 * targets[member]
    fill_stress(pad, stress_ref)
    for side in range(4):
        store_stress_rim(pad, side, stress_rims_ref[0, side], stress_rims_ref[1, side])
    for i in range(SIDE):
        force_east, force_north = forces(pad, i)
        eastward = line[0, i + 1, 8 : 8 + SIDE, :]
        northward = line[1, i + 1, 8 : 8 + SIDE, :]
        mass = mass_ref[i]
        weight = weight_of(cover_ref[i], mass)
        base_ref[0, i] = weight * (mass * (4.0 * eastward + 0.5 * northward) + force_east)
        base_ref[1, i] = weight * (mass * (4.0 * northward - 0.5 * eastward) + force_north)
    for layer, out_ref in enumerate((outer_ref, inner_ref)):
        at = slice(4 * layer, 4 * layer + 4)
        for member in range(2):
            store_strips(out_ref, member, lambda i, j: base_ref[member, i, j, :], layer)
            out_ref[member] += weight_ref[0, at] * forcing_ref[member, at]


def edge_stress_kernel(
    one_ref,
    outer_ref,
    two_ref,
    inner_ref,
    neighbour_ref,
    turn_ref,
    strength_ref,
    *rest,
    opening,
):
    faces_ref, rims_ref, line = rest[-3:]

    def store(side, turns, rows):
        for member, rim in enumerate(turned_vector(turns, rows)):
            rims_ref[member, side] = rim

    gather_rims((one_ref, outer_ref, two_ref), neighbour_ref, turn_ref, store)
    faces_ref[:, :, SIDE:ROWS, :] = jnp.zeros((2, 4, ROWS - SIDE, LANES), F32)
    for side in range(4):
        end = 0 if side < 2 else SIDE - 1
        across, beside = [], []
        for member in range(2):
            line[member, side, 8 : 8 + SIDE, :] = outer_ref[member, side, 0:SIDE, :]
            lower, upper = (1, 3) if side % 2 == 0 else (0, 2)
            line[member, side, 7:8, :] = rims_ref[member, lower, end : end + 1, :]
            line[member, side, 8 + SIDE : 9 + SIDE, :] = rims_ref[member, upper, end : end + 1, :]
            step = 0.5 * (inner_ref[member, side, 0:SIDE, :] - rims_ref[member, side, 0:SIDE, :])
            across.append(step if side < 2 else -step)
            beside.append(
                0.5 * (line[member, side, 9 : 9 + SIDE, :] - line[member, side, 7 : 7 + SIDE, :])
            )
        east, north = (across, beside) if side % 2 == 0 else (beside, across)
        first, second, shear = targets_of(
            east[0], north[0], east[1], north[1], strength_ref[0, side, 0:SIDE, :]
        )
        normal = 0.5 * (first + second) if side % 2 == 0 else 0.5 * (first - second)
        for member, target in enumerate((normal, shear)):
            old = 0.0 if opening else rest[0][member, side, 0:SIDE, :]
            faces_ref[member, side, 0:SIDE, :] = old + 0.5 * (target - old)


def last_kernel(
    one_ref,
    own_ref,
    two_ref,
    neighbour_ref,
    turn_ref,
    base_ref,
    cover_ref,
    mass_ref,
    low_ref,
    high_ref,
    outer_ref,
    inner_ref,
    rims_ref,
    strength_ref,
    old_ref,
    out_hbm,
    stress_hbm,
    line,
    pad,
    stress_ref,
    out_ref,
    sems,
):
    for member in range(2):
        for side in range(4):
            store_rim(line, member, side, rims_ref[member, side])
        for i, ref, side in (
            (0, outer_ref, 0),
            (1, inner_ref, 0),
            (SIDE - 2, inner_ref, 2),
            (SIDE - 1, outer_ref, 2),
        ):
            line[member, i + 1, 8 : 8 + SIDE, :] = ref[member, side, 0:SIDE, :]
        for i in range(2, SIDE - 2):
            for j, ref, side in (
                (0, outer_ref, 1),
                (1, inner_ref, 1),
                (SIDE - 2, inner_ref, 3),
                (SIDE - 1, outer_ref, 3),
            ):
                line[member, i + 1, 8 + j : 9 + j, :] = ref[member, side, i : i + 1, :]
    inside = slice(2, SIDE - 2)
    for i in range(2, SIDE - 2):
        weight = weight_of(cover_ref[i, inside, :], mass_ref[i, inside, :])
        ref, at = (low_ref, i - 2) if i < 2 + HALF else (high_ref, i - 2 - HALF)
        for member in range(2):
            line[member, i + 1, 10 : 10 + INSIDE, :] = base_ref[member, i, inside, :] + weight * (
                ref[member, at * INSIDE : at * INSIDE + INSIDE, :]
            )
    copies = []
    for i in range(SIDE):
        targets = stress_targets(line, strength_ref[i], i)
        now = []
        for member in range(3):
            old = old_ref[member, i]
            now.append(old + 0.5 * (targets[member] - old))
            stress_ref[member, i] = now[member]
        pad[0, i + 1, 8 : 8 + SIDE, :] = 0.5 * (now[0] + now[1])
        pad[1, i + 1, 8 : 8 + SIDE, :] = now[2]
        pad[2, i + 1, 8 : 8 + SIDE, :] = 0.5 * (now[0] - now[1])
        if i % 10 == 9:
            part = pl.ds(i - 9, 10)
            copies.append(
                pltpu.make_async_copy(
                    stress_ref.at[:, part], stress_hbm.at[:, part], sems.at[i // 10]
                )
            )
            copies[-1].start()

    def store(side, turns, rows):
        store_stress_rim(pad, side, *turned_stress(turns, rows))

    gather_rims((one_ref, own_ref, two_ref), neighbour_ref, turn_ref, store)
    for i in range(SIDE):
        force_east, force_north = forces(pad, i)
        eastward = line[0, i + 1, 8 : 8 + SIDE, :]
        northward = line[1, i + 1, 8 : 8 + SIDE, :]
        mass = mass_ref[i]
        weight = weight_of(cover_ref[i], mass)
        out_ref[cell_rows(i, 0), :] = weight * (
            mass * (4.0 * eastward + 0.5 * northward) + force_east
        ) + (eastward - base_ref[0, i])
        out_ref[cell_rows(i, 1), :] = weight * (
            mass * (4.0 * northward - 0.5 * eastward) + force_north
        ) + (northward - base_ref[1, i])
        if i % 6 == 5:
            part = pl.ds(60 * (i - 5), 360)
            copies.append(
                pltpu.make_async_copy(out_ref.at[part], out_hbm.at[part], sems.at[3 + i // 6])
            )
            copies[-1].start()
    for copy in copies:
        copy.wait()


def call(kernel, outs, *args, specs=None, out_specs=None, scratch=(), work=1 << 22, params=PARAMS):
    return pl.pallas_call(
        kernel,
        out_shape=outs,
        in_specs=specs or [VMEM] * len(args),
        out_specs=out_specs or jax.tree.map(lambda _: VMEM, outs),
        scratch_shapes=list(scratch),
        compiler_params=params,
        cost_estimate=pl.CostEstimate(flops=work, bytes_accessed=1 << 22, transcendentals=0),
    )(*args)


def shards(
    velocity,
    strength,
    mass,
    ice_cover,
    neighbour,
    rotation,
    concentration,
    air_wind,
    ocean_current,
    drag,
    slot_cell,
    slot_count,
):
    devices = lax.axis_size(BOTH)
    pairs = [[(i, i + 1) for i in range(start, devices, 2)] for start in (0, 1)]
    swaps = [[(i, j % devices) for i, j in p] + [(j % devices, i) for i, j in p] for p in pairs]

    def both_ways(strips):
        return [lax.ppermute(strips, BOTH, swap) for swap in swaps]

    strip_shape = shape(2, 4, ROWS, LANES)
    block = (SIDE, SIDE, LANES)
    pad2 = [pltpu.VMEM((2, ROWS, 48, LANES), F32)]
    pad3 = [pltpu.VMEM((3, ROWS, 48, LANES), F32)]
    count = slot_count.reshape(1, OWNERS)

    sems = pltpu.SemaphoreType.DMA
    by_cell = jnp.transpose(velocity, (1, 2, 0, 3))
    velocity = by_cell.reshape(2 * SIDE * SIDE, LANES)
    packed = call(
        pack_kernel,
        [shape(OWNERS + EXTRA, SLOTS)] * 4,
        concentration,
        drag.reshape(1, 2),
        specs=[VMEM, SMEM],
        scratch=[pltpu.VMEM((2, 4 * OWNERS, LANES), F32)],
    )
    parts = [packed[0]] + [
        lax.ppermute(packed[step], "cat", [(i, i ^ step) for i in range(4)])
        for step in (1, 2, 3)
    ]

    line = [pltpu.VMEM((2, 4, 48, LANES), F32)]
    winds = call(
        wind_kernel,
        shape(4, OWNERS, SLOTS),
        air_wind,
        ocean_current,
        specs=[ANY] * 2,
        scratch=[pltpu.VMEM((2, 2, 2, 4 * OWNERS, LANES), F32), sems((8,))],
        params=WIND_PARAMS,
    )
    summed = call(partial_kernel, shape(OWNERS, 2, SLOTS), *parts, winds, work=1 << 31)
    arrived = lax.all_to_all(summed, "blocks", split_axis=0, concat_axis=0, tiled=True)

    outer = call(
        outer_strips_kernel,
        strip_shape,
        by_cell,
        ice_cover,
        specs=[ANY] * 2,
        scratch=[
            pltpu.VMEM((4, SIDE, 2, LANES), F32),
            pltpu.VMEM((2, SIDE, LANES), I32),
            pltpu.VMEM((SIDE, 8, LANES), I32),
            pltpu.VMEM((SIDE, 6, LANES), I32),
            sems((8,)),
        ],
        params=ALONE_PARAMS,
    )
    first, second = both_ways(outer)
    inner, strength_strips, weight_strips = call(
        inner_strips_kernel,
        (strip_shape, shape(1, 4, ROWS, LANES), shape(1, 8, ROWS, LANES)),
        velocity, ice_cover, strength, mass, summed,
        specs=[VMEM] * 4 + [ANY],
    )
    faces, rims = call(
        functools.partial(edge_stress_kernel, opening=True),
        (strip_shape, strip_shape),
        first, outer, second, inner, neighbour, rotation, strength_strips,
        scratch=line,
        work=1 << 34,
    )
    first, second = both_ways(faces)

    forcing = scatter_call(
        edge_kernel, 8 * ROWS, shape(2, 8, ROWS, LANES), slot_cell, arrived, count, faces
    )
    stress_rims = call(
        stress_rims_kernel,
        strip_shape,
        first, faces, second, neighbour, rotation, forcing,
        specs=[VMEM] * 5 + [ANY],
    )
    base, stress, outer, inner = call(
        base_kernel,
        (shape(2, *block), shape(3, *block), strip_shape, strip_shape),
        stress_rims, rims, velocity, ice_cover, mass, strength, forcing, weight_strips,
        scratch=pad2 + pad3,
    )
    first, second = both_ways(outer)
    low = scatter_call(
        functools.partial(inside_kernel, 2), HALF_ROWS, shape(2, HALF_ROWS, LANES),
        slot_cell, arrived, count,
    )
    faces, rims = call(
        functools.partial(edge_stress_kernel, opening=False),
        (strip_shape, strip_shape),
        first, outer, second, inner, neighbour, rotation, strength_strips, faces,
        scratch=line,
    )
    first, second = both_ways(faces)
    high = scatter_call(
        functools.partial(inside_kernel, 2 + HALF), HALF_ROWS, shape(2, HALF_ROWS, LANES),
        slot_cell, arrived, count,
    )
    moving, stress = call(
        last_kernel,
        (shape(2 * SIDE * SIDE, LANES), shape(3, *block)),
        first, faces, second, neighbour, rotation, base, ice_cover, mass, low, high,
        outer, inner, rims, strength, stress,
        out_specs=(ANY, ANY),
        scratch=pad2 + pad3
        + [pltpu.VMEM((3, *block), F32), pltpu.VMEM((2 * SIDE * SIDE, LANES), F32), sems((8,))],
        params=SCATTER_PARAMS,
    )
    moving = jnp.transpose(moving.reshape(SIDE, SIDE, 2, LANES), (2, 0, 1, 3))
    return (moving, stress)


def solution(mesh):
    placed = (
        P(None, None, None, BOTH),
        P(None, None, BOTH),
        P(None, None, BOTH),
        P(None, None, BOTH),
        P(None, BOTH),
        P(None, BOTH),
        P("cat", "blocks", None, None),
        P(None, "blocks", None, None),
        P(None, "blocks", None, None),
        P(None, "cat"),
        P(None, BOTH, None),
        P(None, BOTH),
    )
    return jax.shard_map(
        shards,
        mesh=mesh,
        in_specs=placed,
        out_specs=(P(None, None, None, BOTH), P(None, None, None, BOTH)),
        check_vma=False,
    )
```

```python
import functools

import jax
import jax.numpy as jnp
from jax import lax
from jax.experimental import pallas as pl
from jax.experimental.pallas import tpu as pltpu
from jax.sharding import PartitionSpec as P

F32 = jnp.float32
BF16 = jnp.bfloat16
I32 = jnp.int32

SIDE = 30
ROWS = 32
LANES = 128
OWNERS = 64
SLOTS = 256
EXTRA = 8
CHUNK = 16
INSIDE = SIDE - 4
HALF = INSIDE // 2
HALF_ROWS = 352
BOTH = ("blocks", "cat")

PARAMS = pltpu.CompilerParams(vmem_limit_bytes=6 * 1024 * 1024)
SCATTER_PARAMS = pltpu.CompilerParams(vmem_limit_bytes=12 * 1024 * 1024)
ALONE_PARAMS = pltpu.CompilerParams(vmem_limit_bytes=60 * 1024 * 1024)
PACK_PARAMS = pltpu.CompilerParams(vmem_limit_bytes=65000 * 1024)
ANY = pl.BlockSpec(memory_space=pl.ANY)
VMEM = pl.BlockSpec(memory_space=pltpu.VMEM)
SMEM = pl.BlockSpec(memory_space=pltpu.SMEM)


def shape(*dims, dtype=F32):
    return jax.ShapeDtypeStruct(dims, dtype)


def fill_halves(halves, value_of):
    for half in range(2):
        halves[half] = value_of(slice(half * LANES, half * LANES + LANES))


def quarter(halves, half, receiver):
    return halves[half, pl.ds(receiver, OWNERS, stride=4), :]


def wind_kernel(air_ref, ocean_ref, out_ref, wind):
    cat = lax.axis_index("cat")
    for which, ref in enumerate((air_ref, ocean_ref)):
        for member in range(2):
            fill_halves(wind.at[which, member], lambda lanes: ref[member, 0, :, lanes])
    for half in range(2):
        lanes = slice(half * LANES, half * LANES + LANES)
        for which in range(2):
            east = quarter(wind.at[which, 0], half, cat)
            north = quarter(wind.at[which, 1], half, cat)
            speed = jnp.sqrt(east * east + north * north)
            out_ref[2 * which, :, lanes] = speed * east
            out_ref[2 * which + 1, :, lanes] = speed * north


def partial_kernel(mine_ref, first_ref, second_ref, third_ref, wind_ref, out_ref):
    parts = (mine_ref, first_ref, second_ref, third_ref)
    totals = [0.0, 0.0]
    for which in range(2):
        at = OWNERS + which
        weight = jnp.zeros((OWNERS, SLOTS), F32)
        for part in parts:
            weight += part[0:OWNERS, :] * part[at : at + 1, :]
        for member in range(2):
            totals[member] += weight * wind_ref[2 * which + member]
    for member in range(2):
        out_ref[:, member, :] = totals[member]


def split_lanes(lane_hits, value):
    high = value.astype(BF16).astype(F32)
    return (
        jnp.where(lane_hits, high, 0.0).astype(BF16),
        jnp.where(lane_hits, value - high, 0.0).astype(BF16),
    )


def spread_values(cell_ref, value_ref, count_ref, spread, index):
    block = lax.broadcasted_iota(I32, (LANES, SLOTS), 0)
    slot = lax.broadcasted_iota(I32, (1, SLOTS), 1)
    columns = pl.ds(index * SLOTS, SLOTS)
    lane_hits = block == lax.bitwise_and(cell_ref[index], LANES - 1)
    live = slot < count_ref[0, pl.program_id(0) * CHUNK + index]
    for member in range(2):
        value = jnp.where(live, value_ref[index, member : member + 1, :], 0.0)
        high, low = split_lanes(lane_hits, value)
        spread[pl.ds(member * 2 * LANES, LANES), columns] = high
        spread[pl.ds(member * 2 * LANES + LANES, LANES), columns] = low


def cell_number(cell):
    return lax.shift_right_logical(cell, 7)


def accumulate(total, hot, spread):
    total[...] += lax.dot_general(
        hot[...], spread[...], (((1,), (1,)), ((), ())), preferred_element_type=F32
    )


def summed_terms(total, member):
    at = member * 2 * LANES
    return total[:, at : at + LANES] + total[:, at + LANES : at + 2 * LANES]


def edge_kernel(cell_ref, value_ref, count_ref, after_ref, out_ref, hot, spread, total):
    step = pl.program_id(0)

    @pl.when(step == 0)
    def _():
        total[...] = jnp.zeros_like(total)

    along = lax.broadcasted_iota(I32, (ROWS, SLOTS), 0)
    for index in range(CHUNK):
        number = cell_number(cell_ref[index])
        east = lax.shift_right_logical(number * 2185, 16)
        north = number - east * SIDE
        columns = pl.ds(index * SLOTS, SLOTS)
        east_hot = (along == east).astype(F32).astype(BF16)
        north_hot = (along == north).astype(F32).astype(BF16)
        empty = jnp.zeros_like(east_hot)
        for layer in range(2):
            for side, here in enumerate(
                (east == layer, north == layer, east == SIDE - 1 - layer, north == SIDE - 1 - layer)
            ):
                hot[pl.ds((layer * 4 + side) * ROWS, ROWS), columns] = jnp.where(
                    here, east_hot if side % 2 else north_hot, empty
                )
        spread_values(cell_ref, value_ref, count_ref, spread, index)
    accumulate(total, hot, spread)

    @pl.when(step == pl.num_programs(0) - 1)
    def _():
        for member in range(2):
            out_ref[member] = summed_terms(total, member).reshape(8, ROWS, LANES)


def inside_kernel(first, cell_ref, value_ref, count_ref, out_ref, hot, spread, total):
    step = pl.program_id(0)

    @pl.when(step == 0)
    def _():
        total[...] = jnp.zeros_like(total)

    row = lax.broadcasted_iota(I32, (HALF_ROWS, SLOTS), 0)
    east = lax.shift_right_logical(row * 2521, 16)
    wanted = jnp.where(
        east < HALF, (east + first) * SIDE + 2 + (row - east * INSIDE), -1
    )
    for index in range(CHUNK):
        columns = pl.ds(index * SLOTS, SLOTS)
        hits = wanted == cell_number(cell_ref[index])
        hot[:, columns] = hits.astype(F32).astype(BF16)
        spread_values(cell_ref, value_ref, count_ref, spread, index)
    accumulate(total, hot, spread)

    @pl.when(step == pl.num_programs(0) - 1)
    def _():
        for member in range(2):
            out_ref[member] = summed_terms(total, member)


def scatter_call(kernel, rows, outs, cell, value, count, *more):
    width = CHUNK * SLOTS

    def whole(ref):
        return pl.BlockSpec(ref.shape, lambda k, rank=len(ref.shape): (0,) * rank)

    return pl.pallas_call(
        kernel,
        out_shape=outs,
        grid=(OWNERS // CHUNK,),
        in_specs=[
            pl.BlockSpec((CHUNK, 1, SLOTS), lambda k: (k, 0, 0)),
            pl.BlockSpec((CHUNK, 2, SLOTS), lambda k: (k, 0, 0)),
            SMEM,
        ]
        + [ANY] * len(more),
        out_specs=jax.tree.map(whole, outs),
        scratch_shapes=[
            pltpu.VMEM((rows, width), BF16),
            pltpu.VMEM((4 * LANES, width), BF16),
            pltpu.VMEM((rows, 4 * LANES), F32),
        ],
        compiler_params=SCATTER_PARAMS,
        cost_estimate=pl.CostEstimate(
            flops=2 * rows * 4 * LANES * OWNERS * SLOTS, bytes_accessed=1 << 20, transcendentals=0
        ),
    )(cell, value, count, *more)


def gather_rims(strips, neighbour_ref, turn_ref, store):
    devices = lax.axis_size(BOTH)
    here = lax.axis_index(BOTH)
    start = (here - 1) * LANES
    odd = lax.bitwise_and(here, 1)
    holders = (2 - 2 * odd, 1, 2 * odd)
    for side in range(4):
        place = lax.rem(
            neighbour_ref[side : side + 1, :] - start + devices * LANES, devices * LANES
        )
        turns = turn_ref[side : side + 1, :]
        source = lax.bitwise_and(turns + (side + 2), 3)
        holder = lax.shift_right_logical(place, 7)
        lane = jnp.broadcast_to(lax.bitwise_and(place, LANES - 1), (ROWS, LANES))
        rows = [jnp.zeros((ROWS, LANES), F32) for _ in range(2)]
        for where, ref in zip(holders, strips):
            for edge in range(4):
                hits = jnp.broadcast_to((holder == where) & (source == edge), (ROWS, LANES))
                for member in range(2):
                    picked = jnp.take_along_axis(
                        ref[member, edge], lane, axis=1, mode="promise_in_bounds"
                    )
                    rows[member] = jnp.where(hits, picked, rows[member])
        store(side, turns, rows)


def turned_vector(turns, rows):
    cosine = (turns == 0).astype(F32) - (turns == 2).astype(F32)
    sine = (turns == 1).astype(F32) - (turns == 3).astype(F32)
    return cosine * rows[0] - sine * rows[1], sine * rows[0] + cosine * rows[1]


def turned_stress(turns, rows):
    parity = (1 - 2 * lax.bitwise_and(turns, 1)).astype(F32)
    return rows[0], parity * rows[1]


def store_rim(pad, member, side, rim):
    if side == 0 or side == 2:
        pad[member, 0 if side == 0 else SIDE + 1, 8 : 8 + SIDE, :] = rim[0:SIDE]
    else:
        column = 7 if side == 1 else 8 + SIDE
        for i in range(SIDE):
            pad[member, i + 1, column : column + 1, :] = rim[i : i + 1]


def store_strips(out_ref, member, cell_of, layer=0):
    far = SIDE - 1 - layer
    out_ref[member, :, SIDE:ROWS, :] = jnp.zeros((4, ROWS - SIDE, LANES), F32)
    out_ref[member, 0, 0:SIDE, :] = cell_of(layer, slice(0, SIDE))
    out_ref[member, 2, 0:SIDE, :] = cell_of(far, slice(0, SIDE))
    for i in range(SIDE):
        out_ref[member, 1, i : i + 1, :] = cell_of(i, slice(layer, layer + 1))
        out_ref[member, 3, i : i + 1, :] = cell_of(i, slice(far, far + 1))


def cell_rows(i, member, cells=slice(0, SIDE)):
    start = 2 * (SIDE * i + cells.start) + member
    count = cells.stop - cells.start
    return slice(start, start + 1) if count == 1 else pl.ds(start, count, stride=2)


def run_copies(pairs, sems):
    copies = [
        pltpu.make_async_copy(source, target, sems.at[at])
        for at, (source, target) in enumerate(pairs)
    ]
    for copy in copies:
        copy.start()
    return copies


def pack_kernel(conc_hbm, drag_ref, *rest):
    outs, halves, sems = rest[:4], rest[4], rest[5]
    cuts = [(half, start) for half in range(2) for start in (0, 2 * OWNERS)]
    copies = run_copies(
        [
            (
                conc_hbm.at[0, 0, pl.ds(start, 2 * OWNERS), half * LANES : half * LANES + LANES],
                halves.at[half, pl.ds(start, 2 * OWNERS)],
            )
            for half, start in cuts
        ],
        sems,
    )
    cat = lax.axis_index("cat")
    row = lax.broadcasted_iota(I32, (EXTRA, SLOTS), 0)
    coefficients = jnp.where(row == 0, drag_ref[0, 0], drag_ref[0, 1])
    for packed_ref in outs:
        packed_ref[OWNERS : OWNERS + EXTRA, :] = coefficients
    for copy in copies:
        copy.wait()
    for step, packed_ref in enumerate(outs):
        receiver = lax.bitwise_xor(cat, step)
        for half in range(2):
            lanes = slice(half * LANES, half * LANES + LANES)
            packed_ref[0:OWNERS, lanes] = quarter(halves, half, receiver)


def outer_strips_kernel(
    velocity_hbm, cover_hbm, out_ref, lines, cover_rows, cover_low, cover_high, sems
):
    last = SIDE - 1
    copies = run_copies(
        [
            (velocity_hbm.at[0], lines.at[0]),
            (velocity_hbm.at[:, 0], lines.at[1]),
            (velocity_hbm.at[last], lines.at[2]),
            (velocity_hbm.at[:, last], lines.at[3]),
            (cover_hbm.at[0], cover_rows.at[0]),
            (cover_hbm.at[last], cover_rows.at[1]),
            (cover_hbm.at[:, 0:8], cover_low),
            (cover_hbm.at[:, 24:SIDE], cover_high),
        ],
        sems,
    )
    for copy in copies:
        copy.wait()
    out_ref[:, :, SIDE:ROWS, :] = jnp.zeros((2, 4, ROWS - SIDE, LANES), F32)
    for side in range(4):
        for t in range(SIDE):
            if side % 2 == 0:
                covered = cover_rows[side // 2, t : t + 1, :]
            else:
                covered = cover_low[t, 0:1, :] if side == 1 else cover_high[t, 5:6, :]
            covered = covered.astype(F32)
            for member in range(2):
                out_ref[member, side, t : t + 1, :] = (
                    lines[side, t, member : member + 1, :] * covered
                )


def weight_of(cover, mass):
    return cover.astype(F32) / (4.0 * mass + 1.0)


def inner_strips_kernel(
    velocity_ref,
    cover_ref,
    strength_ref,
    mass_ref,
    summed_ref,
    inner_ref,
    strength_strips_ref,
    weight_strips_ref,
):
    for member in range(2):
        store_strips(
            inner_ref,
            member,
            lambda i, j: velocity_ref[cell_rows(i, member, j), :] * cover_ref[i, j, :].astype(F32),
            1,
        )
    store_strips(strength_strips_ref, 0, lambda i, j: strength_ref[i, j, :])
    for layer in range(2):
        at = slice(4 * layer, 4 * layer + 4)
        store_strips(
            weight_strips_ref.at[:, at],
            0,
            lambda i, j: weight_of(cover_ref[i, j, :], mass_ref[i, j, :]),
            layer,
        )


def derivatives(pad, member, i):
    middle = slice(8, 8 + SIDE)
    east = 0.5 * (pad[member, i + 2, middle, :] - pad[member, i, middle, :])
    north = 0.5 * (pad[member, i + 1, 9 : 9 + SIDE, :] - pad[member, i + 1, 7 : 7 + SIDE, :])
    return east, north


def targets_of(east_e, east_n, north_e, north_n, strength):
    divergence = east_e + north_n
    tension = east_e - north_n
    shearing = east_n + north_e
    inverse = lax.rsqrt(
        divergence * divergence + (tension * tension + shearing * shearing) * 0.25 + 0.25
    )
    scaled = strength * inverse
    return (
        divergence * scaled - strength,
        0.25 * (tension * scaled),
        0.125 * (shearing * scaled),
    )


def stress_targets(pad, strength, i):
    return targets_of(*derivatives(pad, 0, i), *derivatives(pad, 1, i), strength)


def forces(pad, i):
    middle = slice(8, 8 + SIDE)
    upper, lower = slice(9, 9 + SIDE), slice(7, 7 + SIDE)
    shear_east, shear_north = derivatives(pad, 1, i)
    force_east = 0.5 * (pad[0, i + 2, middle, :] - pad[0, i, middle, :]) + shear_north
    force_north = shear_east + 0.5 * (pad[2, i + 1, upper, :] - pad[2, i + 1, lower, :])
    return force_east, force_north


def stress_rims_kernel(
    one_ref, own_ref, two_ref, neighbour_ref, turn_ref, forcing_ref, out_ref
):
    def store(side, turns, rows):
        for member, rim in enumerate(turned_stress(turns, rows)):
            out_ref[member, side] = rim

    gather_rims((one_ref, own_ref, two_ref), neighbour_ref, turn_ref, store)


def fill_stress(pad, stress_ref):
    for i in range(SIDE):
        first_stress, second_stress = stress_ref[0, i], stress_ref[1, i]
        pad[0, i + 1, 8 : 8 + SIDE, :] = 0.5 * (first_stress + second_stress)
        pad[1, i + 1, 8 : 8 + SIDE, :] = stress_ref[2, i]
        pad[2, i + 1, 8 : 8 + SIDE, :] = 0.5 * (first_stress - second_stress)


def store_stress_rim(pad, side, normal, shear):
    store_rim(pad, 0 if side in (0, 2) else 2, side, normal)
    store_rim(pad, 1, side, shear)


def base_kernel(
    stress_rims_ref,
    rims_ref,
    velocity_ref,
    cover_ref,
    mass_ref,
    strength_ref,
    forcing_ref,
    weight_ref,
    base_ref,
    stress_ref,
    outer_ref,
    inner_ref,
    line,
    pad,
):
    for i in range(SIDE):
        covered = cover_ref[i].astype(F32)
        for member in range(2):
            line[member, i + 1, 8 : 8 + SIDE, :] = velocity_ref[cell_rows(i, member), :] * covered
    for member in range(2):
        for side in range(4):
            store_rim(line, member, side, rims_ref[member, side])
    for i in range(SIDE):
        targets = stress_targets(line, strength_ref[i], i)
        for member in range(3):
            stress_ref[member, i] = 0.5 * targets[member]
    fill_stress(pad, stress_ref)
    for side in range(4):
        store_stress_rim(pad, side, stress_rims_ref[0, side], stress_rims_ref[1, side])
    for i in range(SIDE):
        force_east, force_north = forces(pad, i)
        eastward = line[0, i + 1, 8 : 8 + SIDE, :]
        northward = line[1, i + 1, 8 : 8 + SIDE, :]
        mass = mass_ref[i]
        weight = weight_of(cover_ref[i], mass)
        base_ref[0, i] = weight * (mass * (4.0 * eastward + 0.5 * northward) + force_east)
        base_ref[1, i] = weight * (mass * (4.0 * northward - 0.5 * eastward) + force_north)
    for layer, out_ref in enumerate((outer_ref, inner_ref)):
        at = slice(4 * layer, 4 * layer + 4)
        for member in range(2):
            store_strips(out_ref, member, lambda i, j: base_ref[member, i, j, :], layer)
            out_ref[member] += weight_ref[0, at] * forcing_ref[member, at]


def edge_stress_kernel(
    one_ref,
    outer_ref,
    two_ref,
    inner_ref,
    neighbour_ref,
    turn_ref,
    strength_ref,
    *rest,
    opening,
):
    faces_ref, rims_ref, line = rest[-3:]

    def store(side, turns, rows):
        for member, rim in enumerate(turned_vector(turns, rows)):
            rims_ref[member, side] = rim

    gather_rims((one_ref, outer_ref, two_ref), neighbour_ref, turn_ref, store)
    faces_ref[:, :, SIDE:ROWS, :] = jnp.zeros((2, 4, ROWS - SIDE, LANES), F32)
    for side in range(4):
        end = 0 if side < 2 else SIDE - 1
        across, beside = [], []
        for member in range(2):
            line[member, side, 8 : 8 + SIDE, :] = outer_ref[member, side, 0:SIDE, :]
            lower, upper = (1, 3) if side % 2 == 0 else (0, 2)
            line[member, side, 7:8, :] = rims_ref[member, lower, end : end + 1, :]
            line[member, side, 8 + SIDE : 9 + SIDE, :] = rims_ref[member, upper, end : end + 1, :]
            step = 0.5 * (inner_ref[member, side, 0:SIDE, :] - rims_ref[member, side, 0:SIDE, :])
            across.append(step if side < 2 else -step)
            beside.append(
                0.5 * (line[member, side, 9 : 9 + SIDE, :] - line[member, side, 7 : 7 + SIDE, :])
            )
        east, north = (across, beside) if side % 2 == 0 else (beside, across)
        first, second, shear = targets_of(
            east[0], north[0], east[1], north[1], strength_ref[0, side, 0:SIDE, :]
        )
        normal = 0.5 * (first + second) if side % 2 == 0 else 0.5 * (first - second)
        for member, target in enumerate((normal, shear)):
            old = 0.0 if opening else rest[0][member, side, 0:SIDE, :]
            faces_ref[member, side, 0:SIDE, :] = old + 0.5 * (target - old)


def last_kernel(
    one_ref,
    own_ref,
    two_ref,
    neighbour_ref,
    turn_ref,
    base_ref,
    cover_ref,
    mass_ref,
    low_ref,
    high_ref,
    outer_ref,
    inner_ref,
    rims_ref,
    strength_ref,
    old_ref,
    out_hbm,
    stress_hbm,
    line,
    pad,
    stress_ref,
    out_ref,
    sems,
):
    for member in range(2):
        for side in range(4):
            store_rim(line, member, side, rims_ref[member, side])
        for i, ref, side in (
            (0, outer_ref, 0),
            (1, inner_ref, 0),
            (SIDE - 2, inner_ref, 2),
            (SIDE - 1, outer_ref, 2),
        ):
            line[member, i + 1, 8 : 8 + SIDE, :] = ref[member, side, 0:SIDE, :]
        for i in range(2, SIDE - 2):
            for j, ref, side in (
                (0, outer_ref, 1),
                (1, inner_ref, 1),
                (SIDE - 2, inner_ref, 3),
                (SIDE - 1, outer_ref, 3),
            ):
                line[member, i + 1, 8 + j : 9 + j, :] = ref[member, side, i : i + 1, :]
    inside = slice(2, SIDE - 2)
    for i in range(2, SIDE - 2):
        weight = weight_of(cover_ref[i, inside, :], mass_ref[i, inside, :])
        ref, at = (low_ref, i - 2) if i < 2 + HALF else (high_ref, i - 2 - HALF)
        for member in range(2):
            line[member, i + 1, 10 : 10 + INSIDE, :] = base_ref[member, i, inside, :] + weight * (
                ref[member, at * INSIDE : at * INSIDE + INSIDE, :]
            )
    copies = []
    for i in range(SIDE):
        targets = stress_targets(line, strength_ref[i], i)
        now = []
        for member in range(3):
            old = old_ref[member, i]
            now.append(old + 0.5 * (targets[member] - old))
            stress_ref[member, i] = now[member]
        pad[0, i + 1, 8 : 8 + SIDE, :] = 0.5 * (now[0] + now[1])
        pad[1, i + 1, 8 : 8 + SIDE, :] = now[2]
        pad[2, i + 1, 8 : 8 + SIDE, :] = 0.5 * (now[0] - now[1])
        if i % 10 == 9:
            part = pl.ds(i - 9, 10)
            copies.append(
                pltpu.make_async_copy(
                    stress_ref.at[:, part], stress_hbm.at[:, part], sems.at[i // 10]
                )
            )
            copies[-1].start()

    def store(side, turns, rows):
        store_stress_rim(pad, side, *turned_stress(turns, rows))

    gather_rims((one_ref, own_ref, two_ref), neighbour_ref, turn_ref, store)
    for i in range(SIDE):
        force_east, force_north = forces(pad, i)
        eastward = line[0, i + 1, 8 : 8 + SIDE, :]
        northward = line[1, i + 1, 8 : 8 + SIDE, :]
        mass = mass_ref[i]
        weight = weight_of(cover_ref[i], mass)
        out_ref[cell_rows(i, 0), :] = weight * (
            mass * (4.0 * eastward + 0.5 * northward) + force_east
        ) + (eastward - base_ref[0, i])
        out_ref[cell_rows(i, 1), :] = weight * (
            mass * (4.0 * northward - 0.5 * eastward) + force_north
        ) + (northward - base_ref[1, i])
        if i % 6 == 5:
            part = pl.ds(60 * (i - 5), 360)
            copies.append(
                pltpu.make_async_copy(out_ref.at[part], out_hbm.at[part], sems.at[3 + i // 6])
            )
            copies[-1].start()
    for copy in copies:
        copy.wait()


def call(kernel, outs, *args, specs=None, out_specs=None, scratch=(), work=1 << 22, params=PARAMS):
    return pl.pallas_call(
        kernel,
        out_shape=outs,
        in_specs=specs or [VMEM] * len(args),
        out_specs=out_specs or jax.tree.map(lambda _: VMEM, outs),
        scratch_shapes=list(scratch),
        compiler_params=params,
        cost_estimate=pl.CostEstimate(flops=work, bytes_accessed=1 << 22, transcendentals=0),
    )(*args)


def shards(
    velocity,
    strength,
    mass,
    ice_cover,
    neighbour,
    rotation,
    concentration,
    air_wind,
    ocean_current,
    drag,
    slot_cell,
    slot_count,
):
    devices = lax.axis_size(BOTH)
    pairs = [[(i, i + 1) for i in range(start, devices, 2)] for start in (0, 1)]
    swaps = [[(i, j % devices) for i, j in p] + [(j % devices, i) for i, j in p] for p in pairs]

    def both_ways(strips):
        return [lax.ppermute(strips, BOTH, swap) for swap in swaps]

    strip_shape = shape(2, 4, ROWS, LANES)
    block = (SIDE, SIDE, LANES)
    pad2 = [pltpu.VMEM((2, ROWS, 48, LANES), F32)]
    pad3 = [pltpu.VMEM((3, ROWS, 48, LANES), F32)]
    count = slot_count.reshape(1, OWNERS)

    sems = pltpu.SemaphoreType.DMA
    by_cell = jnp.transpose(velocity, (1, 2, 0, 3))
    velocity = by_cell.reshape(2 * SIDE * SIDE, LANES)
    packed = call(
        pack_kernel,
        [shape(OWNERS + EXTRA, SLOTS)] * 4,
        concentration,
        drag.reshape(1, 2),
        specs=[ANY, SMEM],
        scratch=[pltpu.VMEM((2, 4 * OWNERS, LANES), F32), sems((4,))],
        params=PACK_PARAMS,
    )
    parts = [packed[0]] + [
        lax.ppermute(packed[step], "cat", [(i, i ^ step) for i in range(4)])
        for step in (1, 2, 3)
    ]

    line = [pltpu.VMEM((2, 4, 48, LANES), F32)]
    winds = call(
        wind_kernel,
        shape(4, OWNERS, SLOTS),
        air_wind,
        ocean_current,
        scratch=[pltpu.VMEM((2, 2, 2, 4 * OWNERS, LANES), F32)],
    )
    summed = call(partial_kernel, shape(OWNERS, 2, SLOTS), *parts, winds, work=1 << 31)
    arrived = lax.all_to_all(summed, "blocks", split_axis=0, concat_axis=0, tiled=True)

    outer = call(
        outer_strips_kernel,
        strip_shape,
        by_cell,
        ice_cover,
        specs=[ANY] * 2,
        scratch=[
            pltpu.VMEM((4, SIDE, 2, LANES), F32),
            pltpu.VMEM((2, SIDE, LANES), I32),
            pltpu.VMEM((SIDE, 8, LANES), I32),
            pltpu.VMEM((SIDE, 6, LANES), I32),
            sems((8,)),
        ],
        params=ALONE_PARAMS,
    )
    first, second = both_ways(outer)
    inner, strength_strips, weight_strips = call(
        inner_strips_kernel,
        (strip_shape, shape(1, 4, ROWS, LANES), shape(1, 8, ROWS, LANES)),
        velocity, ice_cover, strength, mass, summed,
        specs=[VMEM] * 4 + [ANY],
    )
    faces, rims = call(
        functools.partial(edge_stress_kernel, opening=True),
        (strip_shape, strip_shape),
        first, outer, second, inner, neighbour, rotation, strength_strips,
        scratch=line,
        work=1 << 34,
    )
    first, second = both_ways(faces)

    forcing = scatter_call(
        edge_kernel, 8 * ROWS, shape(2, 8, ROWS, LANES), slot_cell, arrived, count, faces
    )
    stress_rims = call(
        stress_rims_kernel,
        strip_shape,
        first, faces, second, neighbour, rotation, forcing,
        specs=[VMEM] * 5 + [ANY],
    )
    base, stress, outer, inner = call(
        base_kernel,
        (shape(2, *block), shape(3, *block), strip_shape, strip_shape),
        stress_rims, rims, velocity, ice_cover, mass, strength, forcing, weight_strips,
        scratch=pad2 + pad3,
    )
    first, second = both_ways(outer)
    low = scatter_call(
        functools.partial(inside_kernel, 2), HALF_ROWS, shape(2, HALF_ROWS, LANES),
        slot_cell, arrived, count,
    )
    faces, rims = call(
        functools.partial(edge_stress_kernel, opening=False),
        (strip_shape, strip_shape),
        first, outer, second, inner, neighbour, rotation, strength_strips, faces,
        scratch=line,
    )
    first, second = both_ways(faces)
    high = scatter_call(
        functools.partial(inside_kernel, 2 + HALF), HALF_ROWS, shape(2, HALF_ROWS, LANES),
        slot_cell, arrived, count,
    )
    moving, stress = call(
        last_kernel,
        (shape(2 * SIDE * SIDE, LANES), shape(3, *block)),
        first, faces, second, neighbour, rotation, base, ice_cover, mass, low, high,
        outer, inner, rims, strength, stress,
        out_specs=(ANY, ANY),
        scratch=pad2 + pad3
        + [pltpu.VMEM((3, *block), F32), pltpu.VMEM((2 * SIDE * SIDE, LANES), F32), sems((8,))],
        params=SCATTER_PARAMS,
    )
    moving = jnp.transpose(moving.reshape(SIDE, SIDE, 2, LANES), (2, 0, 1, 3))
    return (moving, stress)


def solution(mesh):
    placed = (
        P(None, None, None, BOTH),
        P(None, None, BOTH),
        P(None, None, BOTH),
        P(None, None, BOTH),
        P(None, BOTH),
        P(None, BOTH),
        P("cat", "blocks", None, None),
        P(None, "blocks", None, None),
        P(None, "blocks", None, None),
        P(None, "cat"),
        P(None, BOTH, None),
        P(None, BOTH),
    )
    return jax.shard_map(
        shards,
        mesh=mesh,
        in_specs=placed,
        out_specs=(P(None, None, None, BOTH), P(None, None, None, BOTH)),
        check_vma=False,
    )
```

```python
import functools

import jax
import jax.numpy as jnp
from jax import lax
from jax.experimental import pallas as pl
from jax.experimental.pallas import tpu as pltpu
from jax.sharding import PartitionSpec as P

F32 = jnp.float32
BF16 = jnp.bfloat16
I32 = jnp.int32

SIDE = 30
ROWS = 32
LANES = 128
OWNERS = 64
SLOTS = 256
EXTRA = 8
CHUNK = 16
INSIDE = SIDE - 4
HALF = INSIDE // 2
HALF_ROWS = 352
BOTH = ("blocks", "cat")

PARAMS = pltpu.CompilerParams(vmem_limit_bytes=6 * 1024 * 1024)
SCATTER_PARAMS = pltpu.CompilerParams(vmem_limit_bytes=12 * 1024 * 1024)
ALONE_PARAMS = pltpu.CompilerParams(vmem_limit_bytes=60 * 1024 * 1024)
PACK_PARAMS = pltpu.CompilerParams(vmem_limit_bytes=65000 * 1024)
ANY = pl.BlockSpec(memory_space=pl.ANY)
VMEM = pl.BlockSpec(memory_space=pltpu.VMEM)
SMEM = pl.BlockSpec(memory_space=pltpu.SMEM)


def shape(*dims, dtype=F32):
    return jax.ShapeDtypeStruct(dims, dtype)


def fill_halves(halves, value_of):
    for half in range(2):
        halves[half] = value_of(slice(half * LANES, half * LANES + LANES))


def quarter(halves, half, receiver):
    return halves[half, pl.ds(receiver, OWNERS, stride=4), :]


def wind_kernel(air_ref, ocean_ref, out_ref, wind):
    cat = lax.axis_index("cat")
    for which, ref in enumerate((air_ref, ocean_ref)):
        for member in range(2):
            fill_halves(wind.at[which, member], lambda lanes: ref[member, 0, :, lanes])
    for half in range(2):
        lanes = slice(half * LANES, half * LANES + LANES)
        for which in range(2):
            east = quarter(wind.at[which, 0], half, cat)
            north = quarter(wind.at[which, 1], half, cat)
            speed = jnp.sqrt(east * east + north * north)
            out_ref[2 * which, :, lanes] = speed * east
            out_ref[2 * which + 1, :, lanes] = speed * north


def partial_kernel(mine_ref, first_ref, second_ref, third_ref, wind_ref, out_ref):
    parts = (mine_ref, first_ref, second_ref, third_ref)
    totals = [0.0, 0.0]
    for which in range(2):
        at = OWNERS + which
        weight = jnp.zeros((OWNERS, SLOTS), F32)
        for part in parts:
            weight += part[0:OWNERS, :] * part[at : at + 1, :]
        for member in range(2):
            totals[member] += weight * wind_ref[2 * which + member]
    for member in range(2):
        out_ref[:, member, :] = totals[member]


def split_lanes(lane_hits, value):
    high = value.astype(BF16).astype(F32)
    return (
        jnp.where(lane_hits, high, 0.0).astype(BF16),
        jnp.where(lane_hits, value - high, 0.0).astype(BF16),
    )


def spread_values(cell_ref, value_ref, count_ref, spread, index):
    block = lax.broadcasted_iota(I32, (LANES, SLOTS), 0)
    slot = lax.broadcasted_iota(I32, (1, SLOTS), 1)
    columns = pl.ds(index * SLOTS, SLOTS)
    lane_hits = block == lax.bitwise_and(cell_ref[index], LANES - 1)
    live = slot < count_ref[0, pl.program_id(0) * CHUNK + index]
    for member in range(2):
        value = jnp.where(live, value_ref[index, member : member + 1, :], 0.0)
        high, low = split_lanes(lane_hits, value)
        spread[pl.ds(member * 2 * LANES, LANES), columns] = high
        spread[pl.ds(member * 2 * LANES + LANES, LANES), columns] = low


def cell_number(cell):
    return lax.shift_right_logical(cell, 7)


def accumulate(total, hot, spread):
    total[...] += lax.dot_general(
        hot[...], spread[...], (((1,), (1,)), ((), ())), preferred_element_type=F32
    )


def summed_terms(total, member):
    at = member * 2 * LANES
    return total[:, at : at + LANES] + total[:, at + LANES : at + 2 * LANES]


def edge_kernel(cell_ref, value_ref, count_ref, after_ref, out_ref, hot, spread, total):
    step = pl.program_id(0)

    @pl.when(step == 0)
    def _():
        total[...] = jnp.zeros_like(total)

    along = lax.broadcasted_iota(I32, (ROWS, SLOTS), 0)
    for index in range(CHUNK):
        number = cell_number(cell_ref[index])
        east = lax.shift_right_logical(number * 2185, 16)
        north = number - east * SIDE
        columns = pl.ds(index * SLOTS, SLOTS)
        east_hot = (along == east).astype(F32).astype(BF16)
        north_hot = (along == north).astype(F32).astype(BF16)
        empty = jnp.zeros_like(east_hot)
        for layer in range(2):
            for side, here in enumerate(
                (east == layer, north == layer, east == SIDE - 1 - layer, north == SIDE - 1 - layer)
            ):
                hot[pl.ds((layer * 4 + side) * ROWS, ROWS), columns] = jnp.where(
                    here, east_hot if side % 2 else north_hot, empty
                )
        spread_values(cell_ref, value_ref, count_ref, spread, index)
    accumulate(total, hot, spread)

    @pl.when(step == pl.num_programs(0) - 1)
    def _():
        for member in range(2):
            out_ref[member] = summed_terms(total, member).reshape(8, ROWS, LANES)


def inside_kernel(first, cell_ref, value_ref, count_ref, out_ref, hot, spread, total):
    step = pl.program_id(0)

    @pl.when(step == 0)
    def _():
        total[...] = jnp.zeros_like(total)

    row = lax.broadcasted_iota(I32, (HALF_ROWS, SLOTS), 0)
    east = lax.shift_right_logical(row * 2521, 16)
    wanted = jnp.where(
        east < HALF, (east + first) * SIDE + 2 + (row - east * INSIDE), -1
    )
    for index in range(CHUNK):
        columns = pl.ds(index * SLOTS, SLOTS)
        hits = wanted == cell_number(cell_ref[index])
        hot[:, columns] = hits.astype(F32).astype(BF16)
        spread_values(cell_ref, value_ref, count_ref, spread, index)
    accumulate(total, hot, spread)

    @pl.when(step == pl.num_programs(0) - 1)
    def _():
        for member in range(2):
            out_ref[member] = summed_terms(total, member)


def scatter_call(kernel, rows, outs, cell, value, count, *more):
    width = CHUNK * SLOTS

    def whole(ref):
        return pl.BlockSpec(ref.shape, lambda k, rank=len(ref.shape): (0,) * rank)

    return pl.pallas_call(
        kernel,
        out_shape=outs,
        grid=(OWNERS // CHUNK,),
        in_specs=[
            pl.BlockSpec((CHUNK, 1, SLOTS), lambda k: (k, 0, 0)),
            pl.BlockSpec((CHUNK, 2, SLOTS), lambda k: (k, 0, 0)),
            SMEM,
        ]
        + [ANY] * len(more),
        out_specs=jax.tree.map(whole, outs),
        scratch_shapes=[
            pltpu.VMEM((rows, width), BF16),
            pltpu.VMEM((4 * LANES, width), BF16),
            pltpu.VMEM((rows, 4 * LANES), F32),
        ],
        compiler_params=SCATTER_PARAMS,
        cost_estimate=pl.CostEstimate(
            flops=2 * rows * 4 * LANES * OWNERS * SLOTS, bytes_accessed=1 << 20, transcendentals=0
        ),
    )(cell, value, count, *more)


def gather_rims(strips, neighbour_ref, turn_ref, store):
    devices = lax.axis_size(BOTH)
    here = lax.axis_index(BOTH)
    start = (here - 1) * LANES
    odd = lax.bitwise_and(here, 1)
    holders = (2 - 2 * odd, 1, 2 * odd)
    for side in range(4):
        place = lax.rem(
            neighbour_ref[side : side + 1, :] - start + devices * LANES, devices * LANES
        )
        turns = turn_ref[side : side + 1, :]
        source = lax.bitwise_and(turns + (side + 2), 3)
        holder = lax.shift_right_logical(place, 7)
        lane = jnp.broadcast_to(lax.bitwise_and(place, LANES - 1), (ROWS, LANES))
        rows = [jnp.zeros((ROWS, LANES), F32) for _ in range(2)]
        for where, ref in zip(holders, strips):
            for edge in range(4):
                hits = jnp.broadcast_to((holder == where) & (source == edge), (ROWS, LANES))
                for member in range(2):
                    picked = jnp.take_along_axis(
                        ref[member, edge], lane, axis=1, mode="promise_in_bounds"
                    )
                    rows[member] = jnp.where(hits, picked, rows[member])
        store(side, turns, rows)


def turned_vector(turns, rows):
    cosine = (turns == 0).astype(F32) - (turns == 2).astype(F32)
    sine = (turns == 1).astype(F32) - (turns == 3).astype(F32)
    return cosine * rows[0] - sine * rows[1], sine * rows[0] + cosine * rows[1]


def turned_stress(turns, rows):
    parity = (1 - 2 * lax.bitwise_and(turns, 1)).astype(F32)
    return rows[0], parity * rows[1]


def store_rim(pad, member, side, rim):
    if side == 0 or side == 2:
        pad[member, 0 if side == 0 else SIDE + 1, 8 : 8 + SIDE, :] = rim[0:SIDE]
    else:
        column = 7 if side == 1 else 8 + SIDE
        for i in range(SIDE):
            pad[member, i + 1, column : column + 1, :] = rim[i : i + 1]


def store_strips(out_ref, member, cell_of, layer=0):
    far = SIDE - 1 - layer
    out_ref[member, :, SIDE:ROWS, :] = jnp.zeros((4, ROWS - SIDE, LANES), F32)
    out_ref[member, 0, 0:SIDE, :] = cell_of(layer, slice(0, SIDE))
    out_ref[member, 2, 0:SIDE, :] = cell_of(far, slice(0, SIDE))
    for i in range(SIDE):
        out_ref[member, 1, i : i + 1, :] = cell_of(i, slice(layer, layer + 1))
        out_ref[member, 3, i : i + 1, :] = cell_of(i, slice(far, far + 1))


def cell_rows(i, member, cells=slice(0, SIDE)):
    start = 2 * (SIDE * i + cells.start) + member
    count = cells.stop - cells.start
    return slice(start, start + 1) if count == 1 else pl.ds(start, count, stride=2)


def run_copies(pairs, sems):
    copies = [
        pltpu.make_async_copy(source, target, sems.at[at])
        for at, (source, target) in enumerate(pairs)
    ]
    for copy in copies:
        copy.start()
    return copies


def pack_kernel(conc_hbm, drag_hbm, *rest):
    outs = rest[:4]
    whole, halves, drag, sems = rest[4:]
    parts = [pl.ds(start, 2 * OWNERS) for start in (0, 2 * OWNERS)]
    copies = run_copies(
        [(conc_hbm.at[0, 0, part], whole.at[part]) for part in parts] + [(drag_hbm, drag)], sems
    )
    for copy in copies:
        copy.wait()
    cat = lax.axis_index("cat")
    row = lax.broadcasted_iota(I32, (EXTRA, SLOTS), 0)
    coefficients = jnp.where(row == 0, drag[0:1, 0:1], drag[0:1, 1:2])
    fill_halves(halves, lambda lanes: whole[:, lanes])
    for step, packed_ref in enumerate(outs):
        receiver = lax.bitwise_xor(cat, step)
        for half in range(2):
            lanes = slice(half * LANES, half * LANES + LANES)
            packed_ref[0:OWNERS, lanes] = quarter(halves, half, receiver)
        packed_ref[OWNERS : OWNERS + EXTRA, :] = coefficients


def outer_strips_kernel(
    velocity_hbm, cover_hbm, out_ref, lines, cover_rows, cover_low, cover_high, sems
):
    last = SIDE - 1
    copies = run_copies(
        [
            (velocity_hbm.at[0], lines.at[0]),
            (velocity_hbm.at[:, 0], lines.at[1]),
            (velocity_hbm.at[last], lines.at[2]),
            (velocity_hbm.at[:, last], lines.at[3]),
            (cover_hbm.at[0], cover_rows.at[0]),
            (cover_hbm.at[last], cover_rows.at[1]),
            (cover_hbm.at[:, 0:8], cover_low),
            (cover_hbm.at[:, 24:SIDE], cover_high),
        ],
        sems,
    )
    for copy in copies:
        copy.wait()
    out_ref[:, :, SIDE:ROWS, :] = jnp.zeros((2, 4, ROWS - SIDE, LANES), F32)
    for side in range(4):
        for t in range(SIDE):
            if side % 2 == 0:
                covered = cover_rows[side // 2, t : t + 1, :]
            else:
                covered = cover_low[t, 0:1, :] if side == 1 else cover_high[t, 5:6, :]
            covered = covered.astype(F32)
            for member in range(2):
                out_ref[member, side, t : t + 1, :] = (
                    lines[side, t, member : member + 1, :] * covered
                )


def weight_of(cover, mass):
    return cover.astype(F32) / (4.0 * mass + 1.0)


def inner_strips_kernel(
    velocity_ref,
    cover_ref,
    strength_ref,
    mass_ref,
    summed_ref,
    inner_ref,
    strength_strips_ref,
    weight_strips_ref,
):
    for member in range(2):
        store_strips(
            inner_ref,
            member,
            lambda i, j: velocity_ref[cell_rows(i, member, j), :] * cover_ref[i, j, :].astype(F32),
            1,
        )
    store_strips(strength_strips_ref, 0, lambda i, j: strength_ref[i, j, :])
    for layer in range(2):
        at = slice(4 * layer, 4 * layer + 4)
        store_strips(
            weight_strips_ref.at[:, at],
            0,
            lambda i, j: weight_of(cover_ref[i, j, :], mass_ref[i, j, :]),
            layer,
        )


def derivatives(pad, member, i):
    middle = slice(8, 8 + SIDE)
    east = 0.5 * (pad[member, i + 2, middle, :] - pad[member, i, middle, :])
    north = 0.5 * (pad[member, i + 1, 9 : 9 + SIDE, :] - pad[member, i + 1, 7 : 7 + SIDE, :])
    return east, north


def targets_of(east_e, east_n, north_e, north_n, strength):
    divergence = east_e + north_n
    tension = east_e - north_n
    shearing = east_n + north_e
    inverse = lax.rsqrt(
        divergence * divergence + (tension * tension + shearing * shearing) * 0.25 + 0.25
    )
    scaled = strength * inverse
    return (
        divergence * scaled - strength,
        0.25 * (tension * scaled),
        0.125 * (shearing * scaled),
    )


def stress_targets(pad, strength, i):
    return targets_of(*derivatives(pad, 0, i), *derivatives(pad, 1, i), strength)


def forces(pad, i):
    middle = slice(8, 8 + SIDE)
    upper, lower = slice(9, 9 + SIDE), slice(7, 7 + SIDE)
    shear_east, shear_north = derivatives(pad, 1, i)
    force_east = 0.5 * (pad[0, i + 2, middle, :] - pad[0, i, middle, :]) + shear_north
    force_north = shear_east + 0.5 * (pad[2, i + 1, upper, :] - pad[2, i + 1, lower, :])
    return force_east, force_north


def stress_rims_kernel(
    one_ref, own_ref, two_ref, neighbour_ref, turn_ref, forcing_ref, out_ref
):
    def store(side, turns, rows):
        for member, rim in enumerate(turned_stress(turns, rows)):
            out_ref[member, side] = rim

    gather_rims((one_ref, own_ref, two_ref), neighbour_ref, turn_ref, store)


def fill_stress(pad, stress_ref):
    for i in range(SIDE):
        first_stress, second_stress = stress_ref[0, i], stress_ref[1, i]
        pad[0, i + 1, 8 : 8 + SIDE, :] = 0.5 * (first_stress + second_stress)
        pad[1, i + 1, 8 : 8 + SIDE, :] = stress_ref[2, i]
        pad[2, i + 1, 8 : 8 + SIDE, :] = 0.5 * (first_stress - second_stress)


def store_stress_rim(pad, side, normal, shear):
    store_rim(pad, 0 if side in (0, 2) else 2, side, normal)
    store_rim(pad, 1, side, shear)


def base_kernel(
    stress_rims_ref,
    rims_ref,
    velocity_ref,
    cover_ref,
    mass_ref,
    strength_ref,
    forcing_ref,
    weight_ref,
    base_ref,
    stress_ref,
    outer_ref,
    inner_ref,
    line,
    pad,
):
    for i in range(SIDE):
        covered = cover_ref[i].astype(F32)
        for member in range(2):
            line[member, i + 1, 8 : 8 + SIDE, :] = velocity_ref[cell_rows(i, member), :] * covered
    for member in range(2):
        for side in range(4):
            store_rim(line, member, side, rims_ref[member, side])
    for i in range(SIDE):
        targets = stress_targets(line, strength_ref[i], i)
        for member in range(3):
            stress_ref[member, i] = 0.5 * targets[member]
    fill_stress(pad, stress_ref)
    for side in range(4):
        store_stress_rim(pad, side, stress_rims_ref[0, side], stress_rims_ref[1, side])
    for i in range(SIDE):
        force_east, force_north = forces(pad, i)
        eastward = line[0, i + 1, 8 : 8 + SIDE, :]
        northward = line[1, i + 1, 8 : 8 + SIDE, :]
        mass = mass_ref[i]
        weight = weight_of(cover_ref[i], mass)
        base_ref[0, i] = weight * (mass * (4.0 * eastward + 0.5 * northward) + force_east)
        base_ref[1, i] = weight * (mass * (4.0 * northward - 0.5 * eastward) + force_north)
    for layer, out_ref in enumerate((outer_ref, inner_ref)):
        at = slice(4 * layer, 4 * layer + 4)
        for member in range(2):
            store_strips(out_ref, member, lambda i, j: base_ref[member, i, j, :], layer)
            out_ref[member] += weight_ref[0, at] * forcing_ref[member, at]


def edge_stress_kernel(
    one_ref,
    outer_ref,
    two_ref,
    inner_ref,
    neighbour_ref,
    turn_ref,
    strength_ref,
    *rest,
    opening,
):
    faces_ref, rims_ref, line = rest[-3:]

    def store(side, turns, rows):
        for member, rim in enumerate(turned_vector(turns, rows)):
            rims_ref[member, side] = rim

    gather_rims((one_ref, outer_ref, two_ref), neighbour_ref, turn_ref, store)
    faces_ref[:, :, SIDE:ROWS, :] = jnp.zeros((2, 4, ROWS - SIDE, LANES), F32)
    for side in range(4):
        end = 0 if side < 2 else SIDE - 1
        across, beside = [], []
        for member in range(2):
            line[member, side, 8 : 8 + SIDE, :] = outer_ref[member, side, 0:SIDE, :]
            lower, upper = (1, 3) if side % 2 == 0 else (0, 2)
            line[member, side, 7:8, :] = rims_ref[member, lower, end : end + 1, :]
            line[member, side, 8 + SIDE : 9 + SIDE, :] = rims_ref[member, upper, end : end + 1, :]
            step = 0.5 * (inner_ref[member, side, 0:SIDE, :] - rims_ref[member, side, 0:SIDE, :])
            across.append(step if side < 2 else -step)
            beside.append(
                0.5 * (line[member, side, 9 : 9 + SIDE, :] - line[member, side, 7 : 7 + SIDE, :])
            )
        east, north = (across, beside) if side % 2 == 0 else (beside, across)
        first, second, shear = targets_of(
            east[0], north[0], east[1], north[1], strength_ref[0, side, 0:SIDE, :]
        )
        normal = 0.5 * (first + second) if side % 2 == 0 else 0.5 * (first - second)
        for member, target in enumerate((normal, shear)):
            old = 0.0 if opening else rest[0][member, side, 0:SIDE, :]
            faces_ref[member, side, 0:SIDE, :] = old + 0.5 * (target - old)


def last_kernel(
    one_ref,
    own_ref,
    two_ref,
    neighbour_ref,
    turn_ref,
    base_ref,
    cover_ref,
    mass_ref,
    low_ref,
    high_ref,
    outer_ref,
    inner_ref,
    rims_ref,
    strength_ref,
    old_ref,
    out_hbm,
    stress_hbm,
    line,
    pad,
    stress_ref,
    out_ref,
    sems,
):
    for member in range(2):
        for side in range(4):
            store_rim(line, member, side, rims_ref[member, side])
        for i, ref, side in (
            (0, outer_ref, 0),
            (1, inner_ref, 0),
            (SIDE - 2, inner_ref, 2),
            (SIDE - 1, outer_ref, 2),
        ):
            line[member, i + 1, 8 : 8 + SIDE, :] = ref[member, side, 0:SIDE, :]
        for i in range(2, SIDE - 2):
            for j, ref, side in (
                (0, outer_ref, 1),
                (1, inner_ref, 1),
                (SIDE - 2, inner_ref, 3),
                (SIDE - 1, outer_ref, 3),
            ):
                line[member, i + 1, 8 + j : 9 + j, :] = ref[member, side, i : i + 1, :]
    inside = slice(2, SIDE - 2)
    for i in range(2, SIDE - 2):
        weight = weight_of(cover_ref[i, inside, :], mass_ref[i, inside, :])
        ref, at = (low_ref, i - 2) if i < 2 + HALF else (high_ref, i - 2 - HALF)
        for member in range(2):
            line[member, i + 1, 10 : 10 + INSIDE, :] = base_ref[member, i, inside, :] + weight * (
                ref[member, at * INSIDE : at * INSIDE + INSIDE, :]
            )
    copies = []
    for i in range(SIDE):
        targets = stress_targets(line, strength_ref[i], i)
        now = []
        for member in range(3):
            old = old_ref[member, i]
            now.append(old + 0.5 * (targets[member] - old))
            stress_ref[member, i] = now[member]
        pad[0, i + 1, 8 : 8 + SIDE, :] = 0.5 * (now[0] + now[1])
        pad[1, i + 1, 8 : 8 + SIDE, :] = now[2]
        pad[2, i + 1, 8 : 8 + SIDE, :] = 0.5 * (now[0] - now[1])
        if i % 10 == 9:
            part = pl.ds(i - 9, 10)
            copies.append(
                pltpu.make_async_copy(
                    stress_ref.at[:, part], stress_hbm.at[:, part], sems.at[i // 10]
                )
            )
            copies[-1].start()

    def store(side, turns, rows):
        store_stress_rim(pad, side, *turned_stress(turns, rows))

    gather_rims((one_ref, own_ref, two_ref), neighbour_ref, turn_ref, store)
    for i in range(SIDE):
        force_east, force_north = forces(pad, i)
        eastward = line[0, i + 1, 8 : 8 + SIDE, :]
        northward = line[1, i + 1, 8 : 8 + SIDE, :]
        mass = mass_ref[i]
        weight = weight_of(cover_ref[i], mass)
        out_ref[cell_rows(i, 0), :] = weight * (
            mass * (4.0 * eastward + 0.5 * northward) + force_east
        ) + (eastward - base_ref[0, i])
        out_ref[cell_rows(i, 1), :] = weight * (
            mass * (4.0 * northward - 0.5 * eastward) + force_north
        ) + (northward - base_ref[1, i])
        if i % 6 == 5:
            part = pl.ds(60 * (i - 5), 360)
            copies.append(
                pltpu.make_async_copy(out_ref.at[part], out_hbm.at[part], sems.at[3 + i // 6])
            )
            copies[-1].start()
    for copy in copies:
        copy.wait()


def call(kernel, outs, *args, specs=None, out_specs=None, scratch=(), work=1 << 22, params=PARAMS):
    return pl.pallas_call(
        kernel,
        out_shape=outs,
        in_specs=specs or [VMEM] * len(args),
        out_specs=out_specs or jax.tree.map(lambda _: VMEM, outs),
        scratch_shapes=list(scratch),
        compiler_params=params,
        cost_estimate=pl.CostEstimate(flops=work, bytes_accessed=1 << 22, transcendentals=0),
    )(*args)


def shards(
    velocity,
    strength,
    mass,
    ice_cover,
    neighbour,
    rotation,
    concentration,
    air_wind,
    ocean_current,
    drag,
    slot_cell,
    slot_count,
):
    devices = lax.axis_size(BOTH)
    pairs = [[(i, i + 1) for i in range(start, devices, 2)] for start in (0, 1)]
    swaps = [[(i, j % devices) for i, j in p] + [(j % devices, i) for i, j in p] for p in pairs]

    def both_ways(strips):
        return [lax.ppermute(strips, BOTH, swap) for swap in swaps]

    strip_shape = shape(2, 4, ROWS, LANES)
    block = (SIDE, SIDE, LANES)
    pad2 = [pltpu.VMEM((2, ROWS, 48, LANES), F32)]
    pad3 = [pltpu.VMEM((3, ROWS, 48, LANES), F32)]
    count = slot_count.reshape(1, OWNERS)

    sems = pltpu.SemaphoreType.DMA
    by_cell = jnp.transpose(velocity, (1, 2, 0, 3))
    velocity = by_cell.reshape(2 * SIDE * SIDE, LANES)
    packed = call(
        pack_kernel,
        [shape(OWNERS + EXTRA, SLOTS)] * 4,
        concentration,
        drag.reshape(1, 2),
        specs=[ANY, ANY],
        scratch=[
            pltpu.VMEM((4 * OWNERS, SLOTS), F32),
            pltpu.VMEM((2, 4 * OWNERS, LANES), F32),
            pltpu.VMEM((1, 2), F32),
            sems((3,)),
        ],
        params=PACK_PARAMS,
    )
    parts = [packed[0]] + [
        lax.ppermute(packed[step], "cat", [(i, i ^ step) for i in range(4)])
        for step in (1, 2, 3)
    ]

    line = [pltpu.VMEM((2, 4, 48, LANES), F32)]
    winds = call(
        wind_kernel,
        shape(4, OWNERS, SLOTS),
        air_wind,
        ocean_current,
        scratch=[pltpu.VMEM((2, 2, 2, 4 * OWNERS, LANES), F32)],
    )
    summed = call(partial_kernel, shape(OWNERS, 2, SLOTS), *parts, winds, work=1 << 31)
    arrived = lax.all_to_all(summed, "blocks", split_axis=0, concat_axis=0, tiled=True)

    outer = call(
        outer_strips_kernel,
        strip_shape,
        by_cell,
        ice_cover,
        specs=[ANY] * 2,
        scratch=[
            pltpu.VMEM((4, SIDE, 2, LANES), F32),
            pltpu.VMEM((2, SIDE, LANES), I32),
            pltpu.VMEM((SIDE, 8, LANES), I32),
            pltpu.VMEM((SIDE, 6, LANES), I32),
            sems((8,)),
        ],
        params=ALONE_PARAMS,
    )
    first, second = both_ways(outer)
    inner, strength_strips, weight_strips = call(
        inner_strips_kernel,
        (strip_shape, shape(1, 4, ROWS, LANES), shape(1, 8, ROWS, LANES)),
        velocity, ice_cover, strength, mass, summed,
        specs=[VMEM] * 4 + [ANY],
    )
    faces, rims = call(
        functools.partial(edge_stress_kernel, opening=True),
        (strip_shape, strip_shape),
        first, outer, second, inner, neighbour, rotation, strength_strips,
        scratch=line,
        work=1 << 34,
    )
    first, second = both_ways(faces)

    forcing = scatter_call(
        edge_kernel, 8 * ROWS, shape(2, 8, ROWS, LANES), slot_cell, arrived, count, faces
    )
    stress_rims = call(
        stress_rims_kernel,
        strip_shape,
        first, faces, second, neighbour, rotation, forcing,
        specs=[VMEM] * 5 + [ANY],
    )
    base, stress, outer, inner = call(
        base_kernel,
        (shape(2, *block), shape(3, *block), strip_shape, strip_shape),
        stress_rims, rims, velocity, ice_cover, mass, strength, forcing, weight_strips,
        scratch=pad2 + pad3,
    )
    first, second = both_ways(outer)
    low = scatter_call(
        functools.partial(inside_kernel, 2), HALF_ROWS, shape(2, HALF_ROWS, LANES),
        slot_cell, arrived, count,
    )
    faces, rims = call(
        functools.partial(edge_stress_kernel, opening=False),
        (strip_shape, strip_shape),
        first, outer, second, inner, neighbour, rotation, strength_strips, faces,
        scratch=line,
    )
    first, second = both_ways(faces)
    high = scatter_call(
        functools.partial(inside_kernel, 2 + HALF), HALF_ROWS, shape(2, HALF_ROWS, LANES),
        slot_cell, arrived, count,
    )
    moving, stress = call(
        last_kernel,
        (shape(2 * SIDE * SIDE, LANES), shape(3, *block)),
        first, faces, second, neighbour, rotation, base, ice_cover, mass, low, high,
        outer, inner, rims, strength, stress,
        out_specs=(ANY, ANY),
        scratch=pad2 + pad3
        + [pltpu.VMEM((3, *block), F32), pltpu.VMEM((2 * SIDE * SIDE, LANES), F32), sems((8,))],
        params=SCATTER_PARAMS,
    )
    moving = jnp.transpose(moving.reshape(SIDE, SIDE, 2, LANES), (2, 0, 1, 3))
    return (moving, stress)


def solution(mesh):
    placed = (
        P(None, None, None, BOTH),
        P(None, None, BOTH),
        P(None, None, BOTH),
        P(None, None, BOTH),
        P(None, BOTH),
        P(None, BOTH),
        P("cat", "blocks", None, None),
        P(None, "blocks", None, None),
        P(None, "blocks", None, None),
        P(None, "cat"),
        P(None, BOTH, None),
        P(None, BOTH),
    )
    return jax.shard_map(
        shards,
        mesh=mesh,
        in_specs=placed,
        out_specs=(P(None, None, None, BOTH), P(None, None, None, BOTH)),
        check_vma=False,
    )
```
